32 devices in a mesh: dp: 2 (over x), ctx: 16 (over z, y, core).
Axes of the slice: x: 2, y: 2, z: 4, core: 2. Of those that a mesh axis runs over, the one named last changes fastest.
Arguments:
- inputs: bfloat16 [4, 2048, 960], P('dp', 'ctx'), may hold values from -16 to 16
- query_weight: bfloat16 [960, 960], P('ctx', 'dp'), may hold values from -0.1613743 to 0.1613743
- key_weight: bfloat16 [960, 320], P('ctx', 'dp'), may hold values from -0.1613743 to 0.1613743
- value_matrix: bfloat16 [960, 320], P('ctx', 'dp'), may hold values from -0.1875 to 0.1875
- out_weight: bfloat16 [960, 960], P('dp', 'ctx'), may hold values from -1.5 to 1.5
- gate_weight: bfloat16 [960, 2560], P('ctx', 'dp'), may hold values from -0.1875 to 0.1875
- up_weight: bfloat16 [960, 2560], P('ctx', 'dp'), may hold values from -0.1875 to 0.1875
- down_weight: bfloat16 [2560, 960], P('dp', 'ctx'), may hold values from -0.125 to 0.125
- norm_gains: bfloat16 [2, 960], P('dp', 'ctx'), may hold values from 0.5 to 1.5
- cotangent: bfloat16 [4, 2048, 960], P('dp', 'ctx'), may hold values from -6 to 6
Outputs:
- layer_out: bfloat16 [4, 2048, 960], P('dp', 'ctx')
- input_grad: float32 [4, 2048, 960], P('dp', 'ctx')
- query_grad: float32 [960, 960], P('ctx', 'dp')
- key_grad: float32 [960, 320], P('ctx', 'dp')
- value_grad: float32 [960, 320], P('ctx', 'dp')
- out_grad: float32 [960, 960], P('dp', 'ctx')
- gate_grad: float32 [960, 2560], P('ctx', 'dp')
- up_grad: float32 [960, 2560], P('ctx', 'dp')
- down_grad: float32 [2560, 960], P('dp', 'ctx')
- gains_grad: float32 [2, 960], P('dp', 'ctx')
The draws below stay inside these ranges and needn't reach their ends.
All inputs are finite; a program needn't handle non-finite values.
Results may differ from the reference program's by a relative error of at most 0.02.
Values may be sent and summed in bfloat16 or wider, within the bound.
No kernel may reach another device: no remote copies, remote signals or barrier semaphores. Data moves between devices by JAX's collectives and lax.ppermute only.
A program may use at most 256 MiB of HBM per device.

```python
import math
import jax
import jax.numpy as jnp
from jax import lax

MODEL_WIDTH_SIZE = 960
FF = 2560
QUERY_HEAD_COUNT = 15
KEY_VALUE_HEADS = 5
HEAD_WIDTH = 64
BATCH = 4
LENGTH = 2048


def draw_inputs(key, part):
    return jnp.clip(jax.random.normal(jax.random.fold_in(key, 11), (BATCH, LENGTH, MODEL_WIDTH_SIZE), jnp.float32), -6.0, 6.0).astype(jnp.bfloat16)


def draw_query_weight(key, part):
    column_list = QUERY_HEAD_COUNT * HEAD_WIDTH
    return (jnp.clip(jax.random.normal(jax.random.fold_in(key, 21), (MODEL_WIDTH_SIZE, column_list), jnp.float32), -4.0, 4.0) * MODEL_WIDTH_SIZE ** (-0.5)).astype(jnp.bfloat16)


def draw_key_weight(key, part):
    column_list = KEY_VALUE_HEADS * HEAD_WIDTH
    return (jnp.clip(jax.random.normal(jax.random.fold_in(key, 31), (MODEL_WIDTH_SIZE, column_list), jnp.float32), -4.0, 4.0) * MODEL_WIDTH_SIZE ** (-0.5)).astype(jnp.bfloat16)


def raised(values, own_key, source, target, parts, factor):
    def block_of(axis_at):
        return (jnp.arange(values.shape[axis_at]) // (values.shape[axis_at] // parts)).reshape((-1,) + (1,) * (values.ndim - 1 - axis_at))

    first = jax.random.permutation(own_key, parts)[block_of(target)]
    other_side = (block_of(target) + parts // 2) % parts
    return jnp.where((block_of(source) == first) | (block_of(source) == other_side), factor * values, values)


def level_of(rng, shape, pieces, least, high):
    factor_of, own = 1.0, jax.random.fold_in(rng, 6)
    for dim, blocks in pieces:
        heights = jnp.exp(jax.random.uniform(jax.random.fold_in(own, dim), (blocks,), jnp.float32, least / len(pieces), high / len(pieces)))
        factor_of = factor_of * jnp.repeat(heights, shape[dim] // blocks).reshape([-1 if axis == dim else 1 for axis in range(len(shape))])
    return factor_of


def scatter_about(key, shape, width, bound, pieces=(), kind=jnp.bfloat16):
    array = jax.random.normal(key, shape, jnp.float32) * width
    if len(pieces) > 0:
        array = level_of(key, shape, pieces, -0.22, 0.18) * array
    return jnp.clip(array, min=-bound, max=bound).astype(kind)


def noise_with(key, extent, spread, bound, pieces, heavy, kind=jnp.bfloat16):
    array = spread * jax.random.normal(key, extent, jnp.float32)
    if pieces:
        array = array * level_of(key, extent, pieces, -0.22, 0.18)
    return jnp.clip(raised(array, jax.random.fold_in(key, 3), *heavy), -bound, bound).astype(kind)


def setup_inputs(seed: int = 0) -> dict:
    streams_of = jax.random.split(jax.random.key(seed), 11)
    return {
        "inputs": draw_inputs(jax.random.fold_in(streams_of[10], 71), 0),
        "query_weight": draw_query_weight(jax.random.fold_in(streams_of[10], 71), 0),
        "key_weight": draw_key_weight(jax.random.fold_in(streams_of[10], 71), 0),
        "value_matrix": scatter_about(streams_of[3], (MODEL_WIDTH_SIZE, KEY_VALUE_HEADS * HEAD_WIDTH), MODEL_WIDTH_SIZE ** -0.5, 0.1875, ((0, 16), (1, 2))),
        "out_weight": scatter_about(streams_of[4], (QUERY_HEAD_COUNT * HEAD_WIDTH, MODEL_WIDTH_SIZE), (QUERY_HEAD_COUNT * HEAD_WIDTH // 64) ** -0.5, 1.5, ((0, 2), (1, 16))),
        "gate_weight": scatter_about(streams_of[5], (MODEL_WIDTH_SIZE, FF), MODEL_WIDTH_SIZE ** -0.5, 0.1875, ((0, 16), (1, 2))),
        "up_weight": scatter_about(streams_of[6], (MODEL_WIDTH_SIZE, FF), MODEL_WIDTH_SIZE ** -0.5, 0.1875, ((0, 16), (1, 2))),
        "down_weight": scatter_about(streams_of[7], (FF, MODEL_WIDTH_SIZE), FF ** -0.5, 0.125, ((0, 2), (1, 16))),
        "norm_gains": jnp.clip(1.0 + 0.1 * jax.random.normal(streams_of[8], (2, MODEL_WIDTH_SIZE), jnp.float32), 0.5, 1.5).astype(jnp.bfloat16),
        "cotangent": noise_with(streams_of[9], (BATCH, LENGTH, MODEL_WIDTH_SIZE), 1.0, 6.0, ((0, 2), (1, 16)), (1, 2, 16, 2.0)),
    }


EPSILON = 1e-05
PRECISE = lax.Precision.HIGHEST

@jax.custom_vjp
def lower_bound(v):
    return lax.optimization_barrier(v.astype(jnp.bfloat16)).astype(jnp.float32)

@jax.custom_vjp
def low_back(v):
    return v

def low_keep(v):
    return (lower_bound(v), None)

def low_pass(kept, grad):
    return (grad,)

def back_keep(v):
    return (v, None)

def back_low(kept, grad):
    return (lower_bound(grad),)
lower_bound.defvjp(low_keep, low_pass)
low_back.defvjp(back_keep, back_low)

def block_size(rows):
    current_size = 512
    while rows % current_size:
        current_size //= 2
    return current_size

def rope_tables(positions, half_width):
    spectrum = jnp.exp(jnp.arange(half_width, dtype=jnp.float32) * (-math.log(100000.0) / half_width))
    angles = positions.astype(jnp.float32)[:, None] * spectrum[None, :]
    return (jnp.cos(angles), jnp.sin(angles))

def apply_rotation(vectors, cosine_table, sine_table):
    half_width = vectors.shape[-1] // 2
    low_half = vectors[..., :half_width]
    high_half = vectors[..., half_width:]
    cos_rows = cosine_table[:, None, :]
    sin_rows = sine_table[:, None, :]
    return jnp.concatenate([low_half * cos_rows - high_half * sin_rows, high_half * cos_rows + low_half * sin_rows], axis=-1)

def attend_rows(query_rows, key_rows, value_row_list, first_row):
    rows_here = query_rows.shape[0]
    raw_scores = jnp.einsum('rkgd,tkd->kgrt', query_rows, key_rows, precision=PRECISE)
    scores = low_back(raw_scores * 0.125)
    query_pos = first_row + jnp.arange(rows_here, dtype=jnp.int32)
    key_pos = jnp.arange(key_rows.shape[0], dtype=jnp.int32)
    allowed = query_pos[:, None] >= key_pos[None, :]
    scores = jnp.where(allowed[None, None, :, :], scores, -1e+30)
    log_total = jax.nn.logsumexp(scores, axis=-1, keepdims=True)
    probs = lower_bound(jnp.exp(scores - log_total))
    return jnp.einsum('kgrt,tkd->rkgd', probs, value_row_list, precision=PRECISE)

def block_layer(sequence, query_weight, key_weight, value_matrix, out_weight, gate_weight, up_weight, down_weight, norm_gains):
    sequence_length = sequence.shape[0]
    inv_first = lax.rsqrt(lax.optimization_barrier(jnp.mean(sequence * sequence, axis=-1, keepdims=True)) + EPSILON)
    normed = lower_bound(sequence * inv_first * norm_gains[0])
    query_linear = low_back(jnp.dot(normed, query_weight, precision=PRECISE))
    key_mapping = low_back(jnp.dot(normed, key_weight, precision=PRECISE))
    value_entries = lower_bound(low_back(jnp.dot(normed, value_matrix, precision=PRECISE)))
    positions = jnp.arange(sequence_length, dtype=jnp.int32)
    cosine_table, sine_table = rope_tables(positions, HEAD_WIDTH // 2)
    query_rows = lower_bound(apply_rotation(query_linear.reshape(sequence_length, QUERY_HEAD_COUNT, HEAD_WIDTH), cosine_table, sine_table))
    rotated_keys = lower_bound(apply_rotation(key_mapping.reshape(sequence_length, KEY_VALUE_HEADS, HEAD_WIDTH), cosine_table, sine_table))
    value_row_list = value_entries.reshape(sequence_length, KEY_VALUE_HEADS, HEAD_WIDTH)
    current_size = block_size(sequence_length)
    query_block_list = query_rows.reshape(sequence_length // current_size, current_size, KEY_VALUE_HEADS, QUERY_HEAD_COUNT // KEY_VALUE_HEADS, HEAD_WIDTH)
    starts = jnp.arange(sequence_length // current_size, dtype=jnp.int32) * current_size

    def attend(block_pair):
        return attend_rows(block_pair[0], rotated_keys, value_row_list, block_pair[1])
    attended = lax.map(jax.checkpoint(attend), (query_block_list, starts)).reshape(sequence_length, QUERY_HEAD_COUNT * HEAD_WIDTH)
    attended = lower_bound(low_back(attended))
    middle = sequence + low_back(jnp.dot(attended, out_weight, precision=PRECISE))
    inv_second = lax.rsqrt(lax.optimization_barrier(jnp.mean(middle * middle, axis=-1, keepdims=True)) + EPSILON)
    mixed_in = lower_bound(middle * inv_second * norm_gains[1])
    gate_linear = low_back(jnp.dot(mixed_in, gate_weight, precision=PRECISE))
    lift_linear = low_back(jnp.dot(mixed_in, up_weight, precision=PRECISE))
    hidden = lower_bound(jax.nn.silu(gate_linear) * lift_linear)
    return middle + low_back(jnp.dot(hidden, down_weight, precision=PRECISE))

def reference(inputs, query_weight, key_weight, value_matrix, out_weight, gate_weight, up_weight, down_weight, norm_gains, cotangent):
    params = (query_weight.astype(jnp.float32), key_weight.astype(jnp.float32), value_matrix.astype(jnp.float32), out_weight.astype(jnp.float32), gate_weight.astype(jnp.float32), up_weight.astype(jnp.float32), down_weight.astype(jnp.float32), norm_gains.astype(jnp.float32))

    def one_sequence(running, sequence_pair):
        sequence, sequence_grad = sequence_pair
        result, pullback = jax.vjp(block_layer, sequence.astype(jnp.float32), *params)
        gradients = pullback(sequence_grad.astype(jnp.float32))
        running = tuple((earlier + grad_now for earlier, grad_now in zip(running, gradients[1:])))
        return (running, (result.astype(jnp.bfloat16), gradients[0]))
    initial = tuple((jnp.zeros_like(weight_now) for weight_now in params))
    running, (outputs, input_grads) = lax.scan(one_sequence, initial, (inputs, cotangent))
    return (outputs, input_grads, running[0], running[1], running[2], running[3], running[4], running[5], running[6], running[7])
```

```python
import functools
import math

import jax
import jax.numpy as jnp
import numpy as np
from jax import lax
from jax.experimental import pallas as pl
from jax.experimental.pallas import tpu as pltpu
from jax.sharding import Mesh, PartitionSpec as P

HEAD = 64
EPSILON = 1e-05
MASKED = -1e30
FLOOR = -1e20
LOG2E = 1.4426950408889634
SCALE = 0.125 * LOG2E
BF = jnp.bfloat16
F32 = jnp.float32
SWAP = [(0, 1), (1, 0)]


def dot(a, b, ca, cb):
    return lax.dot_general(a, b, (((ca,), (cb,)), ((), ())), preferred_element_type=F32)


def rope_tables(positions, half):
    spectrum = jnp.exp(jnp.arange(half, dtype=F32) * (-math.log(100000.0) / half))
    angles = spectrum[:, None] * positions.astype(F32)[None, :]
    return jnp.cos(angles), jnp.sin(angles)


def rotate(vectors, cos, sin):
    rows = vectors.shape[-1]
    halves = vectors.reshape(-1, 2, HEAD // 2, rows)
    low, high = halves[:, 0], halves[:, 1]
    return jnp.stack([low * cos - high * sin, high * cos + low * sin], axis=1).reshape(-1, rows)


def allowed_mask(y, keys, rows):
    key_pos = lax.broadcasted_iota(jnp.int32, (keys, rows), 0) + y * keys
    row_pos = lax.broadcasted_iota(jnp.int32, (keys, rows), 1)
    return row_pos >= key_pos


def forward_kernel(line, group, place, q_ref, *refs):
    k_refs, v_refs = refs[:line], refs[line : 2 * line]
    o_ref, lse_ref, m_ref, l_ref, acc_ref = refs[2 * line :]
    z, y = place[0], place[1]
    keys, rows = k_refs[0].shape[1], q_ref.shape[1]
    for h in range(group):
        q = q_ref[h * HEAD : (h + 1) * HEAD, :]
        scores = dot(k_refs[0][...], q, 0, 0) * SCALE
        scores = jnp.where(allowed_mask(y, keys, rows), scores, MASKED)
        top = jnp.maximum(jnp.max(scores, axis=0, keepdims=True), FLOOR)
        probs = jnp.exp2(scores - top)
        m_ref[...] = top
        l_ref[...] = jnp.sum(probs, axis=0, keepdims=True)
        acc_ref[...] = dot(v_refs[0][...], probs.astype(BF), 1, 0)
        for s in range(1, line):

            @pl.when(s <= z)
            def _():
                scores = dot(k_refs[s][...], q, 0, 0) * SCALE
                old = m_ref[...]
                top = jnp.maximum(jnp.max(scores, axis=0, keepdims=True), old)
                probs = jnp.exp2(scores - top)
                shrink = jnp.exp2(old - top)
                m_ref[...] = top
                l_ref[...] = l_ref[...] * shrink + jnp.sum(probs, axis=0, keepdims=True)
                acc_ref[...] = acc_ref[...] * shrink + dot(v_refs[s][...], probs.astype(BF), 1, 0)

        total = l_ref[...]
        o_ref[h * HEAD : (h + 1) * HEAD, :] = acc_ref[...] / jnp.maximum(total, 1e-30)
        lse_ref[0, h : h + 1, :] = jnp.where(
            total > 0, m_ref[...] + jnp.log2(jnp.maximum(total, 1e-30)), MASKED
        )


def attend_forward(place, q, kvs, kv_heads):
    line = len(kvs)
    width, rows = q.shape
    group = width // HEAD // kv_heads
    keys = kvs[0].shape[1]
    k_specs = [pl.BlockSpec((HEAD, keys), lambda g: (g, 0))] * line
    v_specs = [pl.BlockSpec((HEAD, keys), lambda g: (g + kv_heads, 0))] * line
    pairs = width // HEAD * keys * line * rows
    return pl.pallas_call(
        functools.partial(forward_kernel, line, group),
        grid=(kv_heads,),
        in_specs=[
            pl.BlockSpec(memory_space=pltpu.SMEM),
            pl.BlockSpec((group * HEAD, rows), lambda g: (g, 0)),
            *k_specs,
            *v_specs,
        ],
        out_specs=[
            pl.BlockSpec((group * HEAD, rows), lambda g: (g, 0)),
            pl.BlockSpec((1, 8, rows), lambda g: (g, 0, 0)),
        ],
        out_shape=[
            jax.ShapeDtypeStruct((width, rows), F32),
            jax.ShapeDtypeStruct((kv_heads, 8, rows), F32),
        ],
        scratch_shapes=[
            pltpu.VMEM((1, rows), F32),
            pltpu.VMEM((1, rows), F32),
            pltpu.VMEM((HEAD, rows), F32),
        ],
        cost_estimate=pl.CostEstimate(
            flops=pairs * HEAD * 4, bytes_accessed=6 * width * rows, transcendentals=pairs
        ),
        compiler_params=pltpu.CompilerParams(vmem_limit_bytes=40 * 2**20),
        name="attend_forward",
    )(place, q, *kvs, *kvs)


def backward_kernel(
    step, group, has_more, place, q_ref, do_ref, lse_ref, dot_ref, k_ref, v_ref, *refs
):
    if has_more:
        more_k, more_v, dq_in, dq_ref, dk_ref, dv_ref = refs
    else:
        dq_ref, dk_ref, dv_ref = refs
    z, y = place[0], place[1]
    keys, rows = k_ref.shape[1], q_ref.shape[1]

    @pl.when(step <= z)
    def _():
        key, value = k_ref[...], v_ref[...]
        if has_more:
            dk, dv = more_k[...].astype(F32), more_v[...].astype(F32)
        else:
            dk = dv = jnp.zeros((HEAD, keys), F32)
        for h in range(group):
            at = slice(h * HEAD, (h + 1) * HEAD)
            q, do = q_ref[at, :], do_ref[at, :]
            scores = dot(key, q, 0, 0) * SCALE
            probs = jnp.exp2(scores - lse_ref[0, h : h + 1, :])
            if step == 0:
                probs = jnp.where(allowed_mask(y, keys, rows), probs, 0.0)
            back_probs = dot(value, do, 0, 0)
            back = (probs * (back_probs - dot_ref[0, h : h + 1, :])).astype(BF)
            dv = dv + dot(do, probs.astype(BF), 1, 1)
            dk = dk + dot(q, back, 1, 1) * 0.125
            dq = dot(key, back, 1, 0) * 0.125
            if has_more:
                dq = dq + dq_in[at, :]
            dq_ref[at, :] = dq
        dk_ref[...] = dk.astype(dk_ref.dtype)
        dv_ref[...] = dv.astype(dv_ref.dtype)

    @pl.when(step > z)
    def _():
        dq_ref[...] = jnp.zeros_like(dq_ref)
        dk_ref[...] = jnp.zeros_like(dk_ref)
        dv_ref[...] = jnp.zeros_like(dv_ref)


def attend_backward(place, step, q, do, lse, row_dot, kv, more, dq, kv_heads):
    width, rows = q.shape
    group = width // HEAD // kv_heads
    keys = kv.shape[1]
    has_more = more is not None
    wide = pl.BlockSpec((group * HEAD, rows), lambda g: (g, 0))
    stat = pl.BlockSpec((1, 8, rows), lambda g: (g, 0, 0))
    first = pl.BlockSpec((HEAD, keys), lambda g: (g, 0))
    second = pl.BlockSpec((HEAD, keys), lambda g: (g + kv_heads, 0))
    kind = F32 if step == 0 else BF
    pairs = width // HEAD * keys * rows
    return pl.pallas_call(
        functools.partial(backward_kernel, step, group, has_more),
        grid=(kv_heads,),
        in_specs=[pl.BlockSpec(memory_space=pltpu.SMEM), wide, wide, stat, stat, first, second]
        + ([first, second, wide] if has_more else []),
        out_specs=[wide, first, first],
        out_shape=[
            jax.ShapeDtypeStruct((width, rows), F32),
            jax.ShapeDtypeStruct((kv_heads * HEAD, keys), kind),
            jax.ShapeDtypeStruct((kv_heads * HEAD, keys), kind),
        ],
        cost_estimate=pl.CostEstimate(
            flops=pairs * HEAD * 10, bytes_accessed=12 * width * rows, transcendentals=pairs
        ),
        compiler_params=pltpu.CompilerParams(vmem_limit_bytes=40 * 2**20),
        name=f"attend_backward_{step}",
    )(place, q, do, lse, row_dot, kv, kv, *((more, more, dq) if has_more else ()))


def padded(count):
    return -(-count // 8) * 8


def pick(pair, index):
    return jnp.where(index == 0, pair[0], pair[1])


def body(
    inputs,
    query_weight,
    key_weight,
    value_matrix,
    out_weight,
    gate_weight,
    up_weight,
    down_weight,
    norm_gains,
    cotangent,
):
    seqs, part_rows, model = inputs.shape
    dps, line = lax.axis_size("dp"), lax.axis_size("z")
    ctx = line * 4
    z, y, c, d = (lax.axis_index(a) for a in ("z", "y", "c", "dp"))
    shard = model // ctx
    slot = padded(shard + 1)
    wide = slot * ctx
    rows = 2 * part_rows
    up_line = [(i, i + 1) for i in range(line - 1)]
    down_line = [(i + 1, i) for i in range(line - 1)]

    q_part, k_part = query_weight.shape[1], key_weight.shape[1]
    qkv_part = q_part + 2 * k_part
    half_ff = gate_weight.shape[1]
    kv_heads = k_part * dps // HEAD
    q_heads = q_part * dps // HEAD
    group = q_heads // kv_heads

    small = jnp.concatenate([query_weight, key_weight, value_matrix, out_weight.T], axis=1)
    gain_row = jnp.pad(norm_gains, ((0, slot - shard - 1), (0, small.shape[1] - shard)))
    small = jnp.concatenate([small, gain_row], axis=0)
    small = lax.all_gather(small, ("dp", "z", "y", "c"), axis=0, tiled=True)
    small = small.reshape(dps, wide, -1)
    large = jnp.concatenate([gate_weight, up_weight, down_weight.T], axis=1)
    large = jnp.pad(large, ((0, slot - shard), (0, 0)))
    large = lax.all_gather(large, ("z", "y", "c"), axis=0, tiled=True)
    w_gate, w_up, w_down = (large[:, i * half_ff : (i + 1) * half_ff] for i in range(3))

    both = jnp.stack([inputs, cotangent], axis=1)
    mine, theirs = pick((both[0], both[1]), c), pick((both[1], both[0]), c)
    theirs = lax.ppermute(theirs, "c", SWAP)
    first, second = pick((mine, theirs), c), pick((theirs, mine), c)
    both = jnp.concatenate([first, second], axis=1)
    spread_row = lax.broadcasted_iota(jnp.int32, (model, wide), 0)
    spread_col = lax.broadcasted_iota(jnp.int32, (model, wide), 1)
    spread = (
        (spread_row // shard == spread_col // slot) & (spread_row % shard == spread_col % slot)
    ).astype(BF)
    tokens = dot(both[0], spread, 1, 0)
    back_out = dot(both[1], spread, 1, 0)
    back_out_low = back_out.astype(BF)

    gains = small.reshape(dps, ctx, slot, -1)[:, :, shard, :shard]
    gains = jnp.pad(gains, ((0, 0), (0, 0), (0, slot - shard))).reshape(dps, wide).astype(F32)
    real = (jnp.arange(wide) % slot < shard)[None, :]

    inv_first = lax.rsqrt(jnp.sum(tokens * tokens, axis=-1, keepdims=True) / model + EPSILON)
    unit_first = tokens * inv_first
    normed = (unit_first * gains[0]).astype(BF)
    heads = [dot(small[i, :, :qkv_part], normed, 0, 1) for i in range(dps)]
    q_lin = jnp.concatenate([h[:q_part] for h in heads], axis=0)
    k_lin = jnp.concatenate([h[q_part : q_part + k_part] for h in heads], axis=0)
    v_lin = jnp.concatenate([h[q_part + k_part :] for h in heads], axis=0)
    positions = (2 * z + y) * rows + jnp.arange(rows, dtype=jnp.int32)
    cos, sin = rope_tables(positions, HEAD // 2)
    q = rotate(q_lin, cos, sin).astype(BF)
    kv = jnp.concatenate([rotate(k_lin, cos, sin).astype(BF), v_lin.astype(BF)], axis=0)

    kvs = [kv]
    for _ in range(line - 1):
        kvs.append(lax.ppermute(kvs[-1], "z", up_line))
    q_other = lax.ppermute(q, "y", SWAP)
    q_both = jnp.concatenate([pick((q, q_other), y), pick((q_other, q), y)], axis=1)
    place = jnp.stack([z, y]).astype(jnp.int32)
    o_both, lse_part = attend_forward(place, q_both, kvs, kv_heads)
    o_mine = pick((o_both[:, :rows], o_both[:, rows:]), y)
    o_send = pick((o_both[:, rows:], o_both[:, :rows]), y).astype(BF)
    o_other = lax.ppermute(o_send, "y", SWAP)
    lse_other = lax.ppermute(lse_part, "y", SWAP)
    top = jnp.maximum(lse_part, lse_other)
    lse = top + jnp.log2(jnp.exp2(lse_part - top) + jnp.exp2(lse_other - top))
    w_mine, w_other = (
        jnp.exp2(pick((s[..., :rows] - lse[..., :rows], s[..., rows:] - lse[..., rows:]), y))
        .at[:, :group]
        .get()
        .reshape(q_heads, 1, rows)
        for s in (lse_part, lse_other)
    )
    attended = (
        o_mine.reshape(q_heads, HEAD, rows) * w_mine
        + o_other.reshape(q_heads, HEAD, rows).astype(F32) * w_other
    )
    attended = attended.reshape(-1, rows).astype(BF)
    half_q = q_part
    proj = sum(
        dot(attended[i * half_q : (i + 1) * half_q], small[i, :, qkv_part:], 0, 1)
        for i in range(dps)
    )
    middle = tokens + jnp.where(real, proj, 0.0)
    inv_second = lax.rsqrt(jnp.sum(middle * middle, axis=-1, keepdims=True) / model + EPSILON)
    unit_second = middle * inv_second
    mixed_own = (unit_second * gains[1]).astype(BF)

    mixed_far = lax.ppermute(mixed_own, "dp", SWAP)
    back_far = lax.ppermute(back_out_low, "dp", SWAP)
    results = []
    for mixed, back in ((mixed_far, back_far), (mixed_own, back_out_low)):
        gate = dot(mixed, w_gate, 1, 0)
        lift = dot(mixed, w_up, 1, 0)
        sig = jax.nn.sigmoid(gate)
        hidden = (gate * sig * lift).astype(BF)
        back_hidden = dot(back, w_down, 1, 0)
        back_gate = (back_hidden * lift * sig * (1.0 + gate * (1.0 - sig))).astype(BF)
        back_lift = (back_hidden * gate * sig).astype(BF)
        partial = dot(hidden, w_down, 1, 1)
        back_mixed = dot(back_gate, w_gate, 1, 1) + dot(back_lift, w_up, 1, 1)
        results.append((hidden, back_gate, back_lift, partial, back_mixed))
    back_mixed = results[1][4] + lax.ppermute(results[0][4].astype(BF), "dp", SWAP).astype(F32)
    result = middle + results[1][3] + lax.ppermute(results[0][3].astype(BF), "dp", SWAP).astype(F32)
    layer_low = result.astype(BF)

    hidden, back_gate, back_lift = (
        jnp.concatenate([results[0][i], results[1][i]], axis=0) for i in range(3)
    )
    mixed = jnp.concatenate([mixed_far, mixed_own], axis=0)
    back = jnp.concatenate([back_far, back_out_low], axis=0)
    grads = jnp.concatenate(
        [
            dot(mixed, back_gate, 0, 0).astype(BF),
            dot(mixed, back_lift, 0, 0).astype(BF),
            dot(back, hidden, 0, 0).astype(BF),
        ],
        axis=1,
    )
    grads = lax.psum_scatter(grads, ("z", "y", "c"), scatter_dimension=0, tiled=True)

    gain_second = jnp.sum(back_mixed * unit_second, axis=0)
    scaled = back_mixed * gains[1]
    back_middle = back_out + inv_second * (
        scaled - unit_second * (jnp.sum(scaled * unit_second, axis=-1, keepdims=True) / model)
    )
    back_proj = back_middle.astype(BF)
    do = jnp.concatenate(
        [dot(small[i, :, qkv_part:], back_proj, 0, 1) for i in range(dps)], axis=0
    ).astype(BF)
    row_dot = jnp.sum(
        do.astype(F32).reshape(q_heads, HEAD, rows)
        * attended.astype(F32).reshape(q_heads, HEAD, rows),
        axis=1,
    )
    row_dot = jnp.pad(row_dot.reshape(kv_heads, group, rows), ((0, 0), (0, 8 - group), (0, 0)))
    do_other = lax.ppermute(do, "y", SWAP)
    dot_other = lax.ppermute(row_dot, "y", SWAP)
    do_both = jnp.concatenate([pick((do, do_other), y), pick((do_other, do), y)], axis=1)
    dot_both = jnp.concatenate(
        [pick((row_dot, dot_other), y), pick((dot_other, row_dot), y)], axis=2
    )
    more = dq = None
    for step in range(line - 1, -1, -1):
        dq, dk, dv = attend_backward(
            place, step, q_both, do_both, lse, dot_both, kvs[step], more, dq, kv_heads
        )
        if step:
            more = lax.ppermute(jnp.concatenate([dk, dv], axis=0), "z", down_line)
    dq_mine = pick((dq[:, :rows], dq[:, rows:]), y)
    dq_send = pick((dq[:, rows:], dq[:, :rows]), y).astype(BF)
    dq = dq_mine + lax.ppermute(dq_send, "y", SWAP).astype(F32)
    dq = rotate(dq, cos, -sin).astype(BF)
    dk = rotate(dk, cos, -sin).astype(BF)
    dv = dv.astype(BF)
    backs = [
        jnp.concatenate(
            [
                dq[i * q_part : (i + 1) * q_part],
                dk[i * k_part : (i + 1) * k_part],
                dv[i * k_part : (i + 1) * k_part],
            ],
            axis=0,
        )
        for i in range(dps)
    ]
    back_normed = sum(dot(backs[i], small[i, :, :qkv_part], 0, 1) for i in range(dps))
    gain_first = jnp.sum(back_normed * unit_first, axis=0)
    scaled = back_normed * gains[0]
    input_grad = back_middle + inv_first * (
        scaled - unit_first * (jnp.sum(scaled * unit_first, axis=-1, keepdims=True) / model)
    )

    terms = []
    for i in range(dps):
        term = jnp.concatenate(
            [
                dot(normed, backs[i], 0, 1).astype(BF),
                dot(back_proj, attended[i * half_q : (i + 1) * half_q], 0, 1).astype(BF),
            ],
            axis=1,
        )
        terms.append(term)
    small_grads = jnp.stack(terms).reshape(dps, line, 2, 2, slot, -1)
    gain_terms = jnp.stack([gain_first, gain_second]).reshape(dps, line, 2, 2, slot)
    gain_terms = gain_terms[..., :shard].astype(BF)
    small_grads = small_grads.at[:, :, :, :, shard, :shard].set(gain_terms)

    def fold(array, axis, name, index):
        parts = jnp.split(array, 2, axis=axis)
        keep = pick(parts, index).squeeze(axis)
        send = pick((parts[1], parts[0]), index).squeeze(axis)
        return (keep.astype(F32) + lax.ppermute(send, name, SWAP).astype(F32)).astype(BF)

    small_grads = fold(small_grads, 3, "c", c)
    columns = small_grads.shape[-1] // 2
    left, right = small_grads[..., :columns], small_grads[..., columns:]
    left = fold(fold(left, 0, "dp", d), 1, "y", y)
    right = fold(fold(right, 2, "y", y), 0, "dp", d)
    small_grads = jnp.concatenate([left, right], axis=-1)
    small_grads = lax.all_to_all(small_grads, "z", split_axis=0, concat_axis=0)
    small_grads = jnp.sum(small_grads.astype(F32), axis=0)
    final_gains = small_grads[shard : shard + 1, :shard]
    small_grads = small_grads[:shard]
    final_query = small_grads[:, :q_part]
    final_key = small_grads[:, q_part : q_part + k_part]
    final_value = small_grads[:, q_part + k_part : qkv_part]
    final_out = small_grads[:, qkv_part:].T

    grads = grads[:shard].astype(F32)
    final_gate, final_lift, final_down = (
        grads[:, i * half_ff : (i + 1) * half_ff] for i in range(3)
    )

    def give_back(array):
        mine, theirs = (
            pick((array[:part_rows], array[part_rows:]), c),
            pick((array[part_rows:], array[:part_rows]), c),
        )
        theirs = lax.ppermute(theirs, "c", SWAP)
        return jnp.stack([pick((mine, theirs), c), pick((theirs, mine), c)])

    layer_out = dot(layer_low, spread, 1, 1).astype(BF)
    input_grad = input_grad.reshape(rows, ctx, slot)[:, :, :shard].reshape(rows, model)
    return (
        give_back(layer_out),
        give_back(input_grad),
        final_query,
        final_key,
        final_value,
        final_out,
        final_gate,
        final_lift,
        final_down.T,
        final_gains,
    )


def solution(mesh):
    devices = mesh.devices
    dps, ctx = devices.shape
    inner = Mesh(devices.reshape(dps, ctx // 4, 2, 2), ("dp", "z", "y", "c"))
    along = ("z", "y", "c")
    rows, by_row, by_col = P("dp", along, None), P(along, "dp"), P("dp", along)
    return jax.shard_map(
        body,
        mesh=inner,
        in_specs=(
            rows, by_row, by_row, by_row, by_col, by_row, by_row, by_col, by_col, rows,
        ),
        out_specs=(
            rows, rows, by_row, by_row, by_row, by_col, by_row, by_row, by_col, by_col,
        ),
        check_vma=False,
    )
```

```python
import functools
import math

import jax
import jax.numpy as jnp
from jax import lax
from jax.experimental import pallas as pl
from jax.experimental.pallas import tpu as pltpu
from jax.sharding import Mesh, PartitionSpec as P

HEAD = 64
HALF_HEAD = HEAD // 2
EPSILON = 1e-05
MASKED = -1e30
FLOOR = -1e20
LOG2E = 1.4426950408889634
SCALE = 0.125 * LOG2E
BF = jnp.bfloat16
F32 = jnp.float32
SWAP = [(0, 1), (1, 0)]
COST = pl.CostEstimate(flops=1000, bytes_accessed=1000, transcendentals=0)
VMEM = pl.BlockSpec(memory_space=pltpu.VMEM)
SMEM = pl.BlockSpec(memory_space=pltpu.SMEM)


def params(mib=32):
    return pltpu.CompilerParams(vmem_limit_bytes=mib * 2**20)


def dot(a, b, ca, cb):
    return lax.dot_general(a, b, (((ca,), (cb,)), ((), ())), preferred_element_type=F32)


def full(array):
    return pl.BlockSpec(array.shape, lambda i: (0,) * len(array.shape))


def like(shape, kind):
    return jax.ShapeDtypeStruct(shape, kind)


def rope_tables(positions, half):
    spectrum = jnp.exp(jnp.arange(half, dtype=F32) * (-math.log(100000.0) / half))
    angles = spectrum[:, None] * positions.astype(F32)[None, :]
    return jnp.cos(angles), jnp.sin(angles)


def project_kernel(
    q_part, k_part, cut, normed_ref, cos_ref, sin_ref, lm, rm, lt, rt, q_ref, kv_ref, raw_ref
):
    sides, ys, block, _ = lm.shape
    half = ys * block
    for x in range(sides):
        left = right = None
        for side, (l, r) in enumerate(((lm, rm), (lt, rt))):
            for y in range(ys):
                at = side * half + y * block
                rows = normed_ref[at : at + block, :]
                a, b = dot(l[x, y], rows, 0, 0), dot(r[y, x], rows, 0, 0)
                left = a if left is None else left + a
                right = b if right is None else right + b
        raw_ref[x, :cut, :] = left
        raw_ref[x, cut:, :] = right
    cos, sin = cos_ref[...], sin_ref[...]

    def half_rows(part, base, index):
        x, at = divmod(index * HALF_HEAD, part)
        return raw_ref[x, base + at : base + at + HALF_HEAD, :]

    def turn(part, base, out_ref, heads):
        for h in range(heads):
            low, high = half_rows(part, base, 2 * h), half_rows(part, base, 2 * h + 1)
            out_ref[h * HEAD : h * HEAD + HALF_HEAD, :] = (low * cos - high * sin).astype(BF)
            out_ref[h * HEAD + HALF_HEAD : (h + 1) * HEAD, :] = (high * cos + low * sin).astype(BF)

    turn(q_part, 0, q_ref, sides * q_part // HEAD)
    turn(k_part, q_part, kv_ref, sides * k_part // HEAD)
    for x in range(sides):
        base = sides * k_part + x * k_part
        kv_ref[base : base + k_part, :] = raw_ref[
            x, q_part + k_part : q_part + 2 * k_part, :
        ].astype(BF)


def project(normed, cos, sin, mine, theirs, q_part, k_part):
    sides, _, _, cut = mine[0].shape
    rows = normed.shape[1]
    return pl.pallas_call(
        functools.partial(project_kernel, q_part, k_part, cut),
        in_specs=[VMEM] * 7,
        out_specs=[VMEM] * 2,
        out_shape=[like((sides * q_part, rows), BF), like((2 * sides * k_part, rows), BF)],
        scratch_shapes=[pltpu.VMEM((sides, cut + mine[1].shape[3], rows), F32)],
        cost_estimate=COST,
        compiler_params=params(),
        name="project",
    )(normed, cos, sin, *mine, *theirs)


def abreast(group, own, far, at):
    parts = []
    for h in range(group):
        parts.append(own[at(h)])
        if far is not None:
            parts.append(far[at(h)])
    return jnp.concatenate(parts, axis=1) if len(parts) > 1 else parts[0]


def head_rows(h):
    return (slice(h * HEAD, (h + 1) * HEAD), slice(None))


def stat_row(h):
    return (0, slice(h, h + 1), slice(None))


def causal(keys, rows, group, both):
    key_pos = lax.broadcasted_iota(jnp.int32, (keys, rows), 0)
    own = lax.broadcasted_iota(jnp.int32, (keys, rows), 1) >= key_pos
    parts = [own, jnp.ones_like(own)] if both else [own]
    return jnp.concatenate(parts * group, axis=1)


def forward_kernel(step, last, group, place, q_ref, far_q_ref, k_ref, v_ref, *refs):
    rows = q_ref.shape[1]
    stat_ref, acc_ref, far_stat_ref, far_acc_ref = refs[-4:]

    def visit(both):
        far = (lambda ref: ref) if both else (lambda ref: None)
        scores = dot(k_ref[...], abreast(group, q_ref, far(far_q_ref), head_rows), 0, 0) * SCALE
        if step == 0:
            scores = jnp.where(causal(scores.shape[0], rows, group, both), scores, MASKED)
        top = jnp.max(scores, axis=0, keepdims=True)
        if step:
            old = abreast(group, refs[0], refs[2], stat_row)
            top = jnp.maximum(top, old)
            shrink = jnp.exp2(old - top)
        probs = jnp.exp2(scores - top)
        total = jnp.sum(probs, axis=0, keepdims=True)
        if step:
            total = total + abreast(group, refs[0], refs[2], lambda h: stat_row(group + h)) * shrink
        acc = dot(v_ref[...], probs.astype(BF), 1, 0)
        sides = ((0, stat_ref, acc_ref), (1, far_stat_ref, far_acc_ref)) if both else ((0, stat_ref, acc_ref),)
        for h in range(group):
            for side, stats, out in sides:
                at = (h * len(sides) + side) * rows
                at = slice(at, at + rows)
                value = acc[:, at]
                if step:
                    value = value + refs[2 * side + 1][head_rows(h)] * shrink[:, at]
                out[head_rows(h)] = value.astype(out.dtype)
                stats[stat_row(h)] = top[:, at]
                stats[stat_row(group + h)] = total[:, at]

    if step == 0:
        pl.when(place[1] == 0)(lambda: visit(True))

        @pl.when(place[1] != 0)
        def _():
            visit(False)
            far_stat_ref[0, :group, :] = jnp.full((group, rows), FLOOR, F32)
            far_stat_ref[0, group : 2 * group, :] = jnp.zeros((group, rows), F32)
            far_acc_ref[...] = jnp.zeros_like(far_acc_ref)
    else:
        pl.when(step <= place[0])(lambda: visit(True))

        @pl.when(step > place[0])
        def _():
            for old, new in zip(refs[:4], refs[-4:]):
                new[...] = old[...].astype(new.dtype)


def attend_forward(place, step, last, q, far_q, kv, state, kv_heads):
    width, rows = q.shape
    group = width // HEAD // kv_heads
    keys = kv.shape[1]
    wide = pl.BlockSpec((group * HEAD, rows), lambda g: (g, 0))
    stat = pl.BlockSpec((1, 8, rows), lambda g: (g, 0, 0))
    first = pl.BlockSpec((HEAD, keys), lambda g: (g, 0))
    second = pl.BlockSpec((HEAD, keys), lambda g: (g + kv_heads, 0))
    stats = like((kv_heads, 8, rows), F32)
    aliases = {5: 0, 6: 1, 7: 2} if last else {5: 0, 6: 1, 7: 2, 8: 3}
    return pl.pallas_call(
        functools.partial(forward_kernel, step, last, group),
        grid=(kv_heads,),
        in_specs=[SMEM, wide, wide, first, second] + ([stat, wide] * 2 if step else []),
        out_specs=[stat, wide] * 2,
        out_shape=[stats, like((width, rows), F32), stats, like((width, rows), BF if last else F32)],
        input_output_aliases=aliases if step else {},
        cost_estimate=COST,
        compiler_params=params(12),
        name=f"attend_forward_{step}",
    )(place, q, far_q, kv, kv, *state)


def backward_kernel(
    step, group, place, q_ref, far_q_ref, do_ref, far_do_ref, lse_ref, far_lse_ref, dot_ref,
    far_dot_ref, k_ref, v_ref, *refs,
):
    dq_ref, far_dq_ref, dkv_ref = refs[-3:]
    more = len(refs) > 3
    rows = q_ref.shape[1]

    def visit(both):
        key, value = k_ref[...], v_ref[...]
        far = (lambda ref: ref) if both else (lambda ref: None)
        q = abreast(group, q_ref, far(far_q_ref), head_rows)
        do = abreast(group, do_ref, far(far_do_ref), head_rows)
        lse = abreast(group, lse_ref, far(far_lse_ref), stat_row)
        total = abreast(group, dot_ref, far(far_dot_ref), stat_row)
        probs = jnp.exp2(dot(key, q, 0, 0) * SCALE - lse)
        if step == 0:
            probs = jnp.where(causal(probs.shape[0], rows, group, both), probs, 0.0)
        back = (probs * (dot(value, do, 0, 0) - total)).astype(BF)
        dkv_ref[0] = (dot(back, q, 1, 1).T * 0.125).astype(dkv_ref.dtype)
        dkv_ref[1] = dot(probs.astype(BF), do, 1, 1).T.astype(dkv_ref.dtype)
        dq = dot(key, back, 1, 0) * 0.125
        sides = (dq_ref, far_dq_ref) if both else (dq_ref,)
        for h in range(group):
            for side, out in enumerate(sides):
                at = (h * len(sides) + side) * rows
                value = dq[:, at : at + rows]
                if more:
                    value = value + refs[side][head_rows(h)]
                out[head_rows(h)] = value.astype(out.dtype)

    if step == 0:
        pl.when(place[1] == 0)(lambda: visit(True))

        @pl.when(place[1] != 0)
        def _():
            visit(False)
            if more:
                far_dq_ref[...] = refs[1][...].astype(far_dq_ref.dtype)
            else:
                far_dq_ref[...] = jnp.zeros_like(far_dq_ref)
    else:
        pl.when(step <= place[0])(lambda: visit(True))

        @pl.when(step > place[0])
        def _():
            for i, ref in enumerate((dq_ref, far_dq_ref)):
                ref[...] = refs[i][...] if more else jnp.zeros_like(ref)
            dkv_ref[...] = jnp.zeros_like(dkv_ref)


def attend_backward(place, step, q, do, lse, row_dot, kv, dq, kv_heads):
    width, rows = q[0].shape
    group = width // HEAD // kv_heads
    keys = kv.shape[1]
    wide = pl.BlockSpec((group * HEAD, rows), lambda g: (g, 0))
    stat = pl.BlockSpec((1, 8, rows), lambda g: (g, 0, 0))
    first = pl.BlockSpec((HEAD, keys), lambda g: (g, 0))
    second = pl.BlockSpec((HEAD, keys), lambda g: (g + kv_heads, 0))
    kind = BF if step else F32
    aliases = ({11: 0, 12: 1} if step else {11: 0}) if dq else {}
    return pl.pallas_call(
        functools.partial(backward_kernel, step, group),
        grid=(kv_heads,),
        in_specs=[SMEM] + [wide] * 4 + [stat] * 4 + [first, second] + [wide] * len(dq),
        out_specs=[wide, wide, pl.BlockSpec((2, HEAD, keys), lambda g: (0, g, 0))],
        out_shape=[
            like((width, rows), F32),
            like((width, rows), F32 if step else BF),
            like((2, kv_heads * HEAD, keys), kind),
        ],
        input_output_aliases=aliases,
        cost_estimate=COST,
        compiler_params=params(12),
        name=f"attend_backward_{step}",
    )(place, *q, *do, *lse, *row_dot, kv, kv, *dq)


def add_kernel(a_ref, b_ref, out_ref):
    out_ref[...] = (a_ref[...].astype(F32) + b_ref[...].astype(F32)).astype(out_ref.dtype)


def add_low(a, b):
    return pl.pallas_call(
        add_kernel,
        in_specs=[VMEM] * 2,
        out_specs=VMEM,
        out_shape=like(a.shape, BF),
        cost_estimate=COST,
        compiler_params=params(12),
        name="add_low",
    )(a, b)


def middle_kernel(
    kv_heads, model, stat_ref, far_stat_ref, got_ref, far_got_ref, acc_ref, far_ref, w_ref,
    tokens_ref, gain_ref, attended_ref, lse_ref, far_lse_ref, middle_ref, unit_ref, inv_ref, mixed_ref,
):
    group = acc_ref.shape[0] // HEAD // kv_heads
    lse_ref[...] = jnp.zeros_like(lse_ref)
    far_lse_ref[...] = jnp.zeros_like(far_lse_ref)
    for g in range(kv_heads):
        for h in range(group):
            at = slice((g * group + h) * HEAD, (g * group + h + 1) * HEAD)
            m, s = slice(h, h + 1), slice(group + h, group + h + 1)
            top = jnp.maximum(far_stat_ref[g, m, :], far_got_ref[g, m, :])
            total = far_stat_ref[g, s, :] * jnp.exp2(far_stat_ref[g, m, :] - top)
            total = total + far_got_ref[g, s, :] * jnp.exp2(far_got_ref[g, m, :] - top)
            far_lse_ref[g, m, :] = top + jnp.log2(total)
            top = jnp.maximum(stat_ref[g, m, :], got_ref[g, m, :])
            near, far = jnp.exp2(stat_ref[g, m, :] - top), jnp.exp2(got_ref[g, m, :] - top)
            total = stat_ref[g, s, :] * near + got_ref[g, s, :] * far
            lse_ref[g, m, :] = top + jnp.log2(total)
            value = acc_ref[at, :] * (near / total) + far_ref[at, :].astype(F32) * (far / total)
            attended_ref[at, :] = value.astype(BF)
    middle = tokens_ref[...] + dot(attended_ref[...], w_ref[...], 0, 1)
    inv = lax.rsqrt(jnp.sum(middle * middle, axis=1, keepdims=True) / model + EPSILON)
    unit = middle * inv
    middle_ref[...] = middle
    unit_ref[...] = unit
    inv_ref[...] = inv
    mixed_ref[...] = (unit * gain_ref[...]).astype(BF)


def to_middle(stats, got, acc, far, w_out, tokens, gain, kv_heads, model):
    width, rows = far.shape
    wide = tokens.shape[1]
    shape = stats[0].shape
    return pl.pallas_call(
        functools.partial(middle_kernel, kv_heads, model),
        in_specs=[VMEM] * 9,
        out_specs=[VMEM] * 7,
        out_shape=[
            like((width, rows), BF),
            like(shape, F32),
            like(shape, F32),
            like((rows, wide), F32),
            like((rows, wide), F32),
            like((rows, 1), F32),
            like((rows, wide), BF),
        ],
        cost_estimate=COST,
        compiler_params=params(16),
        name="to_middle",
    )(*stats, *got, acc, far, w_out, tokens, gain)


def feed_kernel(m0, m1, b0, b1, gate_ref, up_ref, down_ref, *refs):
    hidden_ref, backs_ref, p0, p1, x0, x1 = refs
    rows, unit = m0.shape[0], gate_ref.shape[1]
    for t, (mixed_ref, back_ref, part_ref, mix_ref) in enumerate(((m0, b0, p0, x0), (m1, b1, p1, x1))):
        at = slice(t * rows, (t + 1) * rows)
        gate = dot(mixed_ref[...], gate_ref[...], 1, 0)
        lift = dot(mixed_ref[...], up_ref[...], 1, 0)
        back = dot(back_ref[...], down_ref[...], 1, 0)
        sig = 1.0 / (1.0 + jnp.exp(-gate))
        silu = gate * sig
        hidden = (silu * lift).astype(BF)
        back_gate = (back * lift * sig * (1.0 + gate * (1.0 - sig))).astype(BF)
        back_lift = (back * silu).astype(BF)
        hidden_ref[at, :] = hidden
        backs_ref[at, :unit] = back_gate
        backs_ref[at, unit:] = back_lift
        mix = dot(back_gate, gate_ref[...], 1, 1) + dot(back_lift, up_ref[...], 1, 1)
        mix_ref[...] = mix.astype(mix_ref.dtype)
        part_ref[...] = dot(hidden, down_ref[...], 1, 1).astype(part_ref.dtype)


def feed_forward(core, mixed, back, large, unit, name):
    rows, wide = mixed[0].shape
    whole = pl.BlockSpec((rows, wide), lambda i, core: (0, 0))
    w_specs = [
        pl.BlockSpec((wide, unit), lambda i, core, k=k: (0, 2 * k + core[0])) for k in range(3)
    ]
    kinds = (F32, BF, F32, BF)
    return pl.pallas_call(
        lambda core, *refs: feed_kernel(*refs),
        grid_spec=pltpu.PrefetchScalarGridSpec(
            num_scalar_prefetch=1,
            grid=(1,),
            in_specs=[whole] * 4 + w_specs,
            out_specs=[
                pl.BlockSpec((2 * rows, unit), lambda i, core: (0, 0)),
                pl.BlockSpec((2 * rows, 2 * unit), lambda i, core: (0, 0)),
                *[whole] * 4,
            ],
        ),
        out_shape=[
            like((2 * rows, unit), BF),
            like((2 * rows, 2 * unit), BF),
            *[like((rows, wide), kind) for kind in kinds],
        ],
        cost_estimate=COST,
        compiler_params=params(40),
        name=name,
    )(core, *mixed, *back, large, large, large)


def grads_kernel(y_ref, m0, m1, m2, m3, b0, b1, b2, b3, u0, u1, h0, h1, keep_ref, send_ref):
    rows, unit, half = m0.shape[0], h0.shape[1], keep_ref.shape[1]
    first = y_ref[0] == 0

    def put(at, parts, u0, u1):
        acc = dot(parts[0][...], u0[:rows, :], 0, 0) + dot(parts[1][...], u0[rows:, :], 0, 0)
        acc = acc + dot(parts[2][...], u1[:rows, :], 0, 0) + dot(parts[3][...], u1[rows:, :], 0, 0)
        for z in range(keep_ref.shape[0]):
            low, high = acc[2 * z * half : (2 * z + 1) * half], acc[(2 * z + 1) * half : 2 * (z + 1) * half]
            keep_ref[z, :, at] = jnp.where(first, low, high).astype(BF)
            send_ref[z, :, at] = jnp.where(first, high, low).astype(BF)

    put(slice(0, 2 * unit), (m0, m1, m2, m3), u0, u1)
    put(slice(2 * unit, 3 * unit), (b0, b1, b2, b3), h0, h1)


def feed_grads(y, mixed, back, backs, hidden, line):
    rows, wide = mixed[0].shape
    steps = min(line, wide // 128)
    block, unit = wide // steps, hidden[0].shape[1]
    return pl.pallas_call(
        grads_kernel,
        grid=(steps,),
        in_specs=[SMEM]
        + [pl.BlockSpec((rows, block), lambda z: (0, z))] * 8
        + [pl.BlockSpec((2 * rows, 2 * unit), lambda z: (0, 0))] * 2
        + [pl.BlockSpec((2 * rows, unit), lambda z: (0, 0))] * 2,
        out_specs=[pl.BlockSpec((line // steps, wide // line // 2, 3 * unit), lambda z: (z, 0, 0))] * 2,
        out_shape=[like((line, wide // line // 2, 3 * unit), BF)] * 2,
        cost_estimate=COST,
        compiler_params=params(24),
        name="feed_grads",
    )(y, *mixed, *back, *backs, *hidden)


def after_feed_kernel(
    model, kv_heads, mix_ref, core_ref, far_ref, unit_ref, inv_ref, gain_ref, back_ref, w_ref,
    order_ref, attended_ref, middle_ref, do_ref, dot_ref, gains_ref, split_ref,
):
    unit = unit_ref[...]
    mixed = mix_ref[...] + core_ref[...].astype(F32) + far_ref[...].astype(F32)
    gains_ref[...] = jnp.sum(mixed * unit, axis=0, keepdims=True)
    scaled = mixed * gain_ref[...]
    mean = jnp.sum(scaled * unit, axis=1, keepdims=True) / model
    middle = back_ref[...] + inv_ref[...] * (scaled - unit * mean)
    middle_ref[...] = middle
    low = middle.astype(BF)
    do_ref[...] = dot(w_ref[...], low, 0, 1).astype(BF)
    group = do_ref.shape[0] // HEAD // kv_heads
    dot_ref[...] = jnp.zeros_like(dot_ref)
    for h in range(kv_heads * group):
        at = slice(h * HEAD, (h + 1) * HEAD)
        product = do_ref[at, :].astype(F32) * attended_ref[at, :].astype(F32)
        dot_ref[h // group, h % group : h % group + 1, :] = jnp.sum(product, axis=0, keepdims=True)
    split_ref[...] = dot(order_ref[...], low, 1, 1).astype(BF)


def after_feed(mix, core, far, unit, inv, gain, back, w_out, order, attended, kv_heads, model):
    rows, wide = unit.shape
    width = attended.shape[0]

    shapes = [
        like((rows, wide), F32),
        like((width, rows), BF),
        like((kv_heads, 8, rows), F32),
        like((1, wide), F32),
        like((wide, rows), BF),
    ]
    return pl.pallas_call(
        functools.partial(after_feed_kernel, model, kv_heads),
        in_specs=[VMEM] * 10,
        out_specs=[VMEM] * 5,
        out_shape=shapes,
        cost_estimate=COST,
        compiler_params=params(),
        name="after_feed",
    )(mix, core, far, unit, inv, gain, back, w_out, order, attended)


def backs_kernel(q_part, k_part, dq_ref, far_ref, dkv_ref, chain_ref, cos_ref, sin_ref, out_ref):
    sides = out_ref.shape[0]
    cos, sin = cos_ref[...], sin_ref[...]

    def put(part, base, index, value):
        x, at = divmod(index * HALF_HEAD, part)
        out_ref[x, base + at : base + at + HALF_HEAD, :] = value.astype(BF)

    def turn(part, base, h, value):
        low, high = value[:HALF_HEAD], value[HALF_HEAD:]
        put(part, base, 2 * h, low * cos + high * sin)
        put(part, base, 2 * h + 1, high * cos - low * sin)

    for h in range(sides * q_part // HEAD):
        at = slice(h * HEAD, (h + 1) * HEAD)
        turn(q_part, 0, h, dq_ref[at, :] + far_ref[at, :].astype(F32))
    for h in range(sides * k_part // HEAD):
        at = slice(h * HEAD, (h + 1) * HEAD)
        turn(k_part, q_part, h, dkv_ref[0, at, :] + chain_ref[0, at, :].astype(F32))
    for x in range(sides):
        at = slice(x * k_part, (x + 1) * k_part)
        value = dkv_ref[1, at, :] + chain_ref[1, at, :].astype(F32)
        out_ref[x, q_part + k_part :, :] = value.astype(BF)


def finish_backs(dq, far, dkv, chain, cos, sin, sides, q_part, k_part):
    return pl.pallas_call(
        functools.partial(backs_kernel, q_part, k_part),
        in_specs=[VMEM] * 6,
        out_specs=VMEM,
        out_shape=like((sides, q_part + 2 * k_part, far.shape[1]), BF),
        cost_estimate=COST,
        compiler_params=params(12),
        name="finish_backs",
    )(dq, far, dkv, chain, cos, sin)


def terms_kernel(
    slot, shard, place, n0, n1, p0, p1, d0, d1, o0, o1, l_ref, r_ref, gain_ref, gain2_ref,
    left_keep, left_send, right_keep, right_send, full_ref,
):
    sides, qkv, _ = d0.shape
    half = n0.shape[0]
    ys, cut = l_ref.shape[1], l_ref.shape[3]
    block = half // ys
    spare = lax.broadcasted_iota(jnp.int32, (half, 1), 0) % slot == shard
    first = jnp.zeros((half, 128), F32)
    for x in range(sides - 1, -1, -1):
        acc = dot(n0[...], d0[x], 1, 1) + dot(n1[...], d1[x], 1, 1)
        weights = jnp.concatenate(
            [jnp.concatenate([l_ref[x, y], r_ref[y, x]], axis=1) for y in range(ys)], axis=0
        )
        product = acc * weights[:, :qkv].astype(F32)
        for k in range(0, qkv // 128):
            first = first + product[:, k * 128 : (k + 1) * 128]
        rest = qkv % 128
        if rest:
            tail = product[:, qkv - rest :]
            first = first + jnp.concatenate([tail, jnp.zeros((half, 128 - rest), F32)], axis=1)
        width = left_keep.shape[2] - qkv
        at = slice(x * width, (x + 1) * width)
        other = dot(p0[...], o0[at, :], 1, 1) + dot(p1[...], o1[at, :], 1, 1)
        both = jnp.concatenate([acc, other], axis=1)
        if x == 0:
            gain = jnp.sum(first.T, axis=0, keepdims=True)
            scale = gain_ref[...]
            gain = jnp.where(scale > 0, gain / jnp.maximum(scale, 0.25), 0.0)
        else:
            gain = gain2_ref[...]
        reach = gain.shape[1]
        full_ref[:, :reach] = jnp.where(spare, gain, both[:, :reach]).astype(BF)
        full_ref[:, reach:] = both[:, reach:].astype(BF)
        part = block // 2
        for y in range(ys):
            top = slice(y * block, y * block + part)
            pl.when(place[2] == x)(lambda: left_keep.__setitem__(y, full_ref[top, :]))
            pl.when(place[2] != x)(lambda: left_send.__setitem__(y, full_ref[top, :]))
            low = slice(y * block + part, (y + 1) * block)
            pl.when(place[1] == y)(lambda: right_keep.__setitem__(x, full_ref[low, :]))
            pl.when(place[1] != y)(lambda: right_send.__setitem__(x, full_ref[low, :]))


def small_terms(place, normed, proj, backs, attended, mine, gain, gain2, slot, shard):
    sides, qkv, _ = backs[0].shape
    columns = qkv + attended[0].shape[0] // sides
    half = normed[0].shape[0]
    arrays = (*normed, *proj, *backs, *attended, *mine, gain, gain2)
    outs = [like((2, half // 4, columns), BF)] * 4
    return pl.pallas_call(
        functools.partial(terms_kernel, slot, shard),
        grid=(1,),
        in_specs=[SMEM] + [full(a) for a in arrays],
        out_specs=[full(o) for o in outs],
        out_shape=outs,
        scratch_shapes=[pltpu.VMEM((half, columns), BF)],
        cost_estimate=COST,
        compiler_params=params(24),
        name="small_terms",
    )(place, *arrays)


def second_kernel(which, place, keep_ref, far_ref, out_ref, send_ref):
    total = (keep_ref[...].astype(F32) + far_ref[...].astype(F32)).astype(BF)
    first = place[which] == 0
    out_ref[...] = jnp.where(first, total[0], total[1])
    send_ref[...] = jnp.where(first, total[1], total[0])


def second_fold(place, which, keep, far):
    return pl.pallas_call(
        functools.partial(second_kernel, which),
        in_specs=[SMEM, VMEM, VMEM],
        out_specs=[VMEM] * 2,
        out_shape=[like(keep.shape[1:], BF)] * 2,
        cost_estimate=COST,
        compiler_params=params(12),
        name="second_fold",
    )(place, keep, far)


def join_kernel(a0, a1, b0, b1, out_ref):
    out_ref[0] = (a0[...].astype(F32) + a1[...].astype(F32)).astype(BF)
    out_ref[1] = (b0[...].astype(F32) + b1[...].astype(F32)).astype(BF)


def join(left, right):
    return pl.pallas_call(
        join_kernel,
        in_specs=[VMEM] * 4,
        out_specs=VMEM,
        out_shape=like((2, *left[0].shape), BF),
        cost_estimate=COST,
        compiler_params=params(12),
        name="join",
    )(*left, *right)


def small_sums_kernel(shard, slot, q_part, k_part, at_ref, in_ref, q_ref, k_ref, v_ref, o_ref, gain_ref):
    total = in_ref[0].astype(F32)
    for i in range(1, in_ref.shape[0]):
        total = total + in_ref[i].astype(F32)
    q_ref[...] = total[:shard, :q_part]
    k_ref[...] = total[:shard, q_part : q_part + k_part]
    v_ref[...] = total[:shard, q_part + k_part : q_part + 2 * k_part]
    o_ref[...] = total[:shard, q_part + 2 * k_part :]
    gain = jnp.zeros((1, shard), F32)
    for block in range(total.shape[1] // slot):
        part = total[shard : shard + 1, block * slot : block * slot + shard]
        gain = jnp.where(at_ref[0] == block, part, gain)
    gain_ref[...] = gain


def small_sums(at, parts, shard, q_part, k_part):
    slot = parts.shape[1]
    return pl.pallas_call(
        functools.partial(small_sums_kernel, shard, slot, q_part, k_part),
        in_specs=[SMEM, VMEM],
        out_specs=[VMEM] * 5,
        out_shape=[like((shard, n), F32) for n in (q_part, k_part, k_part, q_part)]
        + [like((1, shard), F32)],
        cost_estimate=COST,
        compiler_params=params(12),
        name="small_sums",
    )(at, parts)


def add_wide(a, b):
    return pl.pallas_call(
        add_kernel,
        grid=(1,),
        in_specs=[full(a), full(b)],
        out_specs=full(a),
        out_shape=pltpu.HBM(a.shape, BF),
        cost_estimate=COST,
        compiler_params=params(24),
        name="add_wide",
    )(a, b)


def sum_blocks_kernel(place, *refs):
    *parts, keep_ref, send_ref = refs
    half = keep_ref.shape[0]
    total = parts[0][...].astype(F32)
    for part in parts[1:]:
        total = total + part[...].astype(F32)
    total = total.astype(BF)
    first = place[3] == 0
    keep_ref[...] = jnp.where(first, total[:half], total[half:])
    send_ref[...] = jnp.where(first, total[half:], total[:half])


def sum_blocks(place, parts):
    outs = [like((parts[0].shape[0] // 2, parts[0].shape[1]), BF)] * 2
    return pl.pallas_call(
        sum_blocks_kernel,
        grid=(1,),
        in_specs=[SMEM] + [full(p) for p in parts],
        out_specs=[full(o) for o in outs],
        out_shape=outs,
        cost_estimate=COST,
        compiler_params=params(16),
        name="sum_blocks",
    )(place, *parts)


def large_sums_kernel(shard, place, own_ref, far_ref, *refs):
    unit = refs[0].shape[1] // 2
    first = place[3] == 0
    own, far = own_ref[:shard, :].astype(F32), far_ref[:shard, :].astype(F32)
    low, high = jnp.where(first, own, far), jnp.where(first, far, own)
    for k, ref in enumerate(refs):
        ref[:, :unit] = low[:, k * unit : (k + 1) * unit]
        ref[:, unit:] = high[:, k * unit : (k + 1) * unit]


def large_sums(place, own, far, shard):
    unit = own.shape[1] // 3
    return pl.pallas_call(
        functools.partial(large_sums_kernel, shard),
        in_specs=[SMEM, VMEM, VMEM],
        out_specs=[VMEM] * 3,
        out_shape=[like((shard, 2 * unit), F32)] * 3,
        cost_estimate=COST,
        compiler_params=params(16),
        name="large_sums",
    )(place, own, far)


def exact_dot(one_hot, wide, ca, cb):
    high = wide.astype(BF)
    low = (wide - high.astype(F32)).astype(BF)
    return dot(one_hot, high, ca, cb) + dot(one_hot, low, ca, cb)


def input_kernel(
    model, d_ref, lm, rm, lt, rt, unit_ref, inv_ref, gain_ref, middle_ref, spread_ref, split_ref,
    out_ref, m_ref,
):
    sides, ys, block, cut = lm.shape
    qkv = d_ref.shape[1]
    half = ys * block
    for side, (l, r) in enumerate(((lm, rm), (lt, rt))):
        for y in range(ys):
            at = slice(side * half + y * block, side * half + (y + 1) * block)
            total = None
            for x in range(sides):
                a = dot(l[x, y], d_ref[x, :cut, :], 1, 0)
                a = a + dot(r[y, x][:, : qkv - cut], d_ref[x, cut:, :], 1, 0)
                total = a if total is None else total + a
            m_ref[at, :] = total * gain_ref[at, :]
    unit = unit_ref[...]
    scaled = m_ref[...]
    mean = jnp.sum(scaled * unit, axis=0, keepdims=True) / model
    back = inv_ref[...] * (scaled - unit * mean)
    grad = exact_dot(spread_ref[...], middle_ref[...], 1, 1) + exact_dot(split_ref[...], back, 1, 0)
    part = grad.shape[1] // 2
    out_ref[0] = grad[:, :part]
    out_ref[1] = grad[:, part:]


def input_gradient(backs, mine, theirs, unit, inv, gain, middle, spread, split, model):
    out = like((2, model, middle.shape[0] // 2), F32)
    arrays = (backs, *mine, *theirs, unit, inv, gain, middle, spread, split)
    return pl.pallas_call(
        functools.partial(input_kernel, model),
        grid=(1,),
        in_specs=[full(a) for a in arrays],
        out_specs=full(out),
        out_shape=out,
        scratch_shapes=[pltpu.VMEM(unit.shape, F32)],
        cost_estimate=COST,
        compiler_params=params(40),
        name="input_gradient",
    )(*arrays)


def output_kernel(middle_ref, own_ref, core_ref, far_ref, spread_ref, out_ref):
    result = middle_ref[...] + own_ref[...] + core_ref[...].astype(F32) + far_ref[...].astype(F32)
    out = dot(spread_ref[...], result.astype(BF), 1, 1).astype(BF)
    part = out.shape[1] // 2
    out_ref[0] = out[:, :part]
    out_ref[1] = out[:, part:]


def layer_output(middle, own, core, far, spread):
    return pl.pallas_call(
        output_kernel,
        in_specs=[VMEM] * 5,
        out_specs=VMEM,
        out_shape=like((2, spread.shape[0], middle.shape[0] // 2), BF),
        cost_estimate=COST,
        compiler_params=params(),
        name="layer_output",
    )(middle, own, core, far, spread)


def padded(count):
    return -(-count // 8) * 8


def pick(pair, index):
    return jnp.where(index == 0, pair[0], pair[1])


def ordered(mine, theirs, index, axis):
    return jnp.concatenate([pick((mine, theirs), index), pick((theirs, mine), index)], axis=axis)


def swap(array, name):
    return lax.ppermute(array, name, SWAP)


def after(value, *earlier):
    return lax.optimization_barrier((value, *earlier))[0]


def spread_matrix(model, shard, slot, ctx):
    row = lax.broadcasted_iota(jnp.int32, (model, slot * ctx), 0)
    col = lax.broadcasted_iota(jnp.int32, (model, slot * ctx), 1)
    return (col == row // shard * slot + row % shard).astype(BF)


def core_order(slot, line, c):
    wide = slot * line * 4
    row = lax.broadcasted_iota(jnp.int32, (wide, wide), 1)
    col = lax.broadcasted_iota(jnp.int32, (wide, wide), 0)
    block, place = row // slot, row % slot
    core, y, z = block % 2, block // 2 % 2, block // 4
    other = (core != c).astype(jnp.int32)
    return (col == ((other * 2 + y) * line + z) * slot + place).astype(BF)


def gather_small(rows_here, cut, meanwhile):
    line = lax.axis_size("zh") * lax.axis_size("zl")
    d, y = lax.axis_index("dp"), lax.axis_index("y")
    z_all = lax.all_to_all(
        jnp.broadcast_to(rows_here[None], (line, *rows_here.shape)),
        ("zh", "zl"),
        split_axis=0,
        concat_axis=0,
    )
    z_all = after(z_all, *meanwhile).reshape(1, -1, rows_here.shape[1])
    left, right = z_all[..., :cut], z_all[..., cut:]
    left, right = ordered(left, swap(left, "y"), y, 0), ordered(right, swap(right, "dp"), d, 0)
    left, right = left[None], right[None]
    return ordered(left, swap(left, "dp"), d, 0), ordered(right, swap(right, "y"), y, 0)


def body(
    inputs,
    query_weight,
    key_weight,
    value_matrix,
    out_weight,
    gate_weight,
    up_weight,
    down_weight,
    norm_gains,
    cotangent,
):
    seqs, part_rows, model = inputs.shape
    dps, high, low = (lax.axis_size(a) for a in ("dp", "zh", "zl"))
    line = high * low
    ctx = line * 4
    y, c, d = (lax.axis_index(a) for a in ("y", "c", "dp"))
    z = lax.axis_index("zh") * low + lax.axis_index("zl")
    shard = model // ctx
    slot = padded(shard + 1)
    wide = slot * ctx
    half = wide // 2
    rows = 2 * part_rows
    up_line = [(i, i + 1) for i in range(line - 1)]
    down_line = [(i + 1, i) for i in range(line - 1)]
    z_axes = ("zh", "zl")
    everywhere = ("zh", "zl", "y", "c")
    place = jnp.stack([z, y, d, c]).astype(jnp.int32)

    q_part, k_part = query_weight.shape[1], key_weight.shape[1]
    qkv_part = q_part + 2 * k_part
    half_ff = gate_weight.shape[1]
    unit = half_ff // 2
    kv_heads = k_part * dps // HEAD

    small = jnp.concatenate([query_weight, key_weight, value_matrix], axis=1)
    small_columns = -(-qkv_part // 128) * 128
    small = jnp.concatenate(
        [
            jnp.pad(small, ((0, 0), (0, small_columns - qkv_part))),
            jnp.pad(norm_gains, ((0, slot - shard - 1), (0, small_columns - shard))),
        ],
        axis=0,
    )
    out_shard = after(out_weight.T, small)
    large = jnp.concatenate(
        [gate_weight, up_weight, down_weight.T, ordered(out_shard, swap(out_shard, "dp"), d, 1)],
        axis=1,
    )
    large = jnp.pad(large, ((0, slot - shard), (0, 0)))
    large = lax.all_gather(large, everywhere, axis=0, tiled=True)
    w_out = large[:, 3 * half_ff :]

    both = jnp.stack([inputs, cotangent], axis=1)
    mine, theirs = pick((both[0], both[1]), c), pick((both[1], both[0]), c)
    both = ordered(mine, swap(theirs, "c"), c, 1)
    spread = spread_matrix(model, shard, slot, ctx)
    by_core = core_order(slot, line, c)
    spread, by_core = after(spread, small), after(by_core, small)
    spread_split = dot(spread, by_core, 1, 1).astype(BF)
    tokens = dot(both[0], spread, 1, 0)
    tokens_t = dot(spread_split, both[0], 0, 1)
    back_out = dot(both[1], spread, 1, 0)
    back_low = back_out.astype(BF)
    inv_first = lax.rsqrt(jnp.sum(tokens_t * tokens_t, axis=0, keepdims=True) / model + EPSILON)
    unit_first = tokens_t * inv_first
    positions = (2 * z + y) * rows + jnp.arange(rows, dtype=jnp.int32)
    cos, sin = rope_tables(positions, HALF_HEAD)

    w_mine = gather_small(small, small_columns // 256 * 128, (unit_first, tokens, back_low))
    w_theirs = tuple(swap(w, "c") for w in w_mine)

    def gains_of(w):
        part = w[0].reshape(dps, 2, line, slot, -1)[:, :, :, shard, :shard]
        return jnp.pad(part, ((0, 0), (0, 0), (0, 0), (0, slot - shard))).astype(F32)

    gains_mine, gains_theirs = gains_of(w_mine), gains_of(w_theirs)
    gain_second = ordered(gains_mine[1, :, :, None], gains_theirs[1, :, :, None], c, 2)
    gain_second = gain_second.transpose(1, 0, 2, 3).reshape(1, wide)
    gain_first = jnp.concatenate([gains_mine[0], gains_theirs[0]], axis=0).reshape(wide, 1)
    gains_mine = gains_mine[0].reshape(1, half)
    gain_first, gain_second, gains_mine = lax.optimization_barrier(
        (gain_first, gain_second, gains_mine)
    )

    normed = (unit_first * gain_first).astype(BF)
    q, kv = project(normed, cos, sin, w_mine, w_theirs, q_part, k_part)

    kvs = [kv]
    back_core, back_far = swap(after(back_low, kv), "c"), swap(after(back_low, kv), "dp")
    q_both = (q, swap(q, "y"))
    state = ()
    for step in range(line - 1):
        here, far_q = kvs[-1], q_both[1]
        if step > 1:
            here, state = lax.optimization_barrier((here, state))
        kvs.append(lax.ppermute(here, z_axes, up_line))
        if step > 0:
            far_q = after(far_q, here)
            state = attend_forward(place, step - 1, False, q, far_q, kvs[step - 1], state, kv_heads)
    far_q = after(q_both[1], kvs[-2])
    state = attend_forward(place, line - 2, False, q, far_q, kvs[line - 2], state, kv_heads)
    stats, acc, far_stats, far_acc = attend_forward(
        place, line - 1, True, *q_both, kvs[line - 1], state, kv_heads
    )
    got = lax.ppermute(jnp.stack([far_stats, stats]), "y", SWAP)
    attended, lse, far_lse, middle, unit_second, inv_second, mixed_own = to_middle(
        (stats, far_stats), (got[0], got[1]), acc, swap(far_acc, "y"), w_out, tokens, gain_second,
        kv_heads, model,
    )

    mixed_core, mixed_far = swap(mixed_own, "c"), swap(mixed_own, "dp")
    core = c.astype(jnp.int32)[None]
    hidden_near, backs_near, part_own, part_core, mix_own, mix_core = feed_forward(
        core, (mixed_own, mixed_core), (back_low, back_core), large, unit, "feed_near"
    )
    mixed_far = after(mixed_far, mix_own)
    back_far = after(back_far, stats)
    mixed_far, back_far = (mixed_far, swap(mixed_far, "c")), (back_far, swap(back_far, "c"))
    hidden_far, backs_far, part_far, part_cross, mix_far, mix_cross = feed_forward(
        core, mixed_far, back_far, large, unit, "feed_far"
    )
    mix_core = swap(mix_core, "c")
    mix_far = add_low(mix_far, swap(mix_cross, "c"))
    hidden_near, mix_far_sum = after(hidden_near, mix_far), mix_far
    mix_far = swap(mix_far_sum, "dp")

    mixed_all, back_all = (mixed_own, mixed_core, *mixed_far), (back_low, back_core, *back_far)
    grads_keep, grads_send = feed_grads(
        y.astype(jnp.int32)[None], mixed_all, back_all, (backs_near, backs_far), (hidden_near, hidden_far), line
    )
    normed_pair = (normed[:half], swap(normed[half:], "c"))
    attended_pair = (attended, swap(attended, "c"))
    part_far = add_low(part_far, swap(part_cross, "c"))
    mix_far = after(mix_far, grads_keep, normed_pair[1], attended_pair[1], part_far)

    back_middle, do, row_dot, gain_terms, proj = after_feed(
        mix_own, mix_core, mix_far, unit_second, inv_second, gain_second, back_out, w_out, by_core,
        attended, kv_heads, model,
    )
    proj_pair = (proj[:half], swap(proj[half:], "c"))
    gain_terms = gain_terms + swap(gain_terms, "c")
    do_far, dot_far = swap(do, "y"), swap(row_dot, "y")
    do_far = after(do_far, proj_pair[1], gain_terms)
    do_both, dot_both, lse_both = (do, do_far), (row_dot, dot_far), (lse, far_lse)

    grads_far = swap(after(grads_send, do_far, dot_far), "y")
    part_far = swap(after(part_far, do_far), "dp")
    part_core = swap(part_core, "c")
    chain, dq = None, ()
    for step in range(line - 1, 0, -1):
        keys_here = kvs[step]
        if step == 1:
            keys_here = after(keys_here, part_far, part_core)
        if step < line - 2:
            keys_here, chain = lax.optimization_barrier((keys_here, chain))
        *dq, total = attend_backward(
            place, step, q_both, do_both, lse_both, dot_both, keys_here, dq, kv_heads
        )
        if chain is not None:
            total = add_low(total, lax.ppermute(chain, z_axes, down_line))
        chain = total
    dq, dq_send, dkv = attend_backward(
        place, 0, q_both, do_both, lse_both, dot_both, after(kvs[0], chain), dq, kv_heads
    )
    dq_far = swap(dq_send, "y")
    chain = lax.ppermute(after(chain, dq_send), z_axes, down_line)
    grads = add_wide(grads_keep, after(grads_far, dq)).reshape(line * 2 * slot, -1)
    grads = lax.psum_scatter(grads, z_axes, scatter_dimension=0, tiled=True)
    backs = finish_backs(dq, dq_far, dkv, chain, cos, sin, dps, q_part, k_part)

    left_keep, left_send, right_keep, right_send = small_terms(
        place, normed_pair, proj_pair, (backs, swap(backs, "c")), attended_pair, w_mine, gains_mine,
        gain_terms, slot, shard,
    )
    left_far, right_far = swap(left_send, "dp"), swap(right_send, "y")
    backs, part_far = after(backs, left_keep), after(part_far, left_keep)
    input_grad = input_gradient(
        backs, w_mine, w_theirs, unit_first, inv_first, gain_first, back_middle, spread,
        spread_split, model,
    )
    layer_out = layer_output(middle, part_own, part_core, part_far, spread)
    left_far = after(left_far, input_grad, layer_out)
    left_keep, left_send = second_fold(place, 1, left_keep, left_far)
    right_keep, right_send = second_fold(place, 2, right_keep, right_far)
    terms = join((left_keep, swap(left_send, "y")), (right_keep, swap(right_send, "dp")))
    grads_keep, grads_send = sum_blocks(place, (grads,))
    gate_grad, up_grad, down_grad = large_sums(place, grads_keep, swap(grads_send, "c"), shard)
    terms = lax.all_to_all(
        terms.reshape(line, slot, -1), z_axes, split_axis=0, concat_axis=0
    )
    place_of_gains = jnp.where(d == 0, y * line + z, (z * 2 + y) * 2 + c).astype(jnp.int32)[None]
    query_grad, key_grad, value_grad, out_grad, gains_grad = small_sums(
        place_of_gains, terms, shard, q_part, k_part
    )

    def give_back(array):
        keep, send = pick((array[0], array[1]), c), pick((array[1], array[0]), c)
        return ordered(keep[None], swap(send, "c")[None], c, 0)

    return (
        give_back(layer_out).transpose(0, 2, 1),
        give_back(input_grad).transpose(0, 2, 1),
        query_grad,
        key_grad,
        value_grad,
        out_grad.T,
        gate_grad,
        up_grad,
        down_grad.T,
        gains_grad,
    )


def solution(mesh):
    devices = mesh.devices
    dps, ctx = devices.shape
    inner = Mesh(devices.reshape(dps, 2, ctx // 8, 2, 2), ("dp", "zh", "zl", "y", "c"))
    along = ("zh", "zl", "y", "c")
    rows, by_row, by_col = P("dp", along, None), P(along, "dp"), P("dp", along)
    return jax.shard_map(
        body,
        mesh=inner,
        in_specs=(rows, by_row, by_row, by_row, by_col, by_row, by_row, by_col, by_col, rows),
        out_specs=(rows, rows, by_row, by_row, by_row, by_col, by_row, by_row, by_col, by_col),
        check_vma=False,
    )
```

```python
import functools
import math

import jax
import jax.numpy as jnp
from jax import lax
from jax.experimental import pallas as pl
from jax.experimental.pallas import tpu as pltpu
from jax.sharding import Mesh, PartitionSpec as P

HEAD = 64
HALF_HEAD = HEAD // 2
EPSILON = 1e-05
MASKED = -1e30
FLOOR = -1e20
LOG2E = 1.4426950408889634
SCALE = 0.125 * LOG2E
BF = jnp.bfloat16
F32 = jnp.float32
SWAP = [(0, 1), (1, 0)]
COST = pl.CostEstimate(flops=1000, bytes_accessed=1000, transcendentals=0)
VMEM = pl.BlockSpec(memory_space=pltpu.VMEM)
SMEM = pl.BlockSpec(memory_space=pltpu.SMEM)


def params(mib=32):
    return pltpu.CompilerParams(vmem_limit_bytes=mib * 2**20)


def dot(a, b, ca, cb):
    return lax.dot_general(a, b, (((ca,), (cb,)), ((), ())), preferred_element_type=F32)


def full(array):
    return pl.BlockSpec(array.shape, lambda i: (0,) * len(array.shape))


def like(shape, kind):
    return jax.ShapeDtypeStruct(shape, kind)


def rope_tables(positions, half):
    spectrum = jnp.exp(jnp.arange(half, dtype=F32) * (-math.log(100000.0) / half))
    angles = spectrum[:, None] * positions.astype(F32)[None, :]
    return jnp.cos(angles), jnp.sin(angles)


def project_kernel(
    q_part, k_part, cut, normed_ref, cos_ref, sin_ref, lm, rm, lt, rt, q_ref, kv_ref, raw_ref
):
    sides, ys, block, _ = lm.shape
    half = ys * block
    for x in range(sides):
        left = right = None
        for side, (l, r) in enumerate(((lm, rm), (lt, rt))):
            for y in range(ys):
                at = side * half + y * block
                rows = normed_ref[at : at + block, :]
                a, b = dot(l[x, y], rows, 0, 0), dot(r[y, x], rows, 0, 0)
                left = a if left is None else left + a
                right = b if right is None else right + b
        raw_ref[x, :cut, :] = left
        raw_ref[x, cut:, :] = right
    cos, sin = cos_ref[...], sin_ref[...]

    def half_rows(part, base, index):
        x, at = divmod(index * HALF_HEAD, part)
        return raw_ref[x, base + at : base + at + HALF_HEAD, :]

    def turn(part, base, out_ref, heads):
        for h in range(heads):
            low, high = half_rows(part, base, 2 * h), half_rows(part, base, 2 * h + 1)
            out_ref[h * HEAD : h * HEAD + HALF_HEAD, :] = (low * cos - high * sin).astype(BF)
            out_ref[h * HEAD + HALF_HEAD : (h + 1) * HEAD, :] = (high * cos + low * sin).astype(BF)

    turn(q_part, 0, q_ref, sides * q_part // HEAD)
    turn(k_part, q_part, kv_ref, sides * k_part // HEAD)
    for x in range(sides):
        base = sides * k_part + x * k_part
        kv_ref[base : base + k_part, :] = raw_ref[
            x, q_part + k_part : q_part + 2 * k_part, :
        ].astype(BF)


def project(normed, cos, sin, mine, theirs, q_part, k_part):
    sides, _, _, cut = mine[0].shape
    rows = normed.shape[1]
    return pl.pallas_call(
        functools.partial(project_kernel, q_part, k_part, cut),
        in_specs=[VMEM] * 7,
        out_specs=[VMEM] * 2,
        out_shape=[like((sides * q_part, rows), BF), like((2 * sides * k_part, rows), BF)],
        scratch_shapes=[pltpu.VMEM((sides, cut + mine[1].shape[3], rows), F32)],
        cost_estimate=COST,
        compiler_params=params(),
        name="project",
    )(normed, cos, sin, *mine, *theirs)


def abreast(group, own, far, at):
    parts = []
    for h in range(group):
        parts.append(own[at(h)])
        if far is not None:
            parts.append(far[at(h)])
    return jnp.concatenate(parts, axis=1) if len(parts) > 1 else parts[0]


def head_rows(h):
    return (slice(h * HEAD, (h + 1) * HEAD), slice(None))


def stat_row(h):
    return (0, slice(h, h + 1), slice(None))


def causal(keys, rows, group, both):
    key_pos = lax.broadcasted_iota(jnp.int32, (keys, rows), 0)
    own = lax.broadcasted_iota(jnp.int32, (keys, rows), 1) >= key_pos
    parts = [own, jnp.ones_like(own)] if both else [own]
    return jnp.concatenate(parts * group, axis=1)


def forward_kernel(step, last, group, place, q_ref, far_q_ref, k_ref, v_ref, *refs):
    rows = q_ref.shape[1]
    stat_ref, acc_ref, far_stat_ref, far_acc_ref = refs[-4:]

    def visit(both):
        far = (lambda ref: ref) if both else (lambda ref: None)
        scores = dot(k_ref[...], abreast(group, q_ref, far(far_q_ref), head_rows), 0, 0) * SCALE
        if step == 0:
            scores = jnp.where(causal(scores.shape[0], rows, group, both), scores, MASKED)
        top = jnp.max(scores, axis=0, keepdims=True)
        if step:
            old = abreast(group, refs[0], refs[2], stat_row)
            top = jnp.maximum(top, old)
            shrink = jnp.exp2(old - top)
        probs = jnp.exp2(scores - top)
        total = jnp.sum(probs, axis=0, keepdims=True)
        if step:
            total = total + abreast(group, refs[0], refs[2], lambda h: stat_row(group + h)) * shrink
        acc = dot(v_ref[...], probs.astype(BF), 1, 0)
        sides = ((0, stat_ref, acc_ref), (1, far_stat_ref, far_acc_ref)) if both else ((0, stat_ref, acc_ref),)
        for h in range(group):
            for side, stats, out in sides:
                at = (h * len(sides) + side) * rows
                at = slice(at, at + rows)
                value = acc[:, at]
                if step:
                    value = value + refs[2 * side + 1][head_rows(h)] * shrink[:, at]
                out[head_rows(h)] = value.astype(out.dtype)
                stats[stat_row(h)] = top[:, at]
                stats[stat_row(group + h)] = total[:, at]

    if step == 0:
        pl.when(place[1] == 0)(lambda: visit(True))

        @pl.when(place[1] != 0)
        def _():
            visit(False)
            far_stat_ref[0, :group, :] = jnp.full((group, rows), FLOOR, F32)
            far_stat_ref[0, group : 2 * group, :] = jnp.zeros((group, rows), F32)
            far_acc_ref[...] = jnp.zeros_like(far_acc_ref)
    else:
        pl.when(step <= place[0])(lambda: visit(True))

        @pl.when(step > place[0])
        def _():
            for old, new in zip(refs[:4], refs[-4:]):
                new[...] = old[...].astype(new.dtype)


def attend_forward(place, step, last, q, far_q, kv, state, kv_heads):
    width, rows = q.shape
    group = width // HEAD // kv_heads
    keys = kv.shape[1]
    wide = pl.BlockSpec((group * HEAD, rows), lambda g: (g, 0))
    stat = pl.BlockSpec((1, 8, rows), lambda g: (g, 0, 0))
    first = pl.BlockSpec((HEAD, keys), lambda g: (g, 0))
    second = pl.BlockSpec((HEAD, keys), lambda g: (g + kv_heads, 0))
    stats = like((kv_heads, 8, rows), F32)
    aliases = {5: 0, 6: 1, 7: 2} if last else {5: 0, 6: 1, 7: 2, 8: 3}
    return pl.pallas_call(
        functools.partial(forward_kernel, step, last, group),
        grid=(kv_heads,),
        in_specs=[SMEM, wide, wide, first, second] + ([stat, wide] * 2 if step else []),
        out_specs=[stat, wide] * 2,
        out_shape=[stats, like((width, rows), F32), stats, like((width, rows), BF if last else F32)],
        input_output_aliases=aliases if step else {},
        cost_estimate=COST,
        compiler_params=params(12),
        name=f"attend_forward_{step}",
    )(place, q, far_q, kv, kv, *state)


def backward_kernel(
    step, group, place, q_ref, far_q_ref, do_ref, far_do_ref, lse_ref, far_lse_ref, dot_ref,
    far_dot_ref, k_ref, v_ref, *refs,
):
    dq_ref, far_dq_ref, dkv_ref = refs[-3:]
    more = len(refs) > 3
    rows = q_ref.shape[1]

    def visit(both):
        key, value = k_ref[...], v_ref[...]
        far = (lambda ref: ref) if both else (lambda ref: None)
        q = abreast(group, q_ref, far(far_q_ref), head_rows)
        do = abreast(group, do_ref, far(far_do_ref), head_rows)
        lse = abreast(group, lse_ref, far(far_lse_ref), stat_row)
        total = abreast(group, dot_ref, far(far_dot_ref), stat_row)
        probs = jnp.exp2(dot(key, q, 0, 0) * SCALE - lse)
        if step == 0:
            probs = jnp.where(causal(probs.shape[0], rows, group, both), probs, 0.0)
        back = (probs * (dot(value, do, 0, 0) - total)).astype(BF)
        dkv_ref[0] = (dot(back, q, 1, 1).T * 0.125).astype(dkv_ref.dtype)
        dkv_ref[1] = dot(probs.astype(BF), do, 1, 1).T.astype(dkv_ref.dtype)
        dq = dot(key, back, 1, 0) * 0.125
        sides = (dq_ref, far_dq_ref) if both else (dq_ref,)
        for h in range(group):
            for side, out in enumerate(sides):
                at = (h * len(sides) + side) * rows
                value = dq[:, at : at + rows]
                if more:
                    value = value + refs[side][head_rows(h)]
                out[head_rows(h)] = value.astype(out.dtype)

    if step == 0:
        pl.when(place[1] == 0)(lambda: visit(True))

        @pl.when(place[1] != 0)
        def _():
            visit(False)
            if more:
                far_dq_ref[...] = refs[1][...].astype(far_dq_ref.dtype)
            else:
                far_dq_ref[...] = jnp.zeros_like(far_dq_ref)
    else:
        pl.when(step <= place[0])(lambda: visit(True))

        @pl.when(step > place[0])
        def _():
            for i, ref in enumerate((dq_ref, far_dq_ref)):
                ref[...] = refs[i][...] if more else jnp.zeros_like(ref)
            dkv_ref[...] = jnp.zeros_like(dkv_ref)


def attend_backward(place, step, q, do, lse, row_dot, kv, dq, kv_heads):
    width, rows = q[0].shape
    group = width // HEAD // kv_heads
    keys = kv.shape[1]
    wide = pl.BlockSpec((group * HEAD, rows), lambda g: (g, 0))
    stat = pl.BlockSpec((1, 8, rows), lambda g: (g, 0, 0))
    first = pl.BlockSpec((HEAD, keys), lambda g: (g, 0))
    second = pl.BlockSpec((HEAD, keys), lambda g: (g + kv_heads, 0))
    kind = BF if step else F32
    aliases = ({11: 0, 12: 1} if step else {11: 0}) if dq else {}
    return pl.pallas_call(
        functools.partial(backward_kernel, step, group),
        grid=(kv_heads,),
        in_specs=[SMEM] + [wide] * 4 + [stat] * 4 + [first, second] + [wide] * len(dq),
        out_specs=[wide, wide, pl.BlockSpec((2, HEAD, keys), lambda g: (0, g, 0))],
        out_shape=[
            like((width, rows), F32),
            like((width, rows), F32 if step else BF),
            like((2, kv_heads * HEAD, keys), kind),
        ],
        input_output_aliases=aliases,
        cost_estimate=COST,
        compiler_params=params(12),
        name=f"attend_backward_{step}",
    )(place, *q, *do, *lse, *row_dot, kv, kv, *dq)


def add_kernel(a_ref, b_ref, out_ref):
    out_ref[...] = (a_ref[...].astype(F32) + b_ref[...].astype(F32)).astype(out_ref.dtype)


def add_low(a, b):
    return pl.pallas_call(
        add_kernel,
        in_specs=[VMEM] * 2,
        out_specs=VMEM,
        out_shape=like(a.shape, BF),
        cost_estimate=COST,
        compiler_params=params(12),
        name="add_low",
    )(a, b)


def middle_kernel(
    kv_heads, model, stat_ref, far_stat_ref, got_ref, far_got_ref, acc_ref, far_ref, w_ref,
    tokens_ref, gain_ref, attended_ref, lse_ref, far_lse_ref, middle_ref, unit_ref, inv_ref, mixed_ref,
):
    group = acc_ref.shape[0] // HEAD // kv_heads
    lse_ref[...] = jnp.zeros_like(lse_ref)
    far_lse_ref[...] = jnp.zeros_like(far_lse_ref)
    for g in range(kv_heads):
        for h in range(group):
            at = slice((g * group + h) * HEAD, (g * group + h + 1) * HEAD)
            m, s = slice(h, h + 1), slice(group + h, group + h + 1)
            top = jnp.maximum(far_stat_ref[g, m, :], far_got_ref[g, m, :])
            total = far_stat_ref[g, s, :] * jnp.exp2(far_stat_ref[g, m, :] - top)
            total = total + far_got_ref[g, s, :] * jnp.exp2(far_got_ref[g, m, :] - top)
            far_lse_ref[g, m, :] = top + jnp.log2(total)
            top = jnp.maximum(stat_ref[g, m, :], got_ref[g, m, :])
            near, far = jnp.exp2(stat_ref[g, m, :] - top), jnp.exp2(got_ref[g, m, :] - top)
            total = stat_ref[g, s, :] * near + got_ref[g, s, :] * far
            lse_ref[g, m, :] = top + jnp.log2(total)
            value = acc_ref[at, :] * (near / total) + far_ref[at, :].astype(F32) * (far / total)
            attended_ref[at, :] = value.astype(BF)
    middle = tokens_ref[...] + dot(attended_ref[...], w_ref[...], 0, 1)
    inv = lax.rsqrt(jnp.sum(middle * middle, axis=1, keepdims=True) / model + EPSILON)
    unit = middle * inv
    middle_ref[...] = middle
    unit_ref[...] = unit
    inv_ref[...] = inv
    mixed_ref[...] = (unit * gain_ref[...]).astype(BF)


def to_middle(stats, got, acc, far, w_out, tokens, gain, kv_heads, model):
    width, rows = far.shape
    wide = tokens.shape[1]
    shape = stats[0].shape
    return pl.pallas_call(
        functools.partial(middle_kernel, kv_heads, model),
        in_specs=[VMEM] * 9,
        out_specs=[VMEM] * 7,
        out_shape=[
            like((width, rows), BF),
            like(shape, F32),
            like(shape, F32),
            like((rows, wide), F32),
            like((rows, wide), F32),
            like((rows, 1), F32),
            like((rows, wide), BF),
        ],
        cost_estimate=COST,
        compiler_params=params(16),
        name="to_middle",
    )(*stats, *got, acc, far, w_out, tokens, gain)


def feed_kernel(m0, m1, b0, b1, gate_ref, up_ref, down_ref, *refs):
    hidden_ref, backs_ref, p0, p1, x0, x1 = refs
    rows, unit = m0.shape[0], gate_ref.shape[1]
    for t, (mixed_ref, back_ref, part_ref, mix_ref) in enumerate(((m0, b0, p0, x0), (m1, b1, p1, x1))):
        at = slice(t * rows, (t + 1) * rows)
        gate = dot(mixed_ref[...], gate_ref[...], 1, 0)
        lift = dot(mixed_ref[...], up_ref[...], 1, 0)
        back = dot(back_ref[...], down_ref[...], 1, 0)
        sig = 1.0 / (1.0 + jnp.exp(-gate))
        silu = gate * sig
        hidden = (silu * lift).astype(BF)
        back_gate = (back * lift * sig * (1.0 + gate * (1.0 - sig))).astype(BF)
        back_lift = (back * silu).astype(BF)
        hidden_ref[at, :] = hidden
        backs_ref[at, :unit] = back_gate
        backs_ref[at, unit:] = back_lift
        mix = dot(back_gate, gate_ref[...], 1, 1) + dot(back_lift, up_ref[...], 1, 1)
        mix_ref[...] = mix.astype(mix_ref.dtype)
        part_ref[...] = dot(hidden, down_ref[...], 1, 1).astype(part_ref.dtype)


def feed_forward(core, mixed, back, large, unit, name):
    rows, wide = mixed[0].shape
    whole = pl.BlockSpec((rows, wide), lambda i, core: (0, 0))
    w_specs = [
        pl.BlockSpec((wide, unit), lambda i, core, k=k: (0, 2 * k + core[0])) for k in range(3)
    ]
    kinds = (F32, BF, F32, BF)
    return pl.pallas_call(
        lambda core, *refs: feed_kernel(*refs),
        grid_spec=pltpu.PrefetchScalarGridSpec(
            num_scalar_prefetch=1,
            grid=(1,),
            in_specs=[whole] * 4 + w_specs,
            out_specs=[
                pl.BlockSpec((2 * rows, unit), lambda i, core: (0, 0)),
                pl.BlockSpec((2 * rows, 2 * unit), lambda i, core: (0, 0)),
                *[whole] * 4,
            ],
        ),
        out_shape=[
            like((2 * rows, unit), BF),
            like((2 * rows, 2 * unit), BF),
            *[like((rows, wide), kind) for kind in kinds],
        ],
        cost_estimate=COST,
        compiler_params=params(40),
        name=name,
    )(core, *mixed, *back, large, large, large)


def grads_kernel(y_ref, m0, m1, m2, m3, b0, b1, b2, b3, u0, u1, h0, h1, keep_ref, send_ref):
    rows, unit, half = m0.shape[0], h0.shape[1], keep_ref.shape[1]
    first = y_ref[0] == 0

    def put(at, parts, u0, u1):
        acc = dot(parts[0][...], u0[:rows, :], 0, 0) + dot(parts[1][...], u0[rows:, :], 0, 0)
        acc = acc + dot(parts[2][...], u1[:rows, :], 0, 0) + dot(parts[3][...], u1[rows:, :], 0, 0)
        for z in range(keep_ref.shape[0]):
            low, high = acc[2 * z * half : (2 * z + 1) * half], acc[(2 * z + 1) * half : 2 * (z + 1) * half]
            keep_ref[z, :, at] = jnp.where(first, low, high).astype(BF)
            send_ref[z, :, at] = jnp.where(first, high, low).astype(BF)

    put(slice(0, 2 * unit), (m0, m1, m2, m3), u0, u1)
    put(slice(2 * unit, 3 * unit), (b0, b1, b2, b3), h0, h1)


def feed_grads(y, mixed, back, backs, hidden, line):
    rows, wide = mixed[0].shape
    steps = min(line, wide // 128)
    block, unit = wide // steps, hidden[0].shape[1]
    return pl.pallas_call(
        grads_kernel,
        grid=(steps,),
        in_specs=[SMEM]
        + [pl.BlockSpec((rows, block), lambda z: (0, z))] * 8
        + [pl.BlockSpec((2 * rows, 2 * unit), lambda z: (0, 0))] * 2
        + [pl.BlockSpec((2 * rows, unit), lambda z: (0, 0))] * 2,
        out_specs=[pl.BlockSpec((line // steps, wide // line // 2, 3 * unit), lambda z: (z, 0, 0))] * 2,
        out_shape=[like((line, wide // line // 2, 3 * unit), BF)] * 2,
        cost_estimate=COST,
        compiler_params=params(24),
        name="feed_grads",
    )(y, *mixed, *back, *backs, *hidden)


def after_feed_kernel(
    model, kv_heads, mix_ref, core_ref, far_ref, unit_ref, inv_ref, gain_ref, back_ref, w_ref,
    order_ref, attended_ref, middle_ref, do_ref, dot_ref, gains_ref, split_ref,
):
    unit = unit_ref[...]
    mixed = mix_ref[...] + core_ref[...].astype(F32) + far_ref[...].astype(F32)
    gains_ref[...] = jnp.sum(mixed * unit, axis=0, keepdims=True)
    scaled = mixed * gain_ref[...]
    mean = jnp.sum(scaled * unit, axis=1, keepdims=True) / model
    middle = back_ref[...] + inv_ref[...] * (scaled - unit * mean)
    middle_ref[...] = middle
    low = middle.astype(BF)
    do_ref[...] = dot(w_ref[...], low, 0, 1).astype(BF)
    group = do_ref.shape[0] // HEAD // kv_heads
    dot_ref[...] = jnp.zeros_like(dot_ref)
    for h in range(kv_heads * group):
        at = slice(h * HEAD, (h + 1) * HEAD)
        product = do_ref[at, :].astype(F32) * attended_ref[at, :].astype(F32)
        dot_ref[h // group, h % group : h % group + 1, :] = jnp.sum(product, axis=0, keepdims=True)
    split_ref[...] = dot(order_ref[...], low, 1, 1).astype(BF)


def after_feed(mix, core, far, unit, inv, gain, back, w_out, order, attended, kv_heads, model):
    rows, wide = unit.shape
    width = attended.shape[0]

    shapes = [
        like((rows, wide), F32),
        like((width, rows), BF),
        like((kv_heads, 8, rows), F32),
        like((1, wide), F32),
        like((wide, rows), BF),
    ]
    return pl.pallas_call(
        functools.partial(after_feed_kernel, model, kv_heads),
        in_specs=[VMEM] * 10,
        out_specs=[VMEM] * 5,
        out_shape=shapes,
        cost_estimate=COST,
        compiler_params=params(),
        name="after_feed",
    )(mix, core, far, unit, inv, gain, back, w_out, order, attended)


def backs_kernel(q_part, k_part, dq_ref, far_ref, dkv_ref, chain_ref, cos_ref, sin_ref, out_ref):
    sides = out_ref.shape[0]
    cos, sin = cos_ref[...], sin_ref[...]

    def put(part, base, index, value):
        x, at = divmod(index * HALF_HEAD, part)
        out_ref[x, base + at : base + at + HALF_HEAD, :] = value.astype(BF)

    def turn(part, base, h, value):
        low, high = value[:HALF_HEAD], value[HALF_HEAD:]
        put(part, base, 2 * h, low * cos + high * sin)
        put(part, base, 2 * h + 1, high * cos - low * sin)

    for h in range(sides * q_part // HEAD):
        at = slice(h * HEAD, (h + 1) * HEAD)
        turn(q_part, 0, h, dq_ref[at, :] + far_ref[at, :].astype(F32))
    for h in range(sides * k_part // HEAD):
        at = slice(h * HEAD, (h + 1) * HEAD)
        turn(k_part, q_part, h, dkv_ref[0, at, :] + chain_ref[0, at, :].astype(F32))
    for x in range(sides):
        at = slice(x * k_part, (x + 1) * k_part)
        value = dkv_ref[1, at, :] + chain_ref[1, at, :].astype(F32)
        out_ref[x, q_part + k_part :, :] = value.astype(BF)


def finish_backs(dq, far, dkv, chain, cos, sin, sides, q_part, k_part):
    return pl.pallas_call(
        functools.partial(backs_kernel, q_part, k_part),
        in_specs=[VMEM] * 6,
        out_specs=VMEM,
        out_shape=like((sides, q_part + 2 * k_part, far.shape[1]), BF),
        cost_estimate=COST,
        compiler_params=params(12),
        name="finish_backs",
    )(dq, far, dkv, chain, cos, sin)


def terms_kernel(
    slot, shard, place, n0, n1, p0, p1, d0, d1, o0, o1, l_ref, r_ref, gain_ref, gain2_ref,
    left_keep, left_send, right_keep, right_send, full_ref,
):
    sides, qkv, _ = d0.shape
    half = n0.shape[0]
    ys, cut = l_ref.shape[1], l_ref.shape[3]
    block = half // ys
    spare = lax.broadcasted_iota(jnp.int32, (half, 1), 0) % slot == shard
    first = jnp.zeros((half, 128), F32)
    for x in range(sides - 1, -1, -1):
        acc = dot(n0[...], d0[x], 1, 1) + dot(n1[...], d1[x], 1, 1)
        weights = jnp.concatenate(
            [jnp.concatenate([l_ref[x, y], r_ref[y, x]], axis=1) for y in range(ys)], axis=0
        )
        product = acc * weights[:, :qkv].astype(F32)
        for k in range(0, qkv // 128):
            first = first + product[:, k * 128 : (k + 1) * 128]
        rest = qkv % 128
        if rest:
            tail = product[:, qkv - rest :]
            first = first + jnp.concatenate([tail, jnp.zeros((half, 128 - rest), F32)], axis=1)
        width = left_keep.shape[2] - qkv
        at = slice(x * width, (x + 1) * width)
        other = dot(p0[...], o0[at, :], 1, 1) + dot(p1[...], o1[at, :], 1, 1)
        both = jnp.concatenate([acc, other], axis=1)
        if x == 0:
            gain = jnp.sum(first.T, axis=0, keepdims=True)
            scale = gain_ref[...]
            gain = jnp.where(scale > 0, gain / jnp.maximum(scale, 0.25), 0.0)
        else:
            gain = gain2_ref[...]
        reach = gain.shape[1]
        full_ref[:, :reach] = jnp.where(spare, gain, both[:, :reach]).astype(BF)
        full_ref[:, reach:] = both[:, reach:].astype(BF)
        part = block // 2
        for y in range(ys):
            top = slice(y * block, y * block + part)
            pl.when(place[2] == x)(lambda: left_keep.__setitem__(y, full_ref[top, :]))
            pl.when(place[2] != x)(lambda: left_send.__setitem__(y, full_ref[top, :]))
            low = slice(y * block + part, (y + 1) * block)
            pl.when(place[1] == y)(lambda: right_keep.__setitem__(x, full_ref[low, :]))
            pl.when(place[1] != y)(lambda: right_send.__setitem__(x, full_ref[low, :]))


def small_terms(place, normed, proj, backs, attended, mine, gain, gain2, slot, shard):
    sides, qkv, _ = backs[0].shape
    columns = qkv + attended[0].shape[0] // sides
    half = normed[0].shape[0]
    arrays = (*normed, *proj, *backs, *attended, *mine, gain, gain2)
    outs = [like((2, half // 4, columns), BF)] * 4
    return pl.pallas_call(
        functools.partial(terms_kernel, slot, shard),
        grid=(1,),
        in_specs=[SMEM] + [full(a) for a in arrays],
        out_specs=[full(o) for o in outs],
        out_shape=outs,
        scratch_shapes=[pltpu.VMEM((half, columns), BF)],
        cost_estimate=COST,
        compiler_params=params(57),
        name="small_terms",
    )(place, *arrays)


def second_kernel(which, place, keep_ref, far_ref, out_ref, send_ref):
    total = (keep_ref[...].astype(F32) + far_ref[...].astype(F32)).astype(BF)
    first = place[which] == 0
    out_ref[...] = jnp.where(first, total[0], total[1])
    send_ref[...] = jnp.where(first, total[1], total[0])


def second_fold(place, which, keep, far):
    return pl.pallas_call(
        functools.partial(second_kernel, which),
        in_specs=[SMEM, VMEM, VMEM],
        out_specs=[VMEM] * 2,
        out_shape=[like(keep.shape[1:], BF)] * 2,
        cost_estimate=COST,
        compiler_params=params(12),
        name="second_fold",
    )(place, keep, far)


def join_kernel(a0, a1, b0, b1, out_ref):
    out_ref[0] = (a0[...].astype(F32) + a1[...].astype(F32)).astype(BF)
    out_ref[1] = (b0[...].astype(F32) + b1[...].astype(F32)).astype(BF)


def join(left, right):
    return pl.pallas_call(
        join_kernel,
        in_specs=[VMEM] * 4,
        out_specs=VMEM,
        out_shape=like((2, *left[0].shape), BF),
        cost_estimate=COST,
        compiler_params=params(12),
        name="join",
    )(*left, *right)


def small_sums_kernel(shard, slot, q_part, k_part, at_ref, in_ref, q_ref, k_ref, v_ref, o_ref, gain_ref):
    total = in_ref[0].astype(F32)
    for i in range(1, in_ref.shape[0]):
        total = total + in_ref[i].astype(F32)
    q_ref[...] = total[:shard, :q_part]
    k_ref[...] = total[:shard, q_part : q_part + k_part]
    v_ref[...] = total[:shard, q_part + k_part : q_part + 2 * k_part]
    o_ref[...] = total[:shard, q_part + 2 * k_part :]
    gain = jnp.zeros((1, shard), F32)
    for block in range(total.shape[1] // slot):
        part = total[shard : shard + 1, block * slot : block * slot + shard]
        gain = jnp.where(at_ref[0] == block, part, gain)
    gain_ref[...] = gain


def small_sums(at, parts, shard, q_part, k_part):
    slot = parts.shape[1]
    return pl.pallas_call(
        functools.partial(small_sums_kernel, shard, slot, q_part, k_part),
        in_specs=[SMEM, VMEM],
        out_specs=[VMEM] * 5,
        out_shape=[like((shard, n), F32) for n in (q_part, k_part, k_part, q_part)]
        + [like((1, shard), F32)],
        cost_estimate=COST,
        compiler_params=params(12),
        name="small_sums",
    )(at, parts)


def add_wide(a, b):
    return pl.pallas_call(
        add_kernel,
        grid=(1,),
        in_specs=[full(a), full(b)],
        out_specs=full(a),
        out_shape=pltpu.HBM(a.shape, BF),
        cost_estimate=COST,
        compiler_params=params(24),
        name="add_wide",
    )(a, b)


def sum_blocks_kernel(place, *refs):
    *parts, keep_ref, send_ref = refs
    half = keep_ref.shape[0]
    total = parts[0][...].astype(F32)
    for part in parts[1:]:
        total = total + part[...].astype(F32)
    total = total.astype(BF)
    first = place[3] == 0
    keep_ref[...] = jnp.where(first, total[:half], total[half:])
    send_ref[...] = jnp.where(first, total[half:], total[:half])


def sum_blocks(place, parts):
    outs = [like((parts[0].shape[0] // 2, parts[0].shape[1]), BF)] * 2
    return pl.pallas_call(
        sum_blocks_kernel,
        grid=(1,),
        in_specs=[SMEM] + [full(p) for p in parts],
        out_specs=[full(o) for o in outs],
        out_shape=outs,
        cost_estimate=COST,
        compiler_params=params(16),
        name="sum_blocks",
    )(place, *parts)


def large_sums_kernel(shard, place, own_ref, far_ref, *refs):
    unit = refs[0].shape[1] // 2
    first = place[3] == 0
    own, far = own_ref[:shard, :].astype(F32), far_ref[:shard, :].astype(F32)
    low, high = jnp.where(first, own, far), jnp.where(first, far, own)
    for k, ref in enumerate(refs):
        ref[:, :unit] = low[:, k * unit : (k + 1) * unit]
        ref[:, unit:] = high[:, k * unit : (k + 1) * unit]


def large_sums(place, own, far, shard):
    unit = own.shape[1] // 3
    return pl.pallas_call(
        functools.partial(large_sums_kernel, shard),
        in_specs=[SMEM, VMEM, VMEM],
        out_specs=[VMEM] * 3,
        out_shape=[like((shard, 2 * unit), F32)] * 3,
        cost_estimate=COST,
        compiler_params=params(16),
        name="large_sums",
    )(place, own, far)


def exact_dot(one_hot, wide, ca, cb):
    high = wide.astype(BF)
    low = (wide - high.astype(F32)).astype(BF)
    return dot(one_hot, high, ca, cb) + dot(one_hot, low, ca, cb)


def input_kernel(
    model, d_ref, lm, rm, lt, rt, unit_ref, inv_ref, gain_ref, middle_ref, spread_ref, split_ref,
    out_ref, m_ref,
):
    sides, ys, block, cut = lm.shape
    qkv = d_ref.shape[1]
    half = ys * block
    for side, (l, r) in enumerate(((lm, rm), (lt, rt))):
        for y in range(ys):
            at = slice(side * half + y * block, side * half + (y + 1) * block)
            total = None
            for x in range(sides):
                a = dot(l[x, y], d_ref[x, :cut, :], 1, 0)
                a = a + dot(r[y, x][:, : qkv - cut], d_ref[x, cut:, :], 1, 0)
                total = a if total is None else total + a
            m_ref[at, :] = total * gain_ref[at, :]
    unit = unit_ref[...]
    scaled = m_ref[...]
    mean = jnp.sum(scaled * unit, axis=0, keepdims=True) / model
    back = inv_ref[...] * (scaled - unit * mean)
    grad = exact_dot(spread_ref[...], middle_ref[...], 1, 1) + exact_dot(split_ref[...], back, 1, 0)
    part = grad.shape[1] // 2
    out_ref[0] = grad[:, :part]
    out_ref[1] = grad[:, part:]


def input_gradient(backs, mine, theirs, unit, inv, gain, middle, spread, split, model):
    out = like((2, model, middle.shape[0] // 2), F32)
    arrays = (backs, *mine, *theirs, unit, inv, gain, middle, spread, split)
    return pl.pallas_call(
        functools.partial(input_kernel, model),
        grid=(1,),
        in_specs=[full(a) for a in arrays],
        out_specs=full(out),
        out_shape=out,
        scratch_shapes=[pltpu.VMEM(unit.shape, F32)],
        cost_estimate=COST,
        compiler_params=params(40),
        name="input_gradient",
    )(*arrays)


def output_kernel(middle_ref, own_ref, core_ref, far_ref, spread_ref, out_ref):
    result = middle_ref[...] + own_ref[...] + core_ref[...].astype(F32) + far_ref[...].astype(F32)
    out = dot(spread_ref[...], result.astype(BF), 1, 1).astype(BF)
    part = out.shape[1] // 2
    out_ref[0] = out[:, :part]
    out_ref[1] = out[:, part:]


def layer_output(middle, own, core, far, spread):
    return pl.pallas_call(
        output_kernel,
        in_specs=[VMEM] * 5,
        out_specs=VMEM,
        out_shape=like((2, spread.shape[0], middle.shape[0] // 2), BF),
        cost_estimate=COST,
        compiler_params=params(),
        name="layer_output",
    )(middle, own, core, far, spread)


def padded(count):
    return -(-count // 8) * 8


def pick(pair, index):
    return jnp.where(index == 0, pair[0], pair[1])


def ordered(mine, theirs, index, axis):
    return jnp.concatenate([pick((mine, theirs), index), pick((theirs, mine), index)], axis=axis)


def swap(array, name):
    return lax.ppermute(array, name, SWAP)


def after(value, *earlier):
    return lax.optimization_barrier((value, *earlier))[0]


def spread_matrix(model, shard, slot, ctx):
    row = lax.broadcasted_iota(jnp.int32, (model, slot * ctx), 0)
    col = lax.broadcasted_iota(jnp.int32, (model, slot * ctx), 1)
    return (col == row // shard * slot + row % shard).astype(BF)


def core_order(slot, line, c):
    wide = slot * line * 4
    row = lax.broadcasted_iota(jnp.int32, (wide, wide), 1)
    col = lax.broadcasted_iota(jnp.int32, (wide, wide), 0)
    block, place = row // slot, row % slot
    core, y, z = block % 2, block // 2 % 2, block // 4
    other = (core != c).astype(jnp.int32)
    return (col == ((other * 2 + y) * line + z) * slot + place).astype(BF)


def gather_small(rows_here, cut, meanwhile):
    line = lax.axis_size("zh") * lax.axis_size("zl")
    d, y = lax.axis_index("dp"), lax.axis_index("y")
    z_all = lax.all_to_all(
        jnp.broadcast_to(rows_here[None], (line, *rows_here.shape)),
        ("zh", "zl"),
        split_axis=0,
        concat_axis=0,
    )
    z_all = after(z_all, *meanwhile).reshape(1, -1, rows_here.shape[1])
    left, right = z_all[..., :cut], z_all[..., cut:]
    left, right = ordered(left, swap(left, "y"), y, 0), ordered(right, swap(right, "dp"), d, 0)
    left, right = left[None], right[None]
    return ordered(left, swap(left, "dp"), d, 0), ordered(right, swap(right, "y"), y, 0)


def body(
    inputs,
    query_weight,
    key_weight,
    value_matrix,
    out_weight,
    gate_weight,
    up_weight,
    down_weight,
    norm_gains,
    cotangent,
):
    seqs, part_rows, model = inputs.shape
    dps, high, low = (lax.axis_size(a) for a in ("dp", "zh", "zl"))
    line = high * low
    ctx = line * 4
    y, c, d = (lax.axis_index(a) for a in ("y", "c", "dp"))
    z = lax.axis_index("zh") * low + lax.axis_index("zl")
    shard = model // ctx
    slot = padded(shard + 1)
    wide = slot * ctx
    half = wide // 2
    rows = 2 * part_rows
    up_line = [(i, i + 1) for i in range(line - 1)]
    down_line = [(i + 1, i) for i in range(line - 1)]
    z_axes = ("zh", "zl")
    everywhere = ("zh", "zl", "y", "c")
    place = jnp.stack([z, y, d, c]).astype(jnp.int32)

    q_part, k_part = query_weight.shape[1], key_weight.shape[1]
    qkv_part = q_part + 2 * k_part
    half_ff = gate_weight.shape[1]
    unit = half_ff // 2
    kv_heads = k_part * dps // HEAD

    small = jnp.concatenate([query_weight, key_weight, value_matrix], axis=1)
    small_columns = -(-qkv_part // 128) * 128
    small = jnp.concatenate(
        [
            jnp.pad(small, ((0, 0), (0, small_columns - qkv_part))),
            jnp.pad(norm_gains, ((0, slot - shard - 1), (0, small_columns - shard))),
        ],
        axis=0,
    )
    out_shard = after(out_weight.T, small)
    large = jnp.concatenate(
        [gate_weight, up_weight, down_weight.T, ordered(out_shard, swap(out_shard, "dp"), d, 1)],
        axis=1,
    )
    large = jnp.pad(large, ((0, slot - shard), (0, 0)))
    large = lax.all_gather(large, everywhere, axis=0, tiled=True)
    w_out = large[:, 3 * half_ff :]

    both = jnp.stack([inputs, cotangent], axis=1)
    mine, theirs = pick((both[0], both[1]), c), pick((both[1], both[0]), c)
    both = ordered(mine, swap(theirs, "c"), c, 1)
    spread = spread_matrix(model, shard, slot, ctx)
    by_core = core_order(slot, line, c)
    spread, by_core = after(spread, small), after(by_core, small)
    spread_split = dot(spread, by_core, 1, 1).astype(BF)
    tokens = dot(both[0], spread, 1, 0)
    tokens_t = dot(spread_split, both[0], 0, 1)
    back_out = dot(both[1], spread, 1, 0)
    back_low = back_out.astype(BF)
    inv_first = lax.rsqrt(jnp.sum(tokens_t * tokens_t, axis=0, keepdims=True) / model + EPSILON)
    unit_first = tokens_t * inv_first
    positions = (2 * z + y) * rows + jnp.arange(rows, dtype=jnp.int32)
    cos, sin = rope_tables(positions, HALF_HEAD)

    w_mine = gather_small(small, small_columns // 256 * 128, (unit_first, tokens, back_low))
    w_theirs = tuple(swap(w, "c") for w in w_mine)

    def gains_of(w):
        part = w[0].reshape(dps, 2, line, slot, -1)[:, :, :, shard, :shard]
        return jnp.pad(part, ((0, 0), (0, 0), (0, 0), (0, slot - shard))).astype(F32)

    gains_mine, gains_theirs = gains_of(w_mine), gains_of(w_theirs)
    gain_second = ordered(gains_mine[1, :, :, None], gains_theirs[1, :, :, None], c, 2)
    gain_second = gain_second.transpose(1, 0, 2, 3).reshape(1, wide)
    gain_first = jnp.concatenate([gains_mine[0], gains_theirs[0]], axis=0).reshape(wide, 1)
    gains_mine = gains_mine[0].reshape(1, half)
    gain_first, gain_second, gains_mine = lax.optimization_barrier(
        (gain_first, gain_second, gains_mine)
    )

    normed = (unit_first * gain_first).astype(BF)
    q, kv = project(normed, cos, sin, w_mine, w_theirs, q_part, k_part)

    kvs = [kv]
    back_core, back_far = swap(after(back_low, kv), "c"), swap(after(back_low, kv), "dp")
    q_both = (q, swap(q, "y"))
    state = ()
    for step in range(line - 1):
        here, far_q = kvs[-1], q_both[1]
        if step > 1:
            here, state = lax.optimization_barrier((here, state))
        kvs.append(lax.ppermute(here, z_axes, up_line))
        if step > 0:
            far_q = after(far_q, here)
            state = attend_forward(place, step - 1, False, q, far_q, kvs[step - 1], state, kv_heads)
    far_q = after(q_both[1], kvs[-2])
    state = attend_forward(place, line - 2, False, q, far_q, kvs[line - 2], state, kv_heads)
    stats, acc, far_stats, far_acc = attend_forward(
        place, line - 1, True, *q_both, kvs[line - 1], state, kv_heads
    )
    got = lax.ppermute(jnp.stack([far_stats, stats]), "y", SWAP)
    attended, lse, far_lse, middle, unit_second, inv_second, mixed_own = to_middle(
        (stats, far_stats), (got[0], got[1]), acc, swap(far_acc, "y"), w_out, tokens, gain_second,
        kv_heads, model,
    )

    mixed_core, mixed_far = swap(mixed_own, "c"), swap(mixed_own, "dp")
    core = c.astype(jnp.int32)[None]
    hidden_near, backs_near, part_own, part_core, mix_own, mix_core = feed_forward(
        core, (mixed_own, mixed_core), (back_low, back_core), large, unit, "feed_near"
    )
    mixed_far = after(mixed_far, mix_own)
    back_far = after(back_far, stats)
    mixed_far, back_far = (mixed_far, swap(mixed_far, "c")), (back_far, swap(back_far, "c"))
    hidden_far, backs_far, part_far, part_cross, mix_far, mix_cross = feed_forward(
        core, mixed_far, back_far, large, unit, "feed_far"
    )
    mix_core = swap(mix_core, "c")
    mix_far = add_low(mix_far, swap(mix_cross, "c"))
    hidden_near, mix_far_sum = after(hidden_near, mix_far), mix_far
    mix_far = swap(mix_far_sum, "dp")

    mixed_all, back_all = (mixed_own, mixed_core, *mixed_far), (back_low, back_core, *back_far)
    grads_keep, grads_send = feed_grads(
        y.astype(jnp.int32)[None], mixed_all, back_all, (backs_near, backs_far), (hidden_near, hidden_far), line
    )
    normed_pair = (normed[:half], swap(normed[half:], "c"))
    attended_pair = (attended, swap(attended, "c"))
    part_far = add_low(part_far, swap(part_cross, "c"))
    mix_far = after(mix_far, grads_keep, normed_pair[1], attended_pair[1], part_far)

    back_middle, do, row_dot, gain_terms, proj = after_feed(
        mix_own, mix_core, mix_far, unit_second, inv_second, gain_second, back_out, w_out, by_core,
        attended, kv_heads, model,
    )
    proj_pair = (proj[:half], swap(proj[half:], "c"))
    gain_terms = gain_terms + swap(gain_terms, "c")
    do_far, dot_far = swap(do, "y"), swap(row_dot, "y")
    do_far = after(do_far, proj_pair[1], gain_terms)
    do_both, dot_both, lse_both = (do, do_far), (row_dot, dot_far), (lse, far_lse)

    grads_far = swap(after(grads_send, do_far, dot_far), "y")
    part_far = swap(after(part_far, do_far), "dp")
    part_core = swap(part_core, "c")
    chain, dq = None, ()
    for step in range(line - 1, 0, -1):
        keys_here = kvs[step]
        if step == 1:
            keys_here = after(keys_here, part_far, part_core)
        if step < line - 2:
            keys_here, chain = lax.optimization_barrier((keys_here, chain))
        *dq, total = attend_backward(
            place, step, q_both, do_both, lse_both, dot_both, keys_here, dq, kv_heads
        )
        if chain is not None:
            total = add_low(total, lax.ppermute(chain, z_axes, down_line))
        chain = total
    dq, dq_send, dkv = attend_backward(
        place, 0, q_both, do_both, lse_both, dot_both, after(kvs[0], chain), dq, kv_heads
    )
    dq_far = swap(dq_send, "y")
    chain = lax.ppermute(after(chain, dq_send), z_axes, down_line)
    grads = add_wide(grads_keep, after(grads_far, dq)).reshape(line * 2 * slot, -1)
    grads = lax.psum_scatter(grads, z_axes, scatter_dimension=0, tiled=True)
    backs = finish_backs(dq, dq_far, dkv, chain, cos, sin, dps, q_part, k_part)

    left_keep, left_send, right_keep, right_send = small_terms(
        place, normed_pair, proj_pair, (backs, swap(backs, "c")), attended_pair, w_mine, gains_mine,
        gain_terms, slot, shard,
    )
    left_far, right_far = swap(left_send, "dp"), swap(right_send, "y")
    (
        backs, part_far, part_core, part_own, middle, back_middle, unit_first, spread, spread_split,
        *weights, _,
    ) = lax.optimization_barrier(
        (
            backs, part_far, part_core, part_own, middle, back_middle, unit_first, spread,
            spread_split, *w_mine, *w_theirs, left_keep,
        )
    )
    input_grad = input_gradient(
        backs, weights[:2], weights[2:], unit_first, inv_first, gain_first, back_middle, spread,
        spread_split, model,
    )
    layer_out = layer_output(middle, part_own, part_core, part_far, spread)
    left_far = after(left_far, input_grad, layer_out)
    left_keep, left_send = second_fold(place, 1, left_keep, left_far)
    right_keep, right_send = second_fold(place, 2, right_keep, right_far)
    terms = join((left_keep, swap(left_send, "y")), (right_keep, swap(right_send, "dp")))
    grads_keep, grads_send = sum_blocks(place, (grads,))
    gate_grad, up_grad, down_grad = large_sums(place, grads_keep, swap(grads_send, "c"), shard)
    terms = lax.all_to_all(
        terms.reshape(line, slot, -1), z_axes, split_axis=0, concat_axis=0
    )
    place_of_gains = jnp.where(d == 0, y * line + z, (z * 2 + y) * 2 + c).astype(jnp.int32)[None]
    terms = after(terms, gate_grad)
    query_grad, key_grad, value_grad, out_grad, gains_grad = small_sums(
        place_of_gains, terms, shard, q_part, k_part
    )

    def give_back(array):
        keep, send = pick((array[0], array[1]), c), pick((array[1], array[0]), c)
        return ordered(keep[None], swap(send, "c")[None], c, 0)

    return (
        give_back(layer_out).transpose(0, 2, 1),
        give_back(input_grad).transpose(0, 2, 1),
        query_grad,
        key_grad,
        value_grad,
        out_grad.T,
        gate_grad,
        up_grad,
        down_grad.T,
        gains_grad,
    )


def solution(mesh):
    devices = mesh.devices
    dps, ctx = devices.shape
    inner = Mesh(devices.reshape(dps, 2, ctx // 8, 2, 2), ("dp", "zh", "zl", "y", "c"))
    along = ("zh", "zl", "y", "c")
    rows, by_row, by_col = P("dp", along, None), P(along, "dp"), P("dp", along)
    return jax.shard_map(
        body,
        mesh=inner,
        in_specs=(rows, by_row, by_row, by_row, by_col, by_row, by_row, by_col, by_col, rows),
        out_specs=(rows, rows, by_row, by_row, by_row, by_col, by_row, by_row, by_col, by_col),
        check_vma=False,
    )
```

```python
import functools
import math

import jax
import jax.numpy as jnp
from jax import lax
from jax.experimental import pallas as pl
from jax.experimental.pallas import tpu as pltpu
from jax.sharding import Mesh, PartitionSpec as P

HEAD = 64
HALF_HEAD = HEAD // 2
EPSILON = 1e-05
MASKED = -1e30
FLOOR = -1e20
LOG2E = 1.4426950408889634
SCALE = 0.125 * LOG2E
BF = jnp.bfloat16
F32 = jnp.float32
SWAP = [(0, 1), (1, 0)]
COST = pl.CostEstimate(flops=1000, bytes_accessed=1000, transcendentals=0)
VMEM = pl.BlockSpec(memory_space=pltpu.VMEM)
SMEM = pl.BlockSpec(memory_space=pltpu.SMEM)


def params(mib=32):
    return pltpu.CompilerParams(vmem_limit_bytes=mib * 2**20)


def dot(a, b, ca, cb):
    return lax.dot_general(a, b, (((ca,), (cb,)), ((), ())), preferred_element_type=F32)


def full(array):
    return pl.BlockSpec(array.shape, lambda i: (0,) * len(array.shape))


def like(shape, kind):
    return jax.ShapeDtypeStruct(shape, kind)


def rope_tables(positions, half):
    spectrum = jnp.exp(jnp.arange(half, dtype=F32) * (-math.log(100000.0) / half))
    angles = spectrum[:, None] * positions.astype(F32)[None, :]
    return jnp.cos(angles), jnp.sin(angles)


def project_kernel(
    q_part, k_part, cut, normed_ref, cos_ref, sin_ref, lm, rm, lt, rt, q_ref, kv_ref, raw_ref
):
    sides, ys, block, _ = lm.shape
    half = ys * block
    for x in range(sides):
        left = right = None
        for side, (l, r) in enumerate(((lm, rm), (lt, rt))):
            for y in range(ys):
                at = side * half + y * block
                rows = normed_ref[at : at + block, :]
                a, b = dot(l[x, y], rows, 0, 0), dot(r[y, x], rows, 0, 0)
                left = a if left is None else left + a
                right = b if right is None else right + b
        raw_ref[x, :cut, :] = left
        raw_ref[x, cut:, :] = right
    cos, sin = cos_ref[...], sin_ref[...]

    def half_rows(part, base, index):
        x, at = divmod(index * HALF_HEAD, part)
        return raw_ref[x, base + at : base + at + HALF_HEAD, :]

    def turn(part, base, out_ref, heads):
        for h in range(heads):
            low, high = half_rows(part, base, 2 * h), half_rows(part, base, 2 * h + 1)
            out_ref[h * HEAD : h * HEAD + HALF_HEAD, :] = (low * cos - high * sin).astype(BF)
            out_ref[h * HEAD + HALF_HEAD : (h + 1) * HEAD, :] = (high * cos + low * sin).astype(BF)

    turn(q_part, 0, q_ref, sides * q_part // HEAD)
    turn(k_part, q_part, kv_ref, sides * k_part // HEAD)
    for x in range(sides):
        base = sides * k_part + x * k_part
        kv_ref[base : base + k_part, :] = raw_ref[
            x, q_part + k_part : q_part + 2 * k_part, :
        ].astype(BF)


def project(normed, cos, sin, mine, theirs, q_part, k_part):
    sides, _, _, cut = mine[0].shape
    rows = normed.shape[1]
    return pl.pallas_call(
        functools.partial(project_kernel, q_part, k_part, cut),
        in_specs=[VMEM] * 7,
        out_specs=[VMEM] * 2,
        out_shape=[like((sides * q_part, rows), BF), like((2 * sides * k_part, rows), BF)],
        scratch_shapes=[pltpu.VMEM((sides, cut + mine[1].shape[3], rows), F32)],
        cost_estimate=COST,
        compiler_params=params(),
        name="project",
    )(normed, cos, sin, *mine, *theirs)


def abreast(group, own, far, at):
    parts = []
    for h in range(group):
        parts.append(own[at(h)])
        if far is not None:
            parts.append(far[at(h)])
    return jnp.concatenate(parts, axis=1) if len(parts) > 1 else parts[0]


def head_rows(h):
    return (slice(h * HEAD, (h + 1) * HEAD), slice(None))


def stat_row(h):
    return (0, slice(h, h + 1), slice(None))


def causal(keys, rows, group, both):
    key_pos = lax.broadcasted_iota(jnp.int32, (keys, rows), 0)
    own = lax.broadcasted_iota(jnp.int32, (keys, rows), 1) >= key_pos
    parts = [own, jnp.ones_like(own)] if both else [own]
    return jnp.concatenate(parts * group, axis=1)


def forward_kernel(step, last, group, place, q_ref, far_q_ref, k_ref, v_ref, *refs):
    rows = q_ref.shape[1]
    stat_ref, acc_ref, far_stat_ref, far_acc_ref = refs[-4:]

    def visit(both):
        far = (lambda ref: ref) if both else (lambda ref: None)
        scores = dot(k_ref[...], abreast(group, q_ref, far(far_q_ref), head_rows), 0, 0) * SCALE
        if step == 0:
            scores = jnp.where(causal(scores.shape[0], rows, group, both), scores, MASKED)
        top = jnp.max(scores, axis=0, keepdims=True)
        if step:
            old = abreast(group, refs[0], refs[2], stat_row)
            top = jnp.maximum(top, old)
            shrink = jnp.exp2(old - top)
        probs = jnp.exp2(scores - top)
        total = jnp.sum(probs, axis=0, keepdims=True)
        if step:
            total = total + abreast(group, refs[0], refs[2], lambda h: stat_row(group + h)) * shrink
        acc = dot(v_ref[...], probs.astype(BF), 1, 0)
        sides = ((0, stat_ref, acc_ref), (1, far_stat_ref, far_acc_ref)) if both else ((0, stat_ref, acc_ref),)
        for h in range(group):
            for side, stats, out in sides:
                at = (h * len(sides) + side) * rows
                at = slice(at, at + rows)
                value = acc[:, at]
                if step:
                    value = value + refs[2 * side + 1][head_rows(h)] * shrink[:, at]
                out[head_rows(h)] = value.astype(out.dtype)
                stats[stat_row(h)] = top[:, at]
                stats[stat_row(group + h)] = total[:, at]

    if step == 0:
        pl.when(place[1] == 0)(lambda: visit(True))

        @pl.when(place[1] != 0)
        def _():
            visit(False)
            far_stat_ref[0, :group, :] = jnp.full((group, rows), FLOOR, F32)
            far_stat_ref[0, group : 2 * group, :] = jnp.zeros((group, rows), F32)
            far_acc_ref[...] = jnp.zeros_like(far_acc_ref)
    else:
        pl.when(step <= place[0])(lambda: visit(True))

        @pl.when(step > place[0])
        def _():
            for old, new in zip(refs[:4], refs[-4:]):
                new[...] = old[...].astype(new.dtype)


def attend_forward(place, step, last, q, far_q, kv, state, kv_heads):
    width, rows = q.shape
    group = width // HEAD // kv_heads
    keys = kv.shape[1]
    wide = pl.BlockSpec((group * HEAD, rows), lambda g: (g, 0))
    stat = pl.BlockSpec((1, 8, rows), lambda g: (g, 0, 0))
    first = pl.BlockSpec((HEAD, keys), lambda g: (g, 0))
    second = pl.BlockSpec((HEAD, keys), lambda g: (g + kv_heads, 0))
    stats = like((kv_heads, 8, rows), F32)
    aliases = {5: 0, 6: 1, 7: 2} if last else {5: 0, 6: 1, 7: 2, 8: 3}
    return pl.pallas_call(
        functools.partial(forward_kernel, step, last, group),
        grid=(kv_heads,),
        in_specs=[SMEM, wide, wide, first, second] + ([stat, wide] * 2 if step else []),
        out_specs=[stat, wide] * 2,
        out_shape=[stats, like((width, rows), F32), stats, like((width, rows), BF if last else F32)],
        input_output_aliases=aliases if step else {},
        cost_estimate=COST,
        compiler_params=params(12),
        name=f"attend_forward_{step}",
    )(place, q, far_q, kv, kv, *state)


def backward_kernel(
    step, group, place, q_ref, far_q_ref, do_ref, far_do_ref, lse_ref, far_lse_ref, dot_ref,
    far_dot_ref, k_ref, v_ref, *refs,
):
    dq_ref, far_dq_ref, dkv_ref = refs[-3:]
    more = len(refs) > 3
    rows = q_ref.shape[1]

    def visit(both):
        key, value = k_ref[...], v_ref[...]
        far = (lambda ref: ref) if both else (lambda ref: None)
        q = abreast(group, q_ref, far(far_q_ref), head_rows)
        do = abreast(group, do_ref, far(far_do_ref), head_rows)
        lse = abreast(group, lse_ref, far(far_lse_ref), stat_row)
        total = abreast(group, dot_ref, far(far_dot_ref), stat_row)
        probs = jnp.exp2(dot(key, q, 0, 0) * SCALE - lse)
        if step == 0:
            probs = jnp.where(causal(probs.shape[0], rows, group, both), probs, 0.0)
        back = (probs * (dot(value, do, 0, 0) - total)).astype(BF)
        dkv_ref[0] = (dot(back, q, 1, 1).T * 0.125).astype(dkv_ref.dtype)
        dkv_ref[1] = dot(probs.astype(BF), do, 1, 1).T.astype(dkv_ref.dtype)
        dq = dot(key, back, 1, 0) * 0.125
        sides = (dq_ref, far_dq_ref) if both else (dq_ref,)
        for h in range(group):
            for side, out in enumerate(sides):
                at = (h * len(sides) + side) * rows
                value = dq[:, at : at + rows]
                if more:
                    value = value + refs[side][head_rows(h)]
                out[head_rows(h)] = value.astype(out.dtype)

    if step == 0:
        pl.when(place[1] == 0)(lambda: visit(True))

        @pl.when(place[1] != 0)
        def _():
            visit(False)
            if more:
                far_dq_ref[...] = refs[1][...].astype(far_dq_ref.dtype)
            else:
                far_dq_ref[...] = jnp.zeros_like(far_dq_ref)
    else:
        pl.when(step <= place[0])(lambda: visit(True))

        @pl.when(step > place[0])
        def _():
            for i, ref in enumerate((dq_ref, far_dq_ref)):
                ref[...] = refs[i][...] if more else jnp.zeros_like(ref)
            dkv_ref[...] = jnp.zeros_like(dkv_ref)


def attend_backward(place, step, q, do, lse, row_dot, kv, dq, kv_heads):
    width, rows = q[0].shape
    group = width // HEAD // kv_heads
    keys = kv.shape[1]
    wide = pl.BlockSpec((group * HEAD, rows), lambda g: (g, 0))
    stat = pl.BlockSpec((1, 8, rows), lambda g: (g, 0, 0))
    first = pl.BlockSpec((HEAD, keys), lambda g: (g, 0))
    second = pl.BlockSpec((HEAD, keys), lambda g: (g + kv_heads, 0))
    kind = BF if step else F32
    aliases = ({11: 0, 12: 1} if step else {11: 0}) if dq else {}
    return pl.pallas_call(
        functools.partial(backward_kernel, step, group),
        grid=(kv_heads,),
        in_specs=[SMEM] + [wide] * 4 + [stat] * 4 + [first, second] + [wide] * len(dq),
        out_specs=[wide, wide, pl.BlockSpec((2, HEAD, keys), lambda g: (0, g, 0))],
        out_shape=[
            like((width, rows), F32),
            like((width, rows), F32 if step else BF),
            like((2, kv_heads * HEAD, keys), kind),
        ],
        input_output_aliases=aliases,
        cost_estimate=COST,
        compiler_params=params(12),
        name=f"attend_backward_{step}",
    )(place, *q, *do, *lse, *row_dot, kv, kv, *dq)


def add_kernel(a_ref, b_ref, out_ref):
    out_ref[...] = (a_ref[...].astype(F32) + b_ref[...].astype(F32)).astype(out_ref.dtype)


def add_low(a, b):
    return pl.pallas_call(
        add_kernel,
        in_specs=[VMEM] * 2,
        out_specs=VMEM,
        out_shape=like(a.shape, BF),
        cost_estimate=COST,
        compiler_params=params(12),
        name="add_low",
    )(a, b)


def pair_rows(side, part):
    return tuple(pl.ds(pl.multiple_of(i * part, 16), part) for i in (side, 1 - side))


def middle_kernel(
    kv_heads, model, place, stat_ref, far_stat_ref, got_ref, far_got_ref, acc_ref, far_ref, w_ref,
    far_w_ref, tokens_ref, gain_ref, attended_ref, lse_ref, far_lse_ref, middle_ref, unit_ref, inv_ref, mixed_ref,
):
    group = acc_ref.shape[0] // HEAD // kv_heads
    lse_ref[...] = jnp.zeros_like(lse_ref)
    far_lse_ref[...] = jnp.zeros_like(far_lse_ref)
    for g in range(kv_heads):
        for h in range(group):
            at = slice((g * group + h) * HEAD, (g * group + h + 1) * HEAD)
            m, s = slice(h, h + 1), slice(group + h, group + h + 1)
            top = jnp.maximum(far_stat_ref[g, m, :], far_got_ref[g, m, :])
            total = far_stat_ref[g, s, :] * jnp.exp2(far_stat_ref[g, m, :] - top)
            total = total + far_got_ref[g, s, :] * jnp.exp2(far_got_ref[g, m, :] - top)
            far_lse_ref[g, m, :] = top + jnp.log2(total)
            top = jnp.maximum(stat_ref[g, m, :], got_ref[g, m, :])
            near, far = jnp.exp2(stat_ref[g, m, :] - top), jnp.exp2(got_ref[g, m, :] - top)
            total = stat_ref[g, s, :] * near + got_ref[g, s, :] * far
            lse_ref[g, m, :] = top + jnp.log2(total)
            value = acc_ref[at, :] * (near / total) + far_ref[at, :].astype(F32) * (far / total)
            attended_ref[at, :] = value.astype(BF)
    part = attended_ref.shape[0] // 2
    near, far = pair_rows(place[2], part)
    middle = tokens_ref[...] + dot(attended_ref[near, :], w_ref[:, :part], 0, 1)
    middle = middle + dot(attended_ref[far, :], far_w_ref[:, :part], 0, 1)
    inv = lax.rsqrt(jnp.sum(middle * middle, axis=1, keepdims=True) / model + EPSILON)
    unit = middle * inv
    middle_ref[...] = middle
    unit_ref[...] = unit
    inv_ref[...] = inv
    mixed_ref[...] = (unit * gain_ref[...]).astype(BF)


def to_middle(place, stats, got, acc, far, w_out, tokens, gain, kv_heads, model):
    width, rows = far.shape
    wide = tokens.shape[1]
    shape = stats[0].shape
    return pl.pallas_call(
        functools.partial(middle_kernel, kv_heads, model),
        in_specs=[SMEM] + [VMEM] * 10,
        out_specs=[VMEM] * 7,
        out_shape=[
            like((width, rows), BF),
            like(shape, F32),
            like(shape, F32),
            like((rows, wide), F32),
            like((rows, wide), F32),
            like((rows, 1), F32),
            like((rows, wide), BF),
        ],
        cost_estimate=COST,
        compiler_params=params(16),
        name="to_middle",
    )(place, *stats, *got, acc, far, *w_out, tokens, gain)


def copy_kernel(in_ref, out_ref):
    out_ref[...] = in_ref[...]


def last_columns(array, columns):
    rows, first = array.shape[0], (array.shape[1] - columns) // 128
    return pl.pallas_call(
        copy_kernel,
        grid=(-(-columns // 128),),
        in_specs=[pl.BlockSpec((rows, 128), lambda i: (0, first + i))],
        out_specs=pl.BlockSpec((rows, 128), lambda i: (0, i)),
        out_shape=like((rows, columns), array.dtype),
        cost_estimate=COST,
        compiler_params=params(57),
        name="last_columns",
    )(array)


def feed_kernel(m0, m1, b0, b1, gate_ref, up_ref, down_ref, *refs):
    hidden_ref, backs_ref, p0, p1, x0, x1 = refs
    rows, unit = m0.shape[0], gate_ref.shape[1]
    for t, (mixed_ref, back_ref, part_ref, mix_ref) in enumerate(((m0, b0, p0, x0), (m1, b1, p1, x1))):
        at = slice(t * rows, (t + 1) * rows)
        gate = dot(mixed_ref[...], gate_ref[...], 1, 0)
        lift = dot(mixed_ref[...], up_ref[...], 1, 0)
        back = dot(back_ref[...], down_ref[...], 1, 0)
        sig = 1.0 / (1.0 + jnp.exp(-gate))
        silu = gate * sig
        hidden = (silu * lift).astype(BF)
        back_gate = (back * lift * sig * (1.0 + gate * (1.0 - sig))).astype(BF)
        back_lift = (back * silu).astype(BF)
        hidden_ref[at, :] = hidden
        backs_ref[at, :unit] = back_gate
        backs_ref[at, unit:] = back_lift
        mix = dot(back_gate, gate_ref[...], 1, 1) + dot(back_lift, up_ref[...], 1, 1)
        mix_ref[...] = mix.astype(mix_ref.dtype)
        part_ref[...] = dot(hidden, down_ref[...], 1, 1).astype(part_ref.dtype)


def feed_forward(core, mixed, back, large, unit, name):
    rows, wide = mixed[0].shape
    whole = pl.BlockSpec((rows, wide), lambda i, core: (0, 0))
    w_specs = [
        pl.BlockSpec((wide, unit), lambda i, core, k=k: (0, 2 * k + core[0])) for k in range(3)
    ]
    kinds = (F32, BF, F32, BF)
    return pl.pallas_call(
        lambda core, *refs: feed_kernel(*refs),
        grid_spec=pltpu.PrefetchScalarGridSpec(
            num_scalar_prefetch=1,
            grid=(1,),
            in_specs=[whole] * 4 + w_specs,
            out_specs=[
                pl.BlockSpec((2 * rows, unit), lambda i, core: (0, 0)),
                pl.BlockSpec((2 * rows, 2 * unit), lambda i, core: (0, 0)),
                *[whole] * 4,
            ],
        ),
        out_shape=[
            like((2 * rows, unit), BF),
            like((2 * rows, 2 * unit), BF),
            *[like((rows, wide), kind) for kind in kinds],
        ],
        cost_estimate=COST,
        compiler_params=params(40),
        name=name,
    )(core, *mixed, *back, large, large, large)


def grads_kernel(y_ref, m0, m1, m2, m3, b0, b1, b2, b3, u0, u1, h0, h1, keep_ref, send_ref):
    rows, unit, half = m0.shape[0], h0.shape[1], keep_ref.shape[1]
    first = y_ref[0] == 0

    def put(at, parts, u0, u1):
        acc = dot(parts[0][...], u0[:rows, :], 0, 0) + dot(parts[1][...], u0[rows:, :], 0, 0)
        acc = acc + dot(parts[2][...], u1[:rows, :], 0, 0) + dot(parts[3][...], u1[rows:, :], 0, 0)
        for z in range(keep_ref.shape[0]):
            low, high = acc[2 * z * half : (2 * z + 1) * half], acc[(2 * z + 1) * half : 2 * (z + 1) * half]
            keep_ref[z, :, at] = jnp.where(first, low, high).astype(BF)
            send_ref[z, :, at] = jnp.where(first, high, low).astype(BF)

    put(slice(0, 2 * unit), (m0, m1, m2, m3), u0, u1)
    put(slice(2 * unit, 3 * unit), (b0, b1, b2, b3), h0, h1)


def feed_grads(y, mixed, back, backs, hidden, line):
    rows, wide = mixed[0].shape
    steps = min(line, wide // 128)
    block, unit = wide // steps, hidden[0].shape[1]
    return pl.pallas_call(
        grads_kernel,
        grid=(steps,),
        in_specs=[SMEM]
        + [pl.BlockSpec((rows, block), lambda z: (0, z))] * 8
        + [pl.BlockSpec((2 * rows, 2 * unit), lambda z: (0, 0))] * 2
        + [pl.BlockSpec((2 * rows, unit), lambda z: (0, 0))] * 2,
        out_specs=[pl.BlockSpec((line // steps, wide // line // 2, 3 * unit), lambda z: (z, 0, 0))] * 2,
        out_shape=[like((line, wide // line // 2, 3 * unit), BF)] * 2,
        cost_estimate=COST,
        compiler_params=params(24),
        name="feed_grads",
    )(y, *mixed, *back, *backs, *hidden)


def after_feed_kernel(
    model, kv_heads, place, mix_ref, core_ref, far_ref, unit_ref, inv_ref, gain_ref, back_ref, w_ref,
    far_w_ref, order_ref, attended_ref, middle_ref, do_ref, dot_ref, gains_ref, split_ref,
):
    unit = unit_ref[...]
    mixed = mix_ref[...] + core_ref[...].astype(F32) + far_ref[...].astype(F32)
    gains_ref[...] = jnp.sum(mixed * unit, axis=0, keepdims=True)
    scaled = mixed * gain_ref[...]
    mean = jnp.sum(scaled * unit, axis=1, keepdims=True) / model
    middle = back_ref[...] + inv_ref[...] * (scaled - unit * mean)
    middle_ref[...] = middle
    low = middle.astype(BF)
    part = do_ref.shape[0] // 2
    near, far = pair_rows(place[2], part)
    do_ref[near, :] = dot(w_ref[:, :part], low, 0, 1).astype(BF)
    do_ref[far, :] = dot(far_w_ref[:, :part], low, 0, 1).astype(BF)
    group = do_ref.shape[0] // HEAD // kv_heads
    dot_ref[...] = jnp.zeros_like(dot_ref)
    for h in range(kv_heads * group):
        at = slice(h * HEAD, (h + 1) * HEAD)
        product = do_ref[at, :].astype(F32) * attended_ref[at, :].astype(F32)
        dot_ref[h // group, h % group : h % group + 1, :] = jnp.sum(product, axis=0, keepdims=True)
    split_ref[...] = dot(order_ref[...], low, 1, 1).astype(BF)


def after_feed(place, mix, core, far, unit, inv, gain, back, w_out, order, attended, kv_heads, model):
    rows, wide = unit.shape
    width = attended.shape[0]

    shapes = [
        like((rows, wide), F32),
        like((width, rows), BF),
        like((kv_heads, 8, rows), F32),
        like((1, wide), F32),
        like((wide, rows), BF),
    ]
    return pl.pallas_call(
        functools.partial(after_feed_kernel, model, kv_heads),
        in_specs=[SMEM] + [VMEM] * 11,
        out_specs=[VMEM] * 5,
        out_shape=shapes,
        cost_estimate=COST,
        compiler_params=params(),
        name="after_feed",
    )(place, mix, core, far, unit, inv, gain, back, *w_out, order, attended)


def backs_kernel(q_part, k_part, dq_ref, far_ref, dkv_ref, chain_ref, cos_ref, sin_ref, out_ref):
    sides = out_ref.shape[0]
    cos, sin = cos_ref[...], sin_ref[...]

    def put(part, base, index, value):
        x, at = divmod(index * HALF_HEAD, part)
        out_ref[x, base + at : base + at + HALF_HEAD, :] = value.astype(BF)

    def turn(part, base, h, value):
        low, high = value[:HALF_HEAD], value[HALF_HEAD:]
        put(part, base, 2 * h, low * cos + high * sin)
        put(part, base, 2 * h + 1, high * cos - low * sin)

    for h in range(sides * q_part // HEAD):
        at = slice(h * HEAD, (h + 1) * HEAD)
        turn(q_part, 0, h, dq_ref[at, :] + far_ref[at, :].astype(F32))
    for h in range(sides * k_part // HEAD):
        at = slice(h * HEAD, (h + 1) * HEAD)
        turn(k_part, q_part, h, dkv_ref[0, at, :] + chain_ref[0, at, :].astype(F32))
    for x in range(sides):
        at = slice(x * k_part, (x + 1) * k_part)
        value = dkv_ref[1, at, :] + chain_ref[1, at, :].astype(F32)
        out_ref[x, q_part + k_part :, :] = value.astype(BF)


def finish_backs(dq, far, dkv, chain, cos, sin, sides, q_part, k_part):
    return pl.pallas_call(
        functools.partial(backs_kernel, q_part, k_part),
        in_specs=[VMEM] * 6,
        out_specs=VMEM,
        out_shape=like((sides, q_part + 2 * k_part, far.shape[1]), BF),
        cost_estimate=COST,
        compiler_params=params(12),
        name="finish_backs",
    )(dq, far, dkv, chain, cos, sin)


def terms_kernel(
    slot, shard, place, n0, n1, p0, p1, d0, d1, o0, o1, l_ref, r_ref, gain_ref, gain2_ref,
    left_keep, left_send, right_keep, right_send, full_ref,
):
    sides, qkv, _ = d0.shape
    half = n0.shape[0]
    ys, cut = l_ref.shape[1], l_ref.shape[3]
    block = half // ys
    spare = lax.broadcasted_iota(jnp.int32, (half, 1), 0) % slot == shard
    first = jnp.zeros((half, 128), F32)
    for x in range(sides - 1, -1, -1):
        acc = dot(n0[...], d0[x], 1, 1) + dot(n1[...], d1[x], 1, 1)
        weights = jnp.concatenate(
            [jnp.concatenate([l_ref[x, y], r_ref[y, x]], axis=1) for y in range(ys)], axis=0
        )
        product = acc * weights[:, :qkv].astype(F32)
        for k in range(0, qkv // 128):
            first = first + product[:, k * 128 : (k + 1) * 128]
        rest = qkv % 128
        if rest:
            tail = product[:, qkv - rest :]
            first = first + jnp.concatenate([tail, jnp.zeros((half, 128 - rest), F32)], axis=1)
        width = left_keep.shape[2] - qkv
        at = slice(x * width, (x + 1) * width)
        other = dot(p0[...], o0[at, :], 1, 1) + dot(p1[...], o1[at, :], 1, 1)
        both = jnp.concatenate([acc, other], axis=1)
        if x == 0:
            gain = jnp.sum(first.T, axis=0, keepdims=True)
            scale = gain_ref[...]
            gain = jnp.where(scale > 0, gain / jnp.maximum(scale, 0.25), 0.0)
        else:
            gain = gain2_ref[...]
        reach = gain.shape[1]
        full_ref[:, :reach] = jnp.where(spare, gain, both[:, :reach]).astype(BF)
        full_ref[:, reach:] = both[:, reach:].astype(BF)
        part = block // 2
        for y in range(ys):
            top = slice(y * block, y * block + part)
            pl.when(place[2] == x)(lambda: left_keep.__setitem__(y, full_ref[top, :]))
            pl.when(place[2] != x)(lambda: left_send.__setitem__(y, full_ref[top, :]))
            low = slice(y * block + part, (y + 1) * block)
            pl.when(place[1] == y)(lambda: right_keep.__setitem__(x, full_ref[low, :]))
            pl.when(place[1] != y)(lambda: right_send.__setitem__(x, full_ref[low, :]))


def small_terms(place, normed, proj, backs, attended, mine, gain, gain2, slot, shard):
    sides, qkv, _ = backs[0].shape
    columns = qkv + attended[0].shape[0] // sides
    half = normed[0].shape[0]
    arrays = (*normed, *proj, *backs, *attended, *mine, gain, gain2)
    outs = [like((2, half // 4, columns), BF)] * 4
    return pl.pallas_call(
        functools.partial(terms_kernel, slot, shard),
        grid=(1,),
        in_specs=[SMEM] + [full(a) for a in arrays],
        out_specs=[full(o) for o in outs],
        out_shape=outs,
        scratch_shapes=[pltpu.VMEM((half, columns), BF)],
        cost_estimate=COST,
        compiler_params=params(57),
        name="small_terms",
    )(place, *arrays)


def second_kernel(which, place, keep_ref, far_ref, out_ref, send_ref):
    total = (keep_ref[...].astype(F32) + far_ref[...].astype(F32)).astype(BF)
    first = place[which] == 0
    out_ref[...] = jnp.where(first, total[0], total[1])
    send_ref[...] = jnp.where(first, total[1], total[0])


def second_fold(place, which, keep, far):
    return pl.pallas_call(
        functools.partial(second_kernel, which),
        in_specs=[SMEM, VMEM, VMEM],
        out_specs=[VMEM] * 2,
        out_shape=[like(keep.shape[1:], BF)] * 2,
        cost_estimate=COST,
        compiler_params=params(12),
        name="second_fold",
    )(place, keep, far)


def join_kernel(a0, a1, b0, b1, out_ref):
    out_ref[0] = (a0[...].astype(F32) + a1[...].astype(F32)).astype(BF)
    out_ref[1] = (b0[...].astype(F32) + b1[...].astype(F32)).astype(BF)


def join(left, right):
    return pl.pallas_call(
        join_kernel,
        in_specs=[VMEM] * 4,
        out_specs=VMEM,
        out_shape=like((2, *left[0].shape), BF),
        cost_estimate=COST,
        compiler_params=params(12),
        name="join",
    )(*left, *right)


def small_sums_kernel(shard, slot, q_part, k_part, at_ref, in_ref, q_ref, k_ref, v_ref, o_ref, gain_ref):
    total = in_ref[0].astype(F32)
    for i in range(1, in_ref.shape[0]):
        total = total + in_ref[i].astype(F32)
    q_ref[...] = total[:shard, :q_part]
    k_ref[...] = total[:shard, q_part : q_part + k_part]
    v_ref[...] = total[:shard, q_part + k_part : q_part + 2 * k_part]
    o_ref[...] = total[:shard, q_part + 2 * k_part :]
    gain = jnp.zeros((1, shard), F32)
    for block in range(total.shape[1] // slot):
        part = total[shard : shard + 1, block * slot : block * slot + shard]
        gain = jnp.where(at_ref[0] == block, part, gain)
    gain_ref[...] = gain


def small_sums(at, parts, shard, q_part, k_part):
    slot = parts.shape[1]
    return pl.pallas_call(
        functools.partial(small_sums_kernel, shard, slot, q_part, k_part),
        in_specs=[SMEM, VMEM],
        out_specs=[VMEM] * 5,
        out_shape=[like((shard, n), F32) for n in (q_part, k_part, k_part, q_part)]
        + [like((1, shard), F32)],
        cost_estimate=COST,
        compiler_params=params(12),
        name="small_sums",
    )(at, parts)


def add_wide(a, b):
    return pl.pallas_call(
        add_kernel,
        grid=(1,),
        in_specs=[full(a), full(b)],
        out_specs=full(a),
        out_shape=pltpu.HBM(a.shape, BF),
        cost_estimate=COST,
        compiler_params=params(24),
        name="add_wide",
    )(a, b)


def sum_blocks_kernel(place, *refs):
    *parts, keep_ref, send_ref = refs
    half = keep_ref.shape[0]
    total = parts[0][...].astype(F32)
    for part in parts[1:]:
        total = total + part[...].astype(F32)
    total = total.astype(BF)
    first = place[3] == 0
    keep_ref[...] = jnp.where(first, total[:half], total[half:])
    send_ref[...] = jnp.where(first, total[half:], total[:half])


def sum_blocks(place, parts):
    outs = [like((parts[0].shape[0] // 2, parts[0].shape[1]), BF)] * 2
    return pl.pallas_call(
        sum_blocks_kernel,
        grid=(1,),
        in_specs=[SMEM] + [full(p) for p in parts],
        out_specs=[full(o) for o in outs],
        out_shape=outs,
        cost_estimate=COST,
        compiler_params=params(16),
        name="sum_blocks",
    )(place, *parts)


def large_sums_kernel(shard, place, own_ref, far_ref, *refs):
    unit = refs[0].shape[1] // 2
    first = place[3] == 0
    own, far = own_ref[...].astype(F32)[:shard], far_ref[...].astype(F32)[:shard]
    low, high = jnp.where(first, own, far), jnp.where(first, far, own)
    for k, ref in enumerate(refs):
        ref[:, :unit] = low[:, k * unit : (k + 1) * unit]
        ref[:, unit:] = high[:, k * unit : (k + 1) * unit]


def large_sums(place, own, far, shard):
    unit = own.shape[1] // 3
    return pl.pallas_call(
        functools.partial(large_sums_kernel, shard),
        in_specs=[SMEM, VMEM, VMEM],
        out_specs=[VMEM] * 3,
        out_shape=[like((shard, 2 * unit), F32)] * 3,
        cost_estimate=COST,
        compiler_params=params(16),
        name="large_sums",
    )(place, own, far)


def exact_dot(one_hot, wide, ca, cb):
    high = wide.astype(BF)
    low = (wide - high.astype(F32)).astype(BF)
    return dot(one_hot, high, ca, cb) + dot(one_hot, low, ca, cb)


def input_kernel(
    model, d_ref, lm, rm, lt, rt, unit_ref, inv_ref, gain_ref, middle_ref, spread_ref, split_ref,
    out_ref, m_ref,
):
    sides, ys, block, cut = lm.shape
    qkv = d_ref.shape[1]
    half = ys * block
    for side, (l, r) in enumerate(((lm, rm), (lt, rt))):
        for y in range(ys):
            at = slice(side * half + y * block, side * half + (y + 1) * block)
            total = None
            for x in range(sides):
                a = dot(l[x, y], d_ref[x, :cut, :], 1, 0)
                a = a + dot(r[y, x][:, : qkv - cut], d_ref[x, cut:, :], 1, 0)
                total = a if total is None else total + a
            m_ref[at, :] = total * gain_ref[at, :]
    unit = unit_ref[...]
    scaled = m_ref[...]
    mean = jnp.sum(scaled * unit, axis=0, keepdims=True) / model
    back = inv_ref[...] * (scaled - unit * mean)
    grad = exact_dot(spread_ref[...], middle_ref[...], 1, 1) + exact_dot(split_ref[...], back, 1, 0)
    part = grad.shape[1] // 2
    out_ref[0] = grad[:, :part]
    out_ref[1] = grad[:, part:]


def input_gradient(backs, mine, theirs, unit, inv, gain, middle, spread, split, model):
    out = like((2, model, middle.shape[0] // 2), F32)
    arrays = (backs, *mine, *theirs, unit, inv, gain, middle, spread, split)
    return pl.pallas_call(
        functools.partial(input_kernel, model),
        grid=(1,),
        in_specs=[full(a) for a in arrays],
        out_specs=full(out),
        out_shape=out,
        scratch_shapes=[pltpu.VMEM(unit.shape, F32)],
        cost_estimate=COST,
        compiler_params=params(40),
        name="input_gradient",
    )(*arrays)


def output_kernel(middle_ref, own_ref, core_ref, far_ref, spread_ref, out_ref):
    result = middle_ref[...] + own_ref[...] + core_ref[...].astype(F32) + far_ref[...].astype(F32)
    out = dot(spread_ref[...], result.astype(BF), 1, 1).astype(BF)
    part = out.shape[1] // 2
    out_ref[0] = out[:, :part]
    out_ref[1] = out[:, part:]


def layer_output(middle, own, core, far, spread):
    return pl.pallas_call(
        output_kernel,
        in_specs=[VMEM] * 5,
        out_specs=VMEM,
        out_shape=like((2, spread.shape[0], middle.shape[0] // 2), BF),
        cost_estimate=COST,
        compiler_params=params(),
        name="layer_output",
    )(middle, own, core, far, spread)


def padded(count):
    return -(-count // 8) * 8


def pick(pair, index):
    return jnp.where(index == 0, pair[0], pair[1])


def ordered(mine, theirs, index, axis):
    return jnp.concatenate([pick((mine, theirs), index), pick((theirs, mine), index)], axis=axis)


def swap(array, name):
    return lax.ppermute(array, name, SWAP)


def after(value, *earlier):
    return lax.optimization_barrier((value, *earlier))[0]


def spread_matrix(model, shard, slot, ctx):
    row = lax.broadcasted_iota(jnp.int32, (model, slot * ctx), 0)
    col = lax.broadcasted_iota(jnp.int32, (model, slot * ctx), 1)
    return (col == row // shard * slot + row % shard).astype(BF)


def core_order(slot, line, c):
    wide = slot * line * 4
    row = lax.broadcasted_iota(jnp.int32, (wide, wide), 1)
    col = lax.broadcasted_iota(jnp.int32, (wide, wide), 0)
    block, place = row // slot, row % slot
    core, y, z = block % 2, block // 2 % 2, block // 4
    other = (core != c).astype(jnp.int32)
    return (col == ((other * 2 + y) * line + z) * slot + place).astype(BF)


def gather_small(rows_here, cut, meanwhile):
    line = lax.axis_size("zh") * lax.axis_size("zl")
    d, y = lax.axis_index("dp"), lax.axis_index("y")
    z_all = lax.all_to_all(
        jnp.broadcast_to(rows_here[None], (line, *rows_here.shape)),
        ("zh", "zl"),
        split_axis=0,
        concat_axis=0,
    )
    z_all = after(z_all, *meanwhile).reshape(1, -1, rows_here.shape[1])
    left, right = z_all[..., :cut], z_all[..., cut:]
    left, right = ordered(left, swap(left, "y"), y, 0), ordered(right, swap(right, "dp"), d, 0)
    left, right = left[None], right[None]
    return ordered(left, swap(left, "dp"), d, 0), ordered(right, swap(right, "y"), y, 0)


def body(
    inputs,
    query_weight,
    key_weight,
    value_matrix,
    out_weight,
    gate_weight,
    up_weight,
    down_weight,
    norm_gains,
    cotangent,
):
    seqs, part_rows, model = inputs.shape
    dps, high, low = (lax.axis_size(a) for a in ("dp", "zh", "zl"))
    line = high * low
    ctx = line * 4
    y, c, d = (lax.axis_index(a) for a in ("y", "c", "dp"))
    z = lax.axis_index("zh") * low + lax.axis_index("zl")
    shard = model // ctx
    slot = padded(shard + 1)
    wide = slot * ctx
    half = wide // 2
    rows = 2 * part_rows
    up_line = [(i, i + 1) for i in range(line - 1)]
    down_line = [(i + 1, i) for i in range(line - 1)]
    z_axes = ("zh", "zl")
    everywhere = ("zh", "zl", "y", "c")
    place = jnp.stack([z, y, d, c]).astype(jnp.int32)

    q_part, k_part = query_weight.shape[1], key_weight.shape[1]
    qkv_part = q_part + 2 * k_part
    half_ff = gate_weight.shape[1]
    unit = half_ff // 2
    kv_heads = k_part * dps // HEAD

    small = jnp.concatenate([query_weight, key_weight, value_matrix], axis=1)
    small_columns = -(-qkv_part // 128) * 128
    small = jnp.concatenate(
        [
            jnp.pad(small, ((0, 0), (0, small_columns - qkv_part))),
            jnp.pad(norm_gains, ((0, slot - shard - 1), (0, small_columns - shard))),
        ],
        axis=0,
    )
    large = jnp.concatenate([gate_weight, up_weight, down_weight.T, out_weight.T], axis=1)
    large = jnp.pad(large, ((0, slot - shard), (0, -large.shape[1] % 128)))
    large = lax.all_gather(large, everywhere, axis=0, tiled=True)

    both = jnp.stack([inputs, cotangent], axis=1)
    mine, theirs = pick((both[0], both[1]), c), pick((both[1], both[0]), c)
    both = ordered(mine, swap(theirs, "c"), c, 1)
    spread = spread_matrix(model, shard, slot, ctx)
    by_core = core_order(slot, line, c)
    spread, by_core = after(spread, small), after(by_core, small)
    spread_split = dot(spread, by_core, 1, 1).astype(BF)
    tokens = dot(both[0], spread, 1, 0)
    tokens_t = dot(spread_split, both[0], 0, 1)
    back_out = dot(both[1], spread, 1, 0)
    back_low = back_out.astype(BF)
    inv_first = lax.rsqrt(jnp.sum(tokens_t * tokens_t, axis=0, keepdims=True) / model + EPSILON)
    unit_first = tokens_t * inv_first
    positions = (2 * z + y) * rows + jnp.arange(rows, dtype=jnp.int32)
    cos, sin = rope_tables(positions, HALF_HEAD)

    w_mine = gather_small(small, small_columns // 256 * 128, (unit_first, tokens, back_low))
    w_theirs = tuple(swap(w, "c") for w in w_mine)

    def gains_of(w):
        part = w[0].reshape(dps, 2, line, slot, -1)[:, :, :, shard, :shard]
        return jnp.pad(part, ((0, 0), (0, 0), (0, 0), (0, slot - shard))).astype(F32)

    gains_mine, gains_theirs = gains_of(w_mine), gains_of(w_theirs)
    gain_second = ordered(gains_mine[1, :, :, None], gains_theirs[1, :, :, None], c, 2)
    gain_second = gain_second.transpose(1, 0, 2, 3).reshape(1, wide)
    gain_first = jnp.concatenate([gains_mine[0], gains_theirs[0]], axis=0).reshape(wide, 1)
    gains_mine = gains_mine[0].reshape(1, half)
    gain_first, gain_second, gains_mine = lax.optimization_barrier(
        (gain_first, gain_second, gains_mine)
    )

    normed = (unit_first * gain_first).astype(BF)
    q, kv = project(normed, cos, sin, w_mine, w_theirs, q_part, k_part)

    kvs = [kv]
    back_core, back_far = swap(after(back_low, kv), "c"), swap(after(back_low, kv), "dp")
    q_both = (q, swap(q, "y"))
    state = ()
    for step in range(line - 1):
        here, far_q = kvs[-1], q_both[1]
        if step > 1:
            here, state = lax.optimization_barrier((here, state))
        kvs.append(lax.ppermute(here, z_axes, up_line))
        if step > 0:
            far_q = after(far_q, here)
            state = attend_forward(place, step - 1, False, q, far_q, kvs[step - 1], state, kv_heads)
        if step == 1:
            large, state = lax.optimization_barrier((large, state))
            out_own = last_columns(large, -(-q_part // 128) * 128)
            w_out = (out_own, swap(out_own, "dp"))
    far_q = after(q_both[1], kvs[-2])
    state = attend_forward(place, line - 2, False, q, far_q, kvs[line - 2], state, kv_heads)
    stats, acc, far_stats, far_acc = attend_forward(
        place, line - 1, True, *q_both, kvs[line - 1], state, kv_heads
    )
    got = lax.ppermute(jnp.stack([far_stats, stats]), "y", SWAP)
    attended, lse, far_lse, middle, unit_second, inv_second, mixed_own = to_middle(
        place, (stats, far_stats), (got[0], got[1]), acc, swap(far_acc, "y"), w_out, tokens, gain_second,
        kv_heads, model,
    )

    mixed_core, mixed_far = swap(mixed_own, "c"), swap(mixed_own, "dp")
    core = c.astype(jnp.int32)[None]
    hidden_near, backs_near, part_own, part_core, mix_own, mix_core = feed_forward(
        core, (mixed_own, mixed_core), (back_low, back_core), large, unit, "feed_near"
    )
    mixed_far = after(mixed_far, mix_own)
    back_far = after(back_far, stats)
    mixed_far, back_far = (mixed_far, swap(mixed_far, "c")), (back_far, swap(back_far, "c"))
    hidden_far, backs_far, part_far, part_cross, mix_far, mix_cross = feed_forward(
        core, mixed_far, back_far, large, unit, "feed_far"
    )
    mix_core = swap(mix_core, "c")
    mix_far = add_low(mix_far, swap(mix_cross, "c"))
    hidden_near, mix_far_sum = after(hidden_near, mix_far), mix_far
    mix_far = swap(mix_far_sum, "dp")

    mixed_all, back_all = (mixed_own, mixed_core, *mixed_far), (back_low, back_core, *back_far)
    grads_keep, grads_send = feed_grads(
        y.astype(jnp.int32)[None], mixed_all, back_all, (backs_near, backs_far), (hidden_near, hidden_far), line
    )
    normed_pair = (normed[:half], swap(normed[half:], "c"))
    attended_pair = (attended, swap(attended, "c"))
    part_far = add_low(part_far, swap(part_cross, "c"))
    part_core = swap(part_core, "c")
    mix_far = after(mix_far, grads_keep, normed_pair[1], attended_pair[1], part_far, part_core)

    back_middle, do, row_dot, gain_terms, proj = after_feed(
        place, mix_own, mix_core, mix_far, unit_second, inv_second, gain_second, back_out, w_out, by_core,
        attended, kv_heads, model,
    )
    proj_pair = (proj[:half], swap(proj[half:], "c"))
    gain_terms = gain_terms + swap(gain_terms, "c")
    do_far, dot_far = swap(do, "y"), swap(row_dot, "y")
    do_far = after(do_far, proj_pair[1], gain_terms)
    do_both, dot_both, lse_both = (do, do_far), (row_dot, dot_far), (lse, far_lse)

    grads_far = swap(after(grads_send, do_far, dot_far), "y")
    part_far = swap(after(part_far, do_far), "dp")
    chain, dq = None, ()
    for step in range(line - 1, 0, -1):
        keys_here = kvs[step]
        if step == 1:
            keys_here = after(keys_here, part_far, part_core)
        if step < line - 2:
            keys_here, chain = lax.optimization_barrier((keys_here, chain))
        *dq, total = attend_backward(
            place, step, q_both, do_both, lse_both, dot_both, keys_here, dq, kv_heads
        )
        if chain is not None:
            total = add_low(total, lax.ppermute(chain, z_axes, down_line))
        chain = total
    dq, dq_send, dkv = attend_backward(
        place, 0, q_both, do_both, lse_both, dot_both, after(kvs[0], chain), dq, kv_heads
    )
    dq_far = swap(dq_send, "y")
    chain = lax.ppermute(after(chain, dq_send), z_axes, down_line)
    grads = add_wide(grads_keep, after(grads_far, dq)).reshape(line * 2 * slot, -1)
    grads = lax.psum_scatter(grads, z_axes, scatter_dimension=0, tiled=True)
    backs = finish_backs(dq, dq_far, dkv, chain, cos, sin, dps, q_part, k_part)

    left_keep, left_send, right_keep, right_send = small_terms(
        place, normed_pair, proj_pair, (backs, swap(backs, "c")), attended_pair, w_mine, gains_mine,
        gain_terms, slot, shard,
    )
    left_far, right_far = swap(left_send, "dp"), swap(right_send, "y")
    (
        backs, part_far, part_core, part_own, middle, back_middle, unit_first, spread, spread_split,
        *weights, _,
    ) = lax.optimization_barrier(
        (
            backs, part_far, part_core, part_own, middle, back_middle, unit_first, spread,
            spread_split, *w_mine, *w_theirs, left_keep,
        )
    )
    input_grad = input_gradient(
        backs, weights[:2], weights[2:], unit_first, inv_first, gain_first, back_middle, spread,
        spread_split, model,
    )
    layer_out = layer_output(middle, part_own, part_core, part_far, spread)
    left_far = after(left_far, input_grad, layer_out)
    left_keep, left_send = second_fold(place, 1, left_keep, left_far)
    right_keep, right_send = second_fold(place, 2, right_keep, right_far)
    terms = join((left_keep, swap(left_send, "y")), (right_keep, swap(right_send, "dp")))
    grads_keep, grads_send = sum_blocks(place, (grads,))
    gate_grad, up_grad, down_grad = large_sums(place, grads_keep, swap(grads_send, "c"), shard)
    terms = lax.all_to_all(
        terms.reshape(line, slot, -1), z_axes, split_axis=0, concat_axis=0
    )
    place_of_gains = jnp.where(d == 0, y * line + z, (z * 2 + y) * 2 + c).astype(jnp.int32)[None]
    terms = after(terms, gate_grad)
    query_grad, key_grad, value_grad, out_grad, gains_grad = small_sums(
        place_of_gains, terms, shard, q_part, k_part
    )

    def give_back(array):
        keep, send = pick((array[0], array[1]), c), pick((array[1], array[0]), c)
        return ordered(keep[None], swap(send, "c")[None], c, 0)

    return (
        give_back(layer_out).transpose(0, 2, 1),
        give_back(input_grad).transpose(0, 2, 1),
        query_grad,
        key_grad,
        value_grad,
        out_grad.T,
        gate_grad,
        up_grad,
        down_grad.T,
        gains_grad,
    )


def solution(mesh):
    devices = mesh.devices
    dps, ctx = devices.shape
    inner = Mesh(devices.reshape(dps, 2, ctx // 8, 2, 2), ("dp", "zh", "zl", "y", "c"))
    along = ("zh", "zl", "y", "c")
    rows, by_row, by_col = P("dp", along, None), P(along, "dp"), P("dp", along)
    return jax.shard_map(
        body,
        mesh=inner,
        in_specs=(rows, by_row, by_row, by_row, by_col, by_row, by_row, by_col, by_col, rows),
        out_specs=(rows, rows, by_row, by_row, by_row, by_col, by_row, by_row, by_col, by_col),
        check_vma=False,
    )
```

```python
import functools
import math

import jax
import jax.numpy as jnp
from jax import lax
from jax.experimental import pallas as pl
from jax.experimental.pallas import tpu as pltpu
from jax.sharding import Mesh, PartitionSpec as P

HEAD = 64
HALF_HEAD = HEAD // 2
EPSILON = 1e-05
MASKED = -1e30
FLOOR = -1e20
LOG2E = 1.4426950408889634
SCALE = 0.125 * LOG2E
BF = jnp.bfloat16
F32 = jnp.float32
SWAP = [(0, 1), (1, 0)]
COST = pl.CostEstimate(flops=1000, bytes_accessed=1000, transcendentals=0)
VMEM = pl.BlockSpec(memory_space=pltpu.VMEM)
SMEM = pl.BlockSpec(memory_space=pltpu.SMEM)


def params(mib=32):
    return pltpu.CompilerParams(vmem_limit_bytes=mib * 2**20)


def dot(a, b, ca, cb):
    return lax.dot_general(a, b, (((ca,), (cb,)), ((), ())), preferred_element_type=F32)


def full(array):
    return pl.BlockSpec(array.shape, lambda i: (0,) * len(array.shape))


def like(shape, kind):
    return jax.ShapeDtypeStruct(shape, kind)


def rope_tables(positions, half):
    spectrum = jnp.exp(jnp.arange(half, dtype=F32) * (-math.log(100000.0) / half))
    angles = spectrum[:, None] * positions.astype(F32)[None, :]
    return jnp.cos(angles), jnp.sin(angles)


def project_kernel(
    q_part, k_part, cut, normed_ref, cos_ref, sin_ref, lm, rm, lt, rt, q_ref, kv_ref, raw_ref
):
    sides, ys, block, _ = lm.shape
    half = ys * block
    for x in range(sides):
        left = right = None
        for side, (l, r) in enumerate(((lm, rm), (lt, rt))):
            for y in range(ys):
                at = side * half + y * block
                rows = normed_ref[at : at + block, :]
                a, b = dot(l[x, y], rows, 0, 0), dot(r[y, x], rows, 0, 0)
                left = a if left is None else left + a
                right = b if right is None else right + b
        raw_ref[x, :cut, :] = left
        raw_ref[x, cut:, :] = right
    cos, sin = cos_ref[...], sin_ref[...]

    def half_rows(part, base, index):
        x, at = divmod(index * HALF_HEAD, part)
        return raw_ref[x, base + at : base + at + HALF_HEAD, :]

    def turn(part, base, out_ref, heads):
        for h in range(heads):
            low, high = half_rows(part, base, 2 * h), half_rows(part, base, 2 * h + 1)
            out_ref[h * HEAD : h * HEAD + HALF_HEAD, :] = (low * cos - high * sin).astype(BF)
            out_ref[h * HEAD + HALF_HEAD : (h + 1) * HEAD, :] = (high * cos + low * sin).astype(BF)

    turn(q_part, 0, q_ref, sides * q_part // HEAD)
    turn(k_part, q_part, kv_ref, sides * k_part // HEAD)
    for x in range(sides):
        base = sides * k_part + x * k_part
        kv_ref[base : base + k_part, :] = raw_ref[
            x, q_part + k_part : q_part + 2 * k_part, :
        ].astype(BF)


def project(normed, cos, sin, mine, theirs, q_part, k_part):
    sides, _, _, cut = mine[0].shape
    rows = normed.shape[1]
    return pl.pallas_call(
        functools.partial(project_kernel, q_part, k_part, cut),
        in_specs=[VMEM] * 7,
        out_specs=[VMEM] * 2,
        out_shape=[like((sides * q_part, rows), BF), like((2 * sides * k_part, rows), BF)],
        scratch_shapes=[pltpu.VMEM((sides, cut + mine[1].shape[3], rows), F32)],
        cost_estimate=COST,
        compiler_params=params(),
        name="project",
    )(normed, cos, sin, *mine, *theirs)


def abreast(group, own, far, at):
    parts = []
    for h in range(group):
        parts.append(own[at(h)])
        if far is not None:
            parts.append(far[at(h)])
    return jnp.concatenate(parts, axis=1) if len(parts) > 1 else parts[0]


def head_rows(h):
    return (slice(h * HEAD, (h + 1) * HEAD), slice(None))


def stat_row(h):
    return (0, slice(h, h + 1), slice(None))


def causal(keys, rows, group, both):
    key_pos = lax.broadcasted_iota(jnp.int32, (keys, rows), 0)
    own = lax.broadcasted_iota(jnp.int32, (keys, rows), 1) >= key_pos
    parts = [own, jnp.ones_like(own)] if both else [own]
    return jnp.concatenate(parts * group, axis=1)


def forward_kernel(step, last, group, place, q_ref, far_q_ref, k_ref, v_ref, *refs):
    rows = q_ref.shape[1]
    stat_ref, acc_ref, far_stat_ref, far_acc_ref = refs[-4:]

    def visit(both):
        far = (lambda ref: ref) if both else (lambda ref: None)
        scores = dot(k_ref[...], abreast(group, q_ref, far(far_q_ref), head_rows), 0, 0) * SCALE
        if step == 0:
            scores = jnp.where(causal(scores.shape[0], rows, group, both), scores, MASKED)
        top = jnp.max(scores, axis=0, keepdims=True)
        if step:
            old = abreast(group, refs[0], refs[2], stat_row)
            top = jnp.maximum(top, old)
            shrink = jnp.exp2(old - top)
        probs = jnp.exp2(scores - top)
        total = jnp.sum(probs, axis=0, keepdims=True)
        if step:
            total = total + abreast(group, refs[0], refs[2], lambda h: stat_row(group + h)) * shrink
        acc = dot(v_ref[...], probs.astype(BF), 1, 0)
        sides = ((0, stat_ref, acc_ref), (1, far_stat_ref, far_acc_ref)) if both else ((0, stat_ref, acc_ref),)
        for h in range(group):
            for side, stats, out in sides:
                at = (h * len(sides) + side) * rows
                at = slice(at, at + rows)
                value = acc[:, at]
                if step:
                    value = value + refs[2 * side + 1][head_rows(h)] * shrink[:, at]
                out[head_rows(h)] = value.astype(out.dtype)
                stats[stat_row(h)] = top[:, at]
                stats[stat_row(group + h)] = total[:, at]

    if step == 0:
        pl.when(place[1] == 0)(lambda: visit(True))

        @pl.when(place[1] != 0)
        def _():
            visit(False)
            far_stat_ref[0, :group, :] = jnp.full((group, rows), FLOOR, F32)
            far_stat_ref[0, group : 2 * group, :] = jnp.zeros((group, rows), F32)
            far_acc_ref[...] = jnp.zeros_like(far_acc_ref)
    else:
        pl.when(step <= place[0])(lambda: visit(True))

        @pl.when(step > place[0])
        def _():
            for old, new in zip(refs[:4], refs[-4:]):
                new[...] = old[...].astype(new.dtype)


def attend_forward(place, step, last, q, far_q, kv, state, kv_heads):
    width, rows = q.shape
    group = width // HEAD // kv_heads
    keys = kv.shape[1]
    wide = pl.BlockSpec((group * HEAD, rows), lambda g: (g, 0))
    stat = pl.BlockSpec((1, 8, rows), lambda g: (g, 0, 0))
    first = pl.BlockSpec((HEAD, keys), lambda g: (g, 0))
    second = pl.BlockSpec((HEAD, keys), lambda g: (g + kv_heads, 0))
    stats = like((kv_heads, 8, rows), F32)
    aliases = {5: 0, 6: 1, 7: 2} if last else {5: 0, 6: 1, 7: 2, 8: 3}
    return pl.pallas_call(
        functools.partial(forward_kernel, step, last, group),
        grid=(kv_heads,),
        in_specs=[SMEM, wide, wide, first, second] + ([stat, wide] * 2 if step else []),
        out_specs=[stat, wide] * 2,
        out_shape=[stats, like((width, rows), F32), stats, like((width, rows), BF if last else F32)],
        input_output_aliases=aliases if step else {},
        cost_estimate=COST,
        compiler_params=params(12),
        name=f"attend_forward_{step}",
    )(place, q, far_q, kv, kv, *state)


def backward_kernel(
    step, group, place, q_ref, far_q_ref, do_ref, far_do_ref, lse_ref, far_lse_ref, dot_ref,
    far_dot_ref, k_ref, v_ref, *refs,
):
    dq_ref, far_dq_ref, dkv_ref = refs[-3:]
    more = len(refs) > 3
    rows = q_ref.shape[1]

    def visit(both):
        key, value = k_ref[...], v_ref[...]
        far = (lambda ref: ref) if both else (lambda ref: None)
        q = abreast(group, q_ref, far(far_q_ref), head_rows)
        do = abreast(group, do_ref, far(far_do_ref), head_rows)
        lse = abreast(group, lse_ref, far(far_lse_ref), stat_row)
        total = abreast(group, dot_ref, far(far_dot_ref), stat_row)
        probs = jnp.exp2(dot(key, q, 0, 0) * SCALE - lse)
        if step == 0:
            probs = jnp.where(causal(probs.shape[0], rows, group, both), probs, 0.0)
        back = (probs * (dot(value, do, 0, 0) - total)).astype(BF)
        dkv_ref[0] = (dot(back, q, 1, 1).T * 0.125).astype(dkv_ref.dtype)
        dkv_ref[1] = dot(probs.astype(BF), do, 1, 1).T.astype(dkv_ref.dtype)
        dq = dot(key, back, 1, 0) * 0.125
        sides = (dq_ref, far_dq_ref) if both else (dq_ref,)
        for h in range(group):
            for side, out in enumerate(sides):
                at = (h * len(sides) + side) * rows
                value = dq[:, at : at + rows]
                if more:
                    value = value + refs[side][head_rows(h)]
                out[head_rows(h)] = value.astype(out.dtype)

    if step == 0:
        pl.when(place[1] == 0)(lambda: visit(True))

        @pl.when(place[1] != 0)
        def _():
            visit(False)
            if more:
                far_dq_ref[...] = refs[1][...].astype(far_dq_ref.dtype)
            else:
                far_dq_ref[...] = jnp.zeros_like(far_dq_ref)
    else:
        pl.when(step <= place[0])(lambda: visit(True))

        @pl.when(step > place[0])
        def _():
            for i, ref in enumerate((dq_ref, far_dq_ref)):
                ref[...] = refs[i][...] if more else jnp.zeros_like(ref)
            dkv_ref[...] = jnp.zeros_like(dkv_ref)


def attend_backward(place, step, q, do, lse, row_dot, kv, dq, kv_heads):
    width, rows = q[0].shape
    group = width // HEAD // kv_heads
    keys = kv.shape[1]
    wide = pl.BlockSpec((group * HEAD, rows), lambda g: (g, 0))
    stat = pl.BlockSpec((1, 8, rows), lambda g: (g, 0, 0))
    first = pl.BlockSpec((HEAD, keys), lambda g: (g, 0))
    second = pl.BlockSpec((HEAD, keys), lambda g: (g + kv_heads, 0))
    kind = BF if step else F32
    aliases = ({11: 0, 12: 1} if step else {11: 0}) if dq else {}
    return pl.pallas_call(
        functools.partial(backward_kernel, step, group),
        grid=(kv_heads,),
        in_specs=[SMEM] + [wide] * 4 + [stat] * 4 + [first, second] + [wide] * len(dq),
        out_specs=[wide, wide, pl.BlockSpec((2, HEAD, keys), lambda g: (0, g, 0))],
        out_shape=[
            like((width, rows), F32),
            like((width, rows), F32 if step else BF),
            like((2, kv_heads * HEAD, keys), kind),
        ],
        input_output_aliases=aliases,
        cost_estimate=COST,
        compiler_params=params(12),
        name=f"attend_backward_{step}",
    )(place, *q, *do, *lse, *row_dot, kv, kv, *dq)


def add_kernel(a_ref, b_ref, out_ref):
    out_ref[...] = (a_ref[...].astype(F32) + b_ref[...].astype(F32)).astype(out_ref.dtype)


def add_low(a, b):
    return pl.pallas_call(
        add_kernel,
        in_specs=[VMEM] * 2,
        out_specs=VMEM,
        out_shape=like(a.shape, BF),
        cost_estimate=COST,
        compiler_params=params(12),
        name="add_low",
    )(a, b)


def pair_rows(side, part):
    return tuple(pl.ds(pl.multiple_of(i * part, 16), part) for i in (side, 1 - side))


def middle_kernel(
    kv_heads, model, place, stat_ref, far_stat_ref, got_ref, far_got_ref, acc_ref, far_ref, w_ref,
    far_w_ref, tokens_ref, gain_ref, attended_ref, lse_ref, far_lse_ref, middle_ref, unit_ref, inv_ref, mixed_ref,
):
    group = acc_ref.shape[0] // HEAD // kv_heads
    lse_ref[...] = jnp.zeros_like(lse_ref)
    far_lse_ref[...] = jnp.zeros_like(far_lse_ref)
    for g in range(kv_heads):
        for h in range(group):
            at = slice((g * group + h) * HEAD, (g * group + h + 1) * HEAD)
            m, s = slice(h, h + 1), slice(group + h, group + h + 1)
            top = jnp.maximum(far_stat_ref[g, m, :], far_got_ref[g, m, :])
            total = far_stat_ref[g, s, :] * jnp.exp2(far_stat_ref[g, m, :] - top)
            total = total + far_got_ref[g, s, :] * jnp.exp2(far_got_ref[g, m, :] - top)
            far_lse_ref[g, m, :] = top + jnp.log2(total)
            top = jnp.maximum(stat_ref[g, m, :], got_ref[g, m, :])
            near, far = jnp.exp2(stat_ref[g, m, :] - top), jnp.exp2(got_ref[g, m, :] - top)
            total = stat_ref[g, s, :] * near + got_ref[g, s, :] * far
            lse_ref[g, m, :] = top + jnp.log2(total)
            value = acc_ref[at, :] * (near / total) + far_ref[at, :].astype(F32) * (far / total)
            attended_ref[at, :] = value.astype(BF)
    part = attended_ref.shape[0] // 2
    near, far = pair_rows(place[2], part)
    middle = tokens_ref[...] + dot(attended_ref[near, :], w_ref[:, :part], 0, 1)
    middle = middle + dot(attended_ref[far, :], far_w_ref[:, :part], 0, 1)
    inv = lax.rsqrt(jnp.sum(middle * middle, axis=1, keepdims=True) / model + EPSILON)
    unit = middle * inv
    middle_ref[...] = middle
    unit_ref[...] = unit
    inv_ref[...] = inv
    mixed_ref[...] = (unit * gain_ref[...]).astype(BF)


def to_middle(place, stats, got, acc, far, w_out, tokens, gain, kv_heads, model):
    width, rows = far.shape
    wide = tokens.shape[1]
    shape = stats[0].shape
    return pl.pallas_call(
        functools.partial(middle_kernel, kv_heads, model),
        in_specs=[SMEM] + [VMEM] * 10,
        out_specs=[VMEM] * 7,
        out_shape=[
            like((width, rows), BF),
            like(shape, F32),
            like(shape, F32),
            like((rows, wide), F32),
            like((rows, wide), F32),
            like((rows, 1), F32),
            like((rows, wide), BF),
        ],
        cost_estimate=COST,
        compiler_params=params(16),
        name="to_middle",
    )(place, *stats, *got, acc, far, *w_out, tokens, gain)


def copy_kernel(in_ref, out_ref):
    out_ref[...] = in_ref[...]


def last_columns(array, columns):
    rows, first = array.shape[0], (array.shape[1] - columns) // 128
    return pl.pallas_call(
        copy_kernel,
        grid=(-(-columns // 128),),
        in_specs=[pl.BlockSpec((rows, 128), lambda i: (0, first + i))],
        out_specs=pl.BlockSpec((rows, 128), lambda i: (0, i)),
        out_shape=like((rows, columns), array.dtype),
        cost_estimate=COST,
        compiler_params=params(57),
        name="last_columns",
    )(array)


def feed_kernel(m0, m1, b0, b1, gate_ref, up_ref, down_ref, *refs):
    hidden_ref, backs_ref, p0, p1, x0, x1 = refs
    rows, unit = m0.shape[0], gate_ref.shape[1]
    for t, (mixed_ref, back_ref, part_ref, mix_ref) in enumerate(((m0, b0, p0, x0), (m1, b1, p1, x1))):
        at = slice(t * rows, (t + 1) * rows)
        gate = dot(mixed_ref[...], gate_ref[...], 1, 0)
        lift = dot(mixed_ref[...], up_ref[...], 1, 0)
        back = dot(back_ref[...], down_ref[...], 1, 0)
        sig = 1.0 / (1.0 + jnp.exp(-gate))
        silu = gate * sig
        hidden = (silu * lift).astype(BF)
        back_gate = (back * lift * sig * (1.0 + gate * (1.0 - sig))).astype(BF)
        back_lift = (back * silu).astype(BF)
        hidden_ref[at, :] = hidden
        backs_ref[at, :unit] = back_gate
        backs_ref[at, unit:] = back_lift
        mix = dot(back_gate, gate_ref[...], 1, 1) + dot(back_lift, up_ref[...], 1, 1)
        mix_ref[...] = mix.astype(mix_ref.dtype)
        part_ref[...] = dot(hidden, down_ref[...], 1, 1).astype(part_ref.dtype)


def feed_forward(core, mixed, back, large, unit, name):
    rows, wide = mixed[0].shape
    whole = pl.BlockSpec((rows, wide), lambda i, core: (0, 0))
    w_specs = [
        pl.BlockSpec((wide, unit), lambda i, core, k=k: (0, 2 * k + core[0])) for k in range(3)
    ]
    kinds = (F32, BF, F32, BF)
    return pl.pallas_call(
        lambda core, *refs: feed_kernel(*refs),
        grid_spec=pltpu.PrefetchScalarGridSpec(
            num_scalar_prefetch=1,
            grid=(1,),
            in_specs=[whole] * 4 + w_specs,
            out_specs=[
                pl.BlockSpec((2 * rows, unit), lambda i, core: (0, 0)),
                pl.BlockSpec((2 * rows, 2 * unit), lambda i, core: (0, 0)),
                *[whole] * 4,
            ],
        ),
        out_shape=[
            like((2 * rows, unit), BF),
            like((2 * rows, 2 * unit), BF),
            *[like((rows, wide), kind) for kind in kinds],
        ],
        cost_estimate=COST,
        compiler_params=params(40),
        name=name,
    )(core, *mixed, *back, large, large, large)


def grads_kernel(y_ref, m0, m1, m2, m3, b0, b1, b2, b3, u0, u1, h0, h1, keep_ref, send_ref):
    rows, unit, half = m0.shape[0], h0.shape[1], keep_ref.shape[1]
    first = y_ref[0] == 0

    def put(at, parts, u0, u1):
        acc = dot(parts[0][...], u0[:rows, :], 0, 0) + dot(parts[1][...], u0[rows:, :], 0, 0)
        acc = acc + dot(parts[2][...], u1[:rows, :], 0, 0) + dot(parts[3][...], u1[rows:, :], 0, 0)
        for z in range(keep_ref.shape[0]):
            low, high = acc[2 * z * half : (2 * z + 1) * half], acc[(2 * z + 1) * half : 2 * (z + 1) * half]
            keep_ref[z, :, at] = jnp.where(first, low, high).astype(BF)
            send_ref[z, :, at] = jnp.where(first, high, low).astype(BF)

    put(slice(0, 2 * unit), (m0, m1, m2, m3), u0, u1)
    put(slice(2 * unit, 3 * unit), (b0, b1, b2, b3), h0, h1)


def feed_grads(y, mixed, back, backs, hidden, line):
    rows, wide = mixed[0].shape
    steps = min(line, wide // 128)
    block, unit = wide // steps, hidden[0].shape[1]
    return pl.pallas_call(
        grads_kernel,
        grid=(steps,),
        in_specs=[SMEM]
        + [pl.BlockSpec((rows, block), lambda z: (0, z))] * 8
        + [pl.BlockSpec((2 * rows, 2 * unit), lambda z: (0, 0))] * 2
        + [pl.BlockSpec((2 * rows, unit), lambda z: (0, 0))] * 2,
        out_specs=[pl.BlockSpec((line // steps, wide // line // 2, 3 * unit), lambda z: (z, 0, 0))] * 2,
        out_shape=[like((line, wide // line // 2, 3 * unit), BF)] * 2,
        cost_estimate=COST,
        compiler_params=params(24),
        name="feed_grads",
    )(y, *mixed, *back, *backs, *hidden)


def after_feed_kernel(
    model, kv_heads, place, mix_ref, core_ref, far_ref, unit_ref, inv_ref, gain_ref, back_ref, w_ref,
    far_w_ref, order_ref, attended_ref, middle_ref, do_ref, dot_ref, gains_ref, split_ref,
):
    unit = unit_ref[...]
    mixed = mix_ref[...] + core_ref[...].astype(F32) + far_ref[...].astype(F32)
    gains_ref[...] = jnp.sum(mixed * unit, axis=0, keepdims=True)
    scaled = mixed * gain_ref[...]
    mean = jnp.sum(scaled * unit, axis=1, keepdims=True) / model
    middle = back_ref[...] + inv_ref[...] * (scaled - unit * mean)
    middle_ref[...] = middle
    low = middle.astype(BF)
    part = do_ref.shape[0] // 2
    near, far = pair_rows(place[2], part)
    do_ref[near, :] = dot(w_ref[:, :part], low, 0, 1).astype(BF)
    do_ref[far, :] = dot(far_w_ref[:, :part], low, 0, 1).astype(BF)
    group = do_ref.shape[0] // HEAD // kv_heads
    dot_ref[...] = jnp.zeros_like(dot_ref)
    for h in range(kv_heads * group):
        at = slice(h * HEAD, (h + 1) * HEAD)
        product = do_ref[at, :].astype(F32) * attended_ref[at, :].astype(F32)
        dot_ref[h // group, h % group : h % group + 1, :] = jnp.sum(product, axis=0, keepdims=True)
    split_ref[...] = dot(order_ref[...], low, 1, 1).astype(BF)


def after_feed(place, mix, core, far, unit, inv, gain, back, w_out, order, attended, kv_heads, model):
    rows, wide = unit.shape
    width = attended.shape[0]

    shapes = [
        like((rows, wide), F32),
        like((width, rows), BF),
        like((kv_heads, 8, rows), F32),
        like((1, wide), F32),
        like((wide, rows), BF),
    ]
    return pl.pallas_call(
        functools.partial(after_feed_kernel, model, kv_heads),
        in_specs=[SMEM] + [VMEM] * 11,
        out_specs=[VMEM] * 5,
        out_shape=shapes,
        cost_estimate=COST,
        compiler_params=params(),
        name="after_feed",
    )(place, mix, core, far, unit, inv, gain, back, *w_out, order, attended)


def backs_kernel(q_part, k_part, dq_ref, far_ref, dkv_ref, chain_ref, cos_ref, sin_ref, out_ref):
    sides = out_ref.shape[0]
    cos, sin = cos_ref[...], sin_ref[...]

    def put(part, base, index, value):
        x, at = divmod(index * HALF_HEAD, part)
        out_ref[x, base + at : base + at + HALF_HEAD, :] = value.astype(BF)

    def turn(part, base, h, value):
        low, high = value[:HALF_HEAD], value[HALF_HEAD:]
        put(part, base, 2 * h, low * cos + high * sin)
        put(part, base, 2 * h + 1, high * cos - low * sin)

    for h in range(sides * q_part // HEAD):
        at = slice(h * HEAD, (h + 1) * HEAD)
        turn(q_part, 0, h, dq_ref[at, :] + far_ref[at, :].astype(F32))
    for h in range(sides * k_part // HEAD):
        at = slice(h * HEAD, (h + 1) * HEAD)
        turn(k_part, q_part, h, dkv_ref[0, at, :] + chain_ref[0, at, :].astype(F32))
    for x in range(sides):
        at = slice(x * k_part, (x + 1) * k_part)
        value = dkv_ref[1, at, :] + chain_ref[1, at, :].astype(F32)
        out_ref[x, q_part + k_part :, :] = value.astype(BF)


def finish_backs(dq, far, dkv, chain, cos, sin, sides, q_part, k_part):
    return pl.pallas_call(
        functools.partial(backs_kernel, q_part, k_part),
        in_specs=[VMEM] * 6,
        out_specs=VMEM,
        out_shape=like((sides, q_part + 2 * k_part, far.shape[1]), BF),
        cost_estimate=COST,
        compiler_params=params(12),
        name="finish_backs",
    )(dq, far, dkv, chain, cos, sin)


def terms_kernel(
    slot, shard, place, n0, n1, p0, p1, d0, d1, o0, o1, l_ref, r_ref, gain_ref, gain2_ref,
    left_keep, left_send, right_keep, right_send, full_ref,
):
    sides, qkv, _ = d0.shape
    half = n0.shape[0]
    ys, cut = l_ref.shape[1], l_ref.shape[3]
    block = half // ys
    spare = lax.broadcasted_iota(jnp.int32, (half, 1), 0) % slot == shard
    first = jnp.zeros((half, 128), F32)
    for x in range(sides - 1, -1, -1):
        acc = dot(n0[...], d0[x], 1, 1) + dot(n1[...], d1[x], 1, 1)
        weights = jnp.concatenate(
            [jnp.concatenate([l_ref[x, y], r_ref[y, x]], axis=1) for y in range(ys)], axis=0
        )
        product = acc * weights[:, :qkv].astype(F32)
        for k in range(0, qkv // 128):
            first = first + product[:, k * 128 : (k + 1) * 128]
        rest = qkv % 128
        if rest:
            tail = product[:, qkv - rest :]
            first = first + jnp.concatenate([tail, jnp.zeros((half, 128 - rest), F32)], axis=1)
        width = left_keep.shape[2] - qkv
        at = slice(x * width, (x + 1) * width)
        other = dot(p0[...], o0[at, :], 1, 1) + dot(p1[...], o1[at, :], 1, 1)
        both = jnp.concatenate([acc, other], axis=1)
        if x == 0:
            gain = jnp.sum(first.T, axis=0, keepdims=True)
            scale = gain_ref[...]
            gain = jnp.where(scale > 0, gain / jnp.maximum(scale, 0.25), 0.0)
        else:
            gain = gain2_ref[...]
        reach = gain.shape[1]
        full_ref[:, :reach] = jnp.where(spare, gain, both[:, :reach]).astype(BF)
        full_ref[:, reach:] = both[:, reach:].astype(BF)
        part = block // 2
        for y in range(ys):
            top = slice(y * block, y * block + part)
            pl.when(place[2] == x)(lambda: left_keep.__setitem__(y, full_ref[top, :]))
            pl.when(place[2] != x)(lambda: left_send.__setitem__(y, full_ref[top, :]))
            low = slice(y * block + part, (y + 1) * block)
            pl.when(place[1] == y)(lambda: right_keep.__setitem__(x, full_ref[low, :]))
            pl.when(place[1] != y)(lambda: right_send.__setitem__(x, full_ref[low, :]))


def small_terms(place, normed, proj, backs, attended, mine, gain, gain2, slot, shard):
    sides, qkv, _ = backs[0].shape
    columns = qkv + attended[0].shape[0] // sides
    half = normed[0].shape[0]
    arrays = (*normed, *proj, *backs, *attended, *mine, gain, gain2)
    outs = [like((2, half // 4, columns), BF)] * 4
    return pl.pallas_call(
        functools.partial(terms_kernel, slot, shard),
        grid=(1,),
        in_specs=[SMEM] + [full(a) for a in arrays],
        out_specs=[full(o) for o in outs],
        out_shape=outs,
        scratch_shapes=[pltpu.VMEM((half, columns), BF)],
        cost_estimate=COST,
        compiler_params=params(57),
        name="small_terms",
    )(place, *arrays)


def second_kernel(which, place, keep_ref, far_ref, out_ref, send_ref):
    total = (keep_ref[...].astype(F32) + far_ref[...].astype(F32)).astype(BF)
    first = place[which] == 0
    out_ref[...] = jnp.where(first, total[0], total[1])
    send_ref[...] = jnp.where(first, total[1], total[0])


def second_fold(place, which, keep, far):
    return pl.pallas_call(
        functools.partial(second_kernel, which),
        in_specs=[SMEM, VMEM, VMEM],
        out_specs=[VMEM] * 2,
        out_shape=[like(keep.shape[1:], BF)] * 2,
        cost_estimate=COST,
        compiler_params=params(12),
        name="second_fold",
    )(place, keep, far)


def join_kernel(a0, a1, b0, b1, out_ref):
    out_ref[0] = (a0[...].astype(F32) + a1[...].astype(F32)).astype(BF)
    out_ref[1] = (b0[...].astype(F32) + b1[...].astype(F32)).astype(BF)


def join(left, right):
    return pl.pallas_call(
        join_kernel,
        in_specs=[VMEM] * 4,
        out_specs=VMEM,
        out_shape=like((2, *left[0].shape), BF),
        cost_estimate=COST,
        compiler_params=params(12),
        name="join",
    )(*left, *right)


def small_sums_kernel(shard, slot, q_part, k_part, at_ref, in_ref, q_ref, k_ref, v_ref, o_ref, gain_ref):
    total = in_ref[0].astype(F32)
    for i in range(1, in_ref.shape[0]):
        total = total + in_ref[i].astype(F32)
    q_ref[...] = total[:shard, :q_part]
    k_ref[...] = total[:shard, q_part : q_part + k_part]
    v_ref[...] = total[:shard, q_part + k_part : q_part + 2 * k_part]
    o_ref[...] = total[:shard, q_part + 2 * k_part :]
    gain = jnp.zeros((1, shard), F32)
    for block in range(total.shape[1] // slot):
        part = total[shard : shard + 1, block * slot : block * slot + shard]
        gain = jnp.where(at_ref[0] == block, part, gain)
    gain_ref[...] = gain


def small_sums(at, parts, shard, q_part, k_part):
    slot = parts.shape[1]
    return pl.pallas_call(
        functools.partial(small_sums_kernel, shard, slot, q_part, k_part),
        in_specs=[SMEM, VMEM],
        out_specs=[VMEM] * 5,
        out_shape=[like((shard, n), F32) for n in (q_part, k_part, k_part, q_part)]
        + [like((1, shard), F32)],
        cost_estimate=COST,
        compiler_params=params(12),
        name="small_sums",
    )(at, parts)


def add_wide(a, b):
    return pl.pallas_call(
        add_kernel,
        grid=(1,),
        in_specs=[full(a), full(b)],
        out_specs=full(a),
        out_shape=pltpu.HBM(a.shape, BF),
        cost_estimate=COST,
        compiler_params=params(24),
        name="add_wide",
    )(a, b)


def sum_blocks_kernel(place, *refs):
    *parts, keep_ref, send_ref = refs
    half = keep_ref.shape[0]
    total = parts[0][...].astype(F32)
    for part in parts[1:]:
        total = total + part[...].astype(F32)
    total = total.astype(BF)
    first = place[3] == 0
    keep_ref[...] = jnp.where(first, total[:half], total[half:])
    send_ref[...] = jnp.where(first, total[half:], total[:half])


def sum_blocks(place, parts):
    outs = [like((parts[0].shape[0] // 2, parts[0].shape[1]), BF)] * 2
    return pl.pallas_call(
        sum_blocks_kernel,
        grid=(1,),
        in_specs=[SMEM] + [full(p) for p in parts],
        out_specs=[full(o) for o in outs],
        out_shape=outs,
        cost_estimate=COST,
        compiler_params=params(16),
        name="sum_blocks",
    )(place, *parts)


def large_sums_kernel(shard, place, own_ref, far_ref, *refs):
    unit = refs[0].shape[1] // 2
    first = place[3] == 0
    own, far = own_ref[...].astype(F32)[:shard], far_ref[...].astype(F32)[:shard]
    low, high = jnp.where(first, own, far), jnp.where(first, far, own)
    for k, ref in enumerate(refs):
        ref[:, :unit] = low[:, k * unit : (k + 1) * unit]
        ref[:, unit:] = high[:, k * unit : (k + 1) * unit]


def large_sums(place, own, far, shard):
    unit = own.shape[1] // 3
    return pl.pallas_call(
        functools.partial(large_sums_kernel, shard),
        in_specs=[SMEM, VMEM, VMEM],
        out_specs=[VMEM] * 3,
        out_shape=[like((shard, 2 * unit), F32)] * 3,
        cost_estimate=COST,
        compiler_params=params(16),
        name="large_sums",
    )(place, own, far)


def exact_dot(one_hot, wide, ca, cb):
    high = wide.astype(BF)
    low = (wide - high.astype(F32)).astype(BF)
    return dot(one_hot, high, ca, cb) + dot(one_hot, low, ca, cb)


def input_kernel(
    model, d_ref, lm, rm, lt, rt, unit_ref, inv_ref, gain_ref, middle_ref, spread_ref, split_ref,
    out_ref, m_ref,
):
    sides, ys, block, cut = lm.shape
    qkv = d_ref.shape[1]
    half = ys * block
    for side, (l, r) in enumerate(((lm, rm), (lt, rt))):
        for y in range(ys):
            at = slice(side * half + y * block, side * half + (y + 1) * block)
            total = None
            for x in range(sides):
                a = dot(l[x, y], d_ref[x, :cut, :], 1, 0)
                a = a + dot(r[y, x][:, : qkv - cut], d_ref[x, cut:, :], 1, 0)
                total = a if total is None else total + a
            m_ref[at, :] = total * gain_ref[at, :]
    unit = unit_ref[...]
    scaled = m_ref[...]
    mean = jnp.sum(scaled * unit, axis=0, keepdims=True) / model
    back = inv_ref[...] * (scaled - unit * mean)
    grad = exact_dot(spread_ref[...], middle_ref[...], 1, 1) + exact_dot(split_ref[...], back, 1, 0)
    part = grad.shape[1] // 2
    out_ref[0] = grad[:, :part]
    out_ref[1] = grad[:, part:]


def input_gradient(backs, mine, theirs, unit, inv, gain, middle, spread, split, model):
    out = like((2, model, middle.shape[0] // 2), F32)
    arrays = (backs, *mine, *theirs, unit, inv, gain, middle, spread, split)
    return pl.pallas_call(
        functools.partial(input_kernel, model),
        grid=(1,),
        in_specs=[full(a) for a in arrays],
        out_specs=full(out),
        out_shape=out,
        scratch_shapes=[pltpu.VMEM(unit.shape, F32)],
        cost_estimate=COST,
        compiler_params=params(40),
        name="input_gradient",
    )(*arrays)


def output_kernel(middle_ref, own_ref, core_ref, far_ref, spread_ref, out_ref):
    result = middle_ref[...] + own_ref[...] + core_ref[...].astype(F32) + far_ref[...].astype(F32)
    out = dot(spread_ref[...], result.astype(BF), 1, 1).astype(BF)
    part = out.shape[1] // 2
    out_ref[0] = out[:, :part]
    out_ref[1] = out[:, part:]


def layer_output(middle, own, core, far, spread):
    return pl.pallas_call(
        output_kernel,
        in_specs=[VMEM] * 5,
        out_specs=VMEM,
        out_shape=like((2, spread.shape[0], middle.shape[0] // 2), BF),
        cost_estimate=COST,
        compiler_params=params(),
        name="layer_output",
    )(middle, own, core, far, spread)


def padded(count):
    return -(-count // 8) * 8


def pick(pair, index):
    return jnp.where(index == 0, pair[0], pair[1])


def ordered(mine, theirs, index, axis):
    return jnp.concatenate([pick((mine, theirs), index), pick((theirs, mine), index)], axis=axis)


def swap(array, name):
    return lax.ppermute(array, name, SWAP)


def after(value, *earlier):
    return lax.optimization_barrier((value, *earlier))[0]


def spread_matrix(model, shard, slot, ctx):
    row = lax.broadcasted_iota(jnp.int32, (model, slot * ctx), 0)
    col = lax.broadcasted_iota(jnp.int32, (model, slot * ctx), 1)
    return (col == row // shard * slot + row % shard).astype(BF)


def core_order(slot, line, c):
    wide = slot * line * 4
    row = lax.broadcasted_iota(jnp.int32, (wide, wide), 1)
    col = lax.broadcasted_iota(jnp.int32, (wide, wide), 0)
    block, place = row // slot, row % slot
    core, y, z = block % 2, block // 2 % 2, block // 4
    other = (core != c).astype(jnp.int32)
    return (col == ((other * 2 + y) * line + z) * slot + place).astype(BF)


def gather_small(rows_here, cut, meanwhile):
    line = lax.axis_size("zh") * lax.axis_size("zl")
    d, y = lax.axis_index("dp"), lax.axis_index("y")
    z_all = lax.all_to_all(
        jnp.broadcast_to(rows_here[None], (line, *rows_here.shape)),
        ("zh", "zl"),
        split_axis=0,
        concat_axis=0,
    )
    z_all = after(z_all, *meanwhile).reshape(1, -1, rows_here.shape[1])
    left, right = z_all[..., :cut], z_all[..., cut:]
    left, right = ordered(left, swap(left, "y"), y, 0), ordered(right, swap(right, "dp"), d, 0)
    left, right = left[None], right[None]
    return ordered(left, swap(left, "dp"), d, 0), ordered(right, swap(right, "y"), y, 0)


def body(
    inputs,
    query_weight,
    key_weight,
    value_matrix,
    out_weight,
    gate_weight,
    up_weight,
    down_weight,
    norm_gains,
    cotangent,
):
    seqs, part_rows, model = inputs.shape
    dps, high, low = (lax.axis_size(a) for a in ("dp", "zh", "zl"))
    line = high * low
    ctx = line * 4
    y, c, d = (lax.axis_index(a) for a in ("y", "c", "dp"))
    z = lax.axis_index("zh") * low + lax.axis_index("zl")
    shard = model // ctx
    slot = padded(shard + 1)
    wide = slot * ctx
    half = wide // 2
    rows = 2 * part_rows
    up_line = [(i, i + 1) for i in range(line - 1)]
    down_line = [(i + 1, i) for i in range(line - 1)]
    z_axes = ("zh", "zl")
    everywhere = ("zh", "zl", "y", "c")
    place = jnp.stack([z, y, d, c]).astype(jnp.int32)

    q_part, k_part = query_weight.shape[1], key_weight.shape[1]
    qkv_part = q_part + 2 * k_part
    half_ff = gate_weight.shape[1]
    unit = half_ff // 2
    kv_heads = k_part * dps // HEAD

    small = jnp.concatenate([query_weight, key_weight, value_matrix], axis=1)
    small_columns = -(-qkv_part // 128) * 128
    small = jnp.concatenate(
        [
            jnp.pad(small, ((0, 0), (0, small_columns - qkv_part))),
            jnp.pad(norm_gains, ((0, slot - shard - 1), (0, small_columns - shard))),
        ],
        axis=0,
    )
    large = jnp.concatenate([gate_weight, up_weight, down_weight.T, out_weight.T], axis=1)
    large = jnp.pad(large, ((0, slot - shard), (0, -large.shape[1] % 128)))
    large = lax.all_gather(large, everywhere, axis=0, tiled=True)

    both = jnp.stack([inputs, cotangent], axis=1)
    mine, theirs = pick((both[0], both[1]), c), pick((both[1], both[0]), c)
    both = ordered(mine, swap(theirs, "c"), c, 1)
    spread = spread_matrix(model, shard, slot, ctx)
    by_core = core_order(slot, line, c)
    spread, by_core = after(spread, small), after(by_core, small)
    spread_split = dot(spread, by_core, 1, 1).astype(BF)
    tokens = dot(both[0], spread, 1, 0)
    tokens_t = dot(spread_split, both[0], 0, 1)
    back_out = dot(both[1], spread, 1, 0)
    back_low = back_out.astype(BF)
    inv_first = lax.rsqrt(jnp.sum(tokens_t * tokens_t, axis=0, keepdims=True) / model + EPSILON)
    unit_first = tokens_t * inv_first
    positions = (2 * z + y) * rows + jnp.arange(rows, dtype=jnp.int32)
    cos, sin = rope_tables(positions, HALF_HEAD)

    w_mine = gather_small(small, small_columns // 256 * 128, (unit_first, tokens, back_low))
    w_theirs = tuple(swap(w, "c") for w in w_mine)

    def gains_of(w):
        part = w[0].reshape(dps, 2, line, slot, -1)[:, :, :, shard, :shard]
        return jnp.pad(part, ((0, 0), (0, 0), (0, 0), (0, slot - shard))).astype(F32)

    gains_mine, gains_theirs = gains_of(w_mine), gains_of(w_theirs)
    gain_second = ordered(gains_mine[1, :, :, None], gains_theirs[1, :, :, None], c, 2)
    gain_second = gain_second.transpose(1, 0, 2, 3).reshape(1, wide)
    gain_first = jnp.concatenate([gains_mine[0], gains_theirs[0]], axis=0).reshape(wide, 1)
    gains_mine = gains_mine[0].reshape(1, half)
    gain_first, gain_second, gains_mine = lax.optimization_barrier(
        (gain_first, gain_second, gains_mine)
    )

    normed = (unit_first * gain_first).astype(BF)
    q, kv = project(normed, cos, sin, w_mine, w_theirs, q_part, k_part)

    kvs = [kv]
    back_core, back_far = swap(after(back_low, kv), "c"), swap(after(back_low, kv), "dp")
    q_both = (q, swap(q, "y"))
    state = ()
    for step in range(line - 1):
        here, far_q = kvs[-1], q_both[1]
        if step > 1:
            here, state = lax.optimization_barrier((here, state))
        kvs.append(lax.ppermute(here, z_axes, up_line))
        if step > 0:
            far_q = after(far_q, here)
            state = attend_forward(place, step - 1, False, q, far_q, kvs[step - 1], state, kv_heads)
        if step == 1:
            large, state = lax.optimization_barrier((large, state))
            out_own = last_columns(large, -(-q_part // 128) * 128)
            w_out = (out_own, swap(out_own, "dp"))
    far_q = after(q_both[1], kvs[-2])
    state = attend_forward(place, line - 2, False, q, far_q, kvs[line - 2], state, kv_heads)
    stats, acc, far_stats, far_acc = attend_forward(
        place, line - 1, True, *q_both, kvs[line - 1], state, kv_heads
    )
    got = lax.ppermute(jnp.stack([far_stats, stats]), "y", SWAP)
    attended, lse, far_lse, middle, unit_second, inv_second, mixed_own = to_middle(
        place, (stats, far_stats), (got[0], got[1]), acc, swap(far_acc, "y"), w_out, tokens, gain_second,
        kv_heads, model,
    )

    mixed_core, mixed_far = swap(mixed_own, "c"), swap(mixed_own, "dp")
    core = c.astype(jnp.int32)[None]
    hidden_near, backs_near, part_own, part_core, mix_own, mix_core = feed_forward(
        core, (mixed_own, mixed_core), (back_low, back_core), large, unit, "feed_near"
    )
    mixed_far = after(mixed_far, mix_own)
    back_far = after(back_far, stats)
    mixed_far, back_far = (mixed_far, swap(mixed_far, "c")), (back_far, swap(back_far, "c"))
    hidden_far, backs_far, part_far, part_cross, mix_far, mix_cross = feed_forward(
        core, mixed_far, back_far, large, unit, "feed_far"
    )
    mix_core = swap(mix_core, "c")
    mix_far = add_low(mix_far, swap(mix_cross, "c"))
    hidden_near, mix_far_sum = after(hidden_near, mix_far), mix_far
    mix_far = swap(mix_far_sum, "dp")

    mixed_all, back_all = (mixed_own, mixed_core, *mixed_far), (back_low, back_core, *back_far)
    grads_keep, grads_send = feed_grads(
        y.astype(jnp.int32)[None], mixed_all, back_all, (backs_near, backs_far), (hidden_near, hidden_far), line
    )
    normed_pair = (normed[:half], swap(normed[half:], "c"))
    attended_pair = (attended, swap(attended, "c"))
    part_far = add_low(part_far, swap(part_cross, "c"))
    part_core = swap(part_core, "c")
    mix_far = after(mix_far, grads_keep, normed_pair[1], attended_pair[1], part_far, part_core)

    back_middle, do, row_dot, gain_terms, proj = after_feed(
        place, mix_own, mix_core, mix_far, unit_second, inv_second, gain_second, back_out, w_out, by_core,
        attended, kv_heads, model,
    )
    proj_pair = (proj[:half], swap(proj[half:], "c"))
    gain_terms = gain_terms + swap(gain_terms, "c")
    do_far, dot_far = swap(do, "y"), swap(row_dot, "y")
    do_far = after(do_far, proj_pair[1], gain_terms)
    do_both, dot_both, lse_both = (do, do_far), (row_dot, dot_far), (lse, far_lse)

    grads_far = swap(after(grads_send, do_far, dot_far), "y")
    part_far = swap(after(part_far, do_far), "dp")
    chain, dq = None, ()
    for step in range(line - 1, 0, -1):
        keys_here = kvs[step]
        if step == 1:
            keys_here = after(keys_here, part_far, part_core)
        if step < line - 2:
            keys_here, chain = lax.optimization_barrier((keys_here, chain))
        *dq, total = attend_backward(
            place, step, q_both, do_both, lse_both, dot_both, keys_here, dq, kv_heads
        )
        if chain is not None:
            total = add_low(total, lax.ppermute(chain, z_axes, down_line))
        chain = total
    dq, dq_send, dkv = attend_backward(
        place, 0, q_both, do_both, lse_both, dot_both, after(kvs[0], chain), dq, kv_heads
    )
    dq_far = swap(dq_send, "y")
    chain = lax.ppermute(after(chain, dq_send), z_axes, down_line)
    grads = add_wide(grads_keep, after(grads_far, dq, chain)).reshape(line * 2 * slot, -1)
    grads = lax.psum_scatter(grads, z_axes, scatter_dimension=0, tiled=True)
    backs = finish_backs(dq, dq_far, dkv, chain, cos, sin, dps, q_part, k_part)

    left_keep, left_send, right_keep, right_send = small_terms(
        place, normed_pair, proj_pair, (backs, swap(backs, "c")), attended_pair, w_mine, gains_mine,
        gain_terms, slot, shard,
    )
    left_far, right_far = swap(left_send, "dp"), swap(right_send, "y")
    (
        backs, part_far, part_core, part_own, middle, back_middle, unit_first, spread, spread_split,
        *weights, _,
    ) = lax.optimization_barrier(
        (
            backs, part_far, part_core, part_own, middle, back_middle, unit_first, spread,
            spread_split, *w_mine, *w_theirs, left_keep,
        )
    )
    input_grad = input_gradient(
        backs, weights[:2], weights[2:], unit_first, inv_first, gain_first, back_middle, spread,
        spread_split, model,
    )
    layer_out = layer_output(middle, part_own, part_core, part_far, spread)
    left_far = after(left_far, input_grad, layer_out)
    left_keep, left_send = second_fold(place, 1, left_keep, left_far)
    right_keep, right_send = second_fold(place, 2, right_keep, right_far)
    terms = join((left_keep, swap(left_send, "y")), (right_keep, swap(right_send, "dp")))
    grads_keep, grads_send = sum_blocks(place, (grads,))
    gate_grad, up_grad, down_grad = large_sums(place, grads_keep, swap(grads_send, "c"), shard)
    terms = lax.all_to_all(
        terms.reshape(line, slot, -1), z_axes, split_axis=0, concat_axis=0
    )
    place_of_gains = jnp.where(d == 0, y * line + z, (z * 2 + y) * 2 + c).astype(jnp.int32)[None]
    terms = after(terms, gate_grad)
    query_grad, key_grad, value_grad, out_grad, gains_grad = small_sums(
        place_of_gains, terms, shard, q_part, k_part
    )

    def give_back(array):
        keep, send = pick((array[0], array[1]), c), pick((array[1], array[0]), c)
        return ordered(keep[None], swap(send, "c")[None], c, 0)

    return (
        give_back(layer_out).transpose(0, 2, 1),
        give_back(input_grad).transpose(0, 2, 1),
        query_grad,
        key_grad,
        value_grad,
        out_grad.T,
        gate_grad,
        up_grad,
        down_grad.T,
        gains_grad,
    )


def solution(mesh):
    devices = mesh.devices
    dps, ctx = devices.shape
    inner = Mesh(devices.reshape(dps, 2, ctx // 8, 2, 2), ("dp", "zh", "zl", "y", "c"))
    along = ("zh", "zl", "y", "c")
    rows, by_row, by_col = P("dp", along, None), P(along, "dp"), P("dp", along)
    return jax.shard_map(
        body,
        mesh=inner,
        in_specs=(rows, by_row, by_row, by_row, by_col, by_row, by_row, by_col, by_col, rows),
        out_specs=(rows, rows, by_row, by_row, by_row, by_col, by_row, by_row, by_col, by_col),
        check_vma=False,
    )
```
